32 devices in a mesh: rows: 8 (over z, y), cols: 4 (over x, core).
Axes of the slice: x: 2, y: 2, z: 4, core: 2. Of those that a mesh axis runs over, the one named last changes fastest.
Arguments:
- residual_block: float32 [65536, 64], P('rows', 'cols'), may hold values from -6 to 6
- basis: bfloat16 [65536, 64], P('rows', 'cols'), may hold values from -0.0234375 to 0.0234375
- fine_tiles: bfloat16 [512, 4, 128, 128], P('rows')
- fine_index: int32 [512, 4], P('rows'), may hold values from 0 to 511, as said below
- mid_tiles: bfloat16 [64, 3, 128, 128], P('rows')
- fine_owner: int32 [65536], P('rows'), may hold values from 0 to 8191, as said below
- mid_owner: int32 [8192], P('rows'), may hold values from 0 to 1023, as said below
- coarse_inverse: float32 [1024, 1024], P('rows'), as said below
Outputs:
- directions: float32 [65536, 64], P('rows', 'cols')
- gram: float32 [64, 64], P(None, 'cols')
The draws below stay inside these ranges and needn't reach their ends.
Inputs may be any that keep to these rules, and one draw needn't show every extreme that they name: `fine_index`: slot 0 of block row g names g itself; every block named in a block row of partition p (block rows p*64 to p*64 + 63) belongs to partition p - 1, p or p + 1. `fine_owner`: the fine vertices of partition p map to level-one rows p*1024 to p*1024 + 1023; every level-one row receives exactly 8 vertices. `mid_owner`: the level-one rows of partitions 2q and 2q + 1 map to level-two rows 2q*128 to 2q*128 + 2*128 - 1; every level-two row receives exactly 8 level-one rows. coarse_inverse is symmetric.
All inputs are finite; a program needn't handle non-finite values.
Results may differ from the reference program's by a relative error of at most 0.013.
Values may be sent and summed in bfloat16 or wider, within the bound.
No kernel may reach another device: no remote copies, remote signals or barrier semaphores. Data moves between devices by JAX's collectives and lax.ppermute only.
A program may use at most 64 MiB of HBM per device.

```python
import math
import jax
import jax.numpy as jnp
from jax import lax

BLOCK = 128
SLOTS = 4
COLUMNS = 64
BLOCKS_DEV = 64
FINE_BLOCKS = 512
FINE_ROWS = 65536
MID_DEV = 1024
MID_BLOCKS = 64
MID_ROWS = 8192
COARSE_DEV = 128
COARSE_ROWS = 1024
N_ROWS = 8


def tile_draw(key, blocks, slots, diag_slot):
    shape = (blocks, slots, BLOCK, BLOCK)
    spread = 1.1 / math.sqrt(slots * BLOCK)
    noise = jax.random.truncated_normal(key, -4.0, 4.0, shape, jnp.float32) * spread
    level = jax.random.uniform(jax.random.fold_in(key, 1), (blocks, 1, BLOCK, 1), jnp.float32, 1.5, 3.0)
    diag_rows = lax.broadcasted_iota(jnp.int32, (1, slots, BLOCK, BLOCK), 2)
    diag_cols = lax.broadcasted_iota(jnp.int32, (1, slots, BLOCK, BLOCK), 3)
    slot_ids = lax.broadcasted_iota(jnp.int32, (1, slots, BLOCK, BLOCK), 1)
    marked = ((diag_rows == diag_cols) & (slot_ids == diag_slot)).astype(jnp.float32)
    return (noise + level * marked).astype(jnp.bfloat16)


def draw_fine_tiles(key, part):
    return tile_draw(key, FINE_BLOCKS, SLOTS, 0)


def draw_mid_tiles(key, part):
    return tile_draw(key, MID_BLOCKS, 3, 1)


def draw_fine_index(key, part):
    rows_id = lax.iota(jnp.int32, FINE_BLOCKS)
    part_id = rows_id // BLOCKS_DEV
    base = part_id * BLOCKS_DEV
    left_pick = jax.random.randint(jax.random.fold_in(key, 11), (FINE_BLOCKS,), 0, BLOCKS_DEV)
    right_pick = jax.random.randint(jax.random.fold_in(key, 12), (FINE_BLOCKS,), 0, BLOCKS_DEV)
    inner_pick = jax.random.randint(jax.random.fold_in(key, 13), (FINE_BLOCKS,), 0, BLOCKS_DEV)
    left = jnp.where(part_id > 0, base - BLOCKS_DEV + left_pick, base + left_pick)
    right = jnp.where(part_id < N_ROWS - 1, base + BLOCKS_DEV + right_pick, base + right_pick)
    inner = base + inner_pick
    return jnp.stack([rows_id, left, right, inner], axis=1).astype(jnp.int32)


def draw_fine_owner(key, part):
    keys = jax.random.split(key, N_ROWS)

    def shuffled(single):
        return jax.random.permutation(single, BLOCKS_DEV * BLOCK) // 8
    local = jax.vmap(shuffled)(keys).astype(jnp.int32)
    offsets = lax.iota(jnp.int32, N_ROWS)[:, None] * MID_DEV
    return (local + offsets).reshape(-1).astype(jnp.int32)


def draw_mid_owner(key, part):
    pairs = N_ROWS // 2
    keys = jax.random.split(key, pairs)

    def shuffled(single):
        return jax.random.permutation(single, 2 * MID_DEV) // 8
    local = jax.vmap(shuffled)(keys).astype(jnp.int32)
    offsets = lax.iota(jnp.int32, pairs)[:, None] * (2 * COARSE_DEV)
    return (local + offsets).reshape(-1).astype(jnp.int32)


def draw_coarse_inverse(key, part):
    shape = (COARSE_ROWS, COARSE_ROWS)
    raw = jax.random.normal(key, shape, jnp.float32)
    mixed = (raw + raw.T) * (0.5 / math.sqrt(COARSE_ROWS))
    leading = jax.random.uniform(jax.random.fold_in(key, 3), (COARSE_ROWS,), jnp.float32, 0.2, 0.6)
    return mixed + jnp.diag(leading)


def shard_levels(rng, dims, pieces, low, largest):
    factor_of, own = 1.0, jax.random.fold_in(rng, 6)
    for axis_at, blocks in pieces:
        steps = jnp.exp(jax.random.uniform(jax.random.fold_in(own, axis_at), (blocks,), jnp.float32, low / len(pieces), largest / len(pieces)))
        factor_of = factor_of * jnp.repeat(steps, dims[axis_at] // blocks).reshape([-1 if axis == axis_at else 1 for axis in range(len(dims))])
    return factor_of


def scatter_about(key, dims, scale, reach, cuts=(), held_as=jnp.bfloat16):
    result = jax.random.normal(key, dims, jnp.float32) * scale
    if len(cuts) > 0:
        result = shard_levels(key, dims, cuts, -0.22, 0.18) * result
    return jnp.clip(result, min=-reach, max=reach).astype(held_as)


def setup_inputs(seed: int = 0) -> dict:
    arg_keys = jax.random.split(jax.random.key(seed), 9)
    residual_block = scatter_about(arg_keys[0], (FINE_ROWS, COLUMNS), 1.0, 6.0, ((0, 8), (1, 4)), jnp.float32)
    basis = scatter_about(arg_keys[1], (FINE_ROWS, COLUMNS), FINE_ROWS ** -0.5, 0.0234375, ((0, 8), (1, 4)))
    fine_tiles = draw_fine_tiles(jax.random.fold_in(arg_keys[8], 71), 0)
    fine_index = draw_fine_index(jax.random.fold_in(arg_keys[8], 71), 0)
    mid_tiles = draw_mid_tiles(jax.random.fold_in(arg_keys[8], 71), 0)
    fine_owner = draw_fine_owner(jax.random.fold_in(arg_keys[8], 71), 0)
    mid_owner = draw_mid_owner(jax.random.fold_in(arg_keys[8], 71), 0)
    coarse_inverse = draw_coarse_inverse(jax.random.fold_in(arg_keys[8], 71), 0)
    return dict(residual_block=residual_block, basis=basis, fine_tiles=fine_tiles, fine_index=fine_index, mid_tiles=mid_tiles, fine_owner=fine_owner, mid_owner=mid_owner, coarse_inverse=coarse_inverse)


DAMPING = 0.6666666666666666


def fine_apply(matrix, slot_index, vector):
    packed = lax.optimization_barrier(vector.astype(jnp.bfloat16)).reshape(FINE_BLOCKS, BLOCK, COLUMNS)
    tile_groups = matrix.reshape(N_ROWS, BLOCKS_DEV, SLOTS, BLOCK, BLOCK)
    index_groups = slot_index.reshape(N_ROWS, BLOCKS_DEV, SLOTS)

    def one_group(bundle):
        group_tiles, group_index = bundle
        picked = packed[group_index].astype(jnp.float32)
        return jnp.einsum("bkij,bkjc->bic", group_tiles.astype(jnp.float32), picked)

    product = lax.map(one_group, (tile_groups, index_groups))
    return product.reshape(FINE_ROWS, COLUMNS)


def mid_apply(matrix, vector):
    packed = lax.optimization_barrier(vector.astype(jnp.bfloat16)).astype(jnp.float32)
    packed = packed.reshape(MID_BLOCKS, BLOCK, COLUMNS)
    padded = jnp.pad(packed, ((1, 1), (0, 0), (0, 0)))
    wide = matrix.astype(jnp.float32)
    product = jnp.einsum("bij,bjc->bic", wide[:, 0], padded[:-2])
    product = product + jnp.einsum("bij,bjc->bic", wide[:, 1], padded[1:-1])
    product = product + jnp.einsum("bij,bjc->bic", wide[:, 2], padded[2:])
    return product.reshape(MID_ROWS, COLUMNS)


def reference(residual_block, basis, fine_tiles, fine_index, mid_tiles, fine_owner, mid_owner, coarse_inverse):
    fine_inv = 1.0 / jnp.diagonal(fine_tiles[:, 0], axis1=1, axis2=2).astype(jnp.float32).reshape(FINE_ROWS, 1)
    mid_inv = 1.0 / jnp.diagonal(mid_tiles[:, 1], axis1=1, axis2=2).astype(jnp.float32).reshape(MID_ROWS, 1)
    fine_x = DAMPING * fine_inv * residual_block
    fine_x = fine_x + DAMPING * fine_inv * (residual_block - fine_apply(fine_tiles, fine_index, fine_x))
    fine_res = residual_block - fine_apply(fine_tiles, fine_index, fine_x)
    mid_rhs = jax.ops.segment_sum(fine_res, fine_owner, num_segments=MID_ROWS)
    mid_x = DAMPING * mid_inv * mid_rhs
    mid_x = mid_x + DAMPING * mid_inv * (mid_rhs - mid_apply(mid_tiles, mid_x))
    mid_res = mid_rhs - mid_apply(mid_tiles, mid_x)
    coarse_rhs = jax.ops.segment_sum(mid_res, mid_owner, num_segments=COARSE_ROWS)
    coarse_fix = jnp.dot(coarse_inverse, coarse_rhs, precision=lax.Precision.HIGHEST)
    mid_x = mid_x + coarse_fix[mid_owner]
    mid_x = mid_x + DAMPING * mid_inv * (mid_rhs - mid_apply(mid_tiles, mid_x))
    fine_x = fine_x + mid_x[fine_owner]
    directions = fine_x + DAMPING * fine_inv * (residual_block - fine_apply(fine_tiles, fine_index, fine_x))
    gram = jnp.dot(basis.T, directions.astype(jnp.bfloat16), preferred_element_type=jnp.float32)
    return directions, gram
```

```python
import jax
import jax.numpy as jnp
from jax import lax
from jax.experimental import pallas as pl
from jax.experimental.pallas import tpu as pltpu
from jax.sharding import PartitionSpec as P

DAMPING = 0.6666666666666666
F32 = jnp.float32
BF16 = jnp.bfloat16
NT = (((1,), (1,)), ((), ()))
VM = pl.BlockSpec(memory_space=pltpu.VMEM)
SM = pl.BlockSpec(memory_space=pltpu.SMEM)
ANY = pl.BlockSpec(memory_space=pl.ANY)

TILES_AT, HI_AT, LO_AT, MISC_AT = 0, 640, 704, 768
MESSAGE = 832


def dot_nt(a, b):
    return lax.dot_general(a, b, NT, preferred_element_type=F32)


def eye_mask(n):
    return lax.broadcasted_iota(jnp.int32, (n, n), 0) == lax.broadcasted_iota(jnp.int32, (n, n), 1)


def diag_row(tile, eye):
    return jnp.sum(jnp.where(eye, tile.astype(F32), 0.0), axis=0, keepdims=True)


def params(mib, flops, size):
    return dict(
        compiler_params=pltpu.CompilerParams(vmem_limit_bytes=mib << 20),
        cost_estimate=pl.CostEstimate(flops=flops, bytes_accessed=size, transcendentals=0),
    )


def first_kernel(res, tiles, a_out, winv_out, held, sems):
    blocks, ext = held.shape[0], held.shape[1]
    parts = sems.shape[0]
    per = blocks // parts

    def copy(part):
        rows = pl.ds(part * per, per)
        return pltpu.make_async_copy(tiles.at[rows, 0], held.at[rows], sems.at[part])

    for part in range(parts):
        copy(part).start()
    eye = eye_mask(ext)
    for part in range(parts):
        copy(part).wait()
        for g in range(part * per, (part + 1) * per):
            winv = DAMPING * (1.0 / diag_row(held[g], eye))
            winv_out[pl.ds(g, 1), :] = winv
            a_out[g] = (winv * res[:, g * ext : (g + 1) * ext]).astype(BF16)


def fill_window(window, left, own, right):
    blocks = own.shape[0]
    window[0:blocks] = left[...]
    window[blocks : 2 * blocks] = own[...]
    window[2 * blocks : 3 * blocks] = right[...]


def fine_row(index, offset, tiles, window, g):
    slots = tiles.shape[1]
    picked = [window[index[s, g] - offset] for s in range(slots)]
    return dot_nt(
        jnp.concatenate(picked, axis=1),
        jnp.concatenate([tiles[g, s] for s in range(slots)], axis=1),
    )


def second_kernel(index, place, tiles, left, own, right, res, winv, b_out, b16_out, window):
    blocks, ext = own.shape[0], own.shape[2]
    offset = (place[0] - 1) * blocks
    fill_window(window, left, own, right)
    for g in range(blocks):
        product = fine_row(index, offset, tiles, window, g)
        w = winv[pl.ds(g, 1), :]
        r = res[:, g * ext : (g + 1) * ext]
        b = w * r + w * (r - product)
        b_out[g] = b
        b16_out[g] = b.astype(BF16)


def split(row, ext):
    return lax.shift_right_logical(row, ext.bit_length() - 1), row & (ext - 1)


def one_hot(row, n):
    ids = lax.broadcasted_iota(jnp.int32, (n, row.shape[1]), 0)
    return jnp.where(ids == row, 1.0, 0.0).astype(BF16)


def spread(value, row, n):
    return jnp.concatenate(
        [jnp.where(row == l, value, 0.0).astype(BF16) for l in range(n)], axis=0
    )


def edge(message, row, n=128):
    return message[row : row + n, :]


def as_int(row):
    return row.astype(F32).astype(jnp.int32)


def inverse(row, present):
    return DAMPING * (1.0 / jnp.where(present, row, 1.0))


def mid_inverse(mid_tiles, eye):
    return [
        DAMPING * (1.0 / diag_row(mid_tiles[b, 1], eye)) for b in range(mid_tiles.shape[0])
    ]


def mid_product(mid_tiles, v, b):
    ext = mid_tiles.shape[2]
    count = mid_tiles.shape[0]
    ks = [k for k in range(3) if v.get(b - 1 + k) is not None]
    return dot_nt(
        jnp.concatenate([v[b - 1 + k] for k in ks], axis=1),
        jnp.concatenate([mid_tiles[b, k] for k in ks], axis=1),
    )


def third_kernel(
    index, place, tiles, left, own, right, res, b_in, owner, mid_tiles, mid_owner, from_left,
    from_right, fres_out, u_out, bpart_out, send, window, spread_rows, hot,
):
    blocks, ext = own.shape[0], own.shape[2]
    width = own.shape[1]
    mids = mid_tiles.shape[0]
    me = place[0]
    peers = place[1]
    offset = (me - 1) * blocks
    fill_window(window, left, own, right)
    for g in range(blocks):
        product = fine_row(index, offset, tiles, window, g)
        r = res[:, g * ext : (g + 1) * ext] - product
        fres_out[g] = r
        lo, hi = split(owner[pl.ds(g, 1), :] - me * (mids * ext), ext)
        cols = slice(g * ext, (g + 1) * ext)
        spread_rows[:, cols] = spread(r, lo, mids)
        hot[:, cols] = one_hot(hi, ext)
    total = dot_nt(spread_rows[...], hot[...])
    u = [total[b * width : (b + 1) * width] for b in range(mids)]
    eye = eye_mask(ext)
    winv = mid_inverse(mid_tiles, eye)
    has_left, has_right = me > 0, me < peers - 1
    left_prev, left_mid, left_next = (edge(from_left, 128 * k) for k in range(3))
    left_far = edge(from_left, 384)
    right_prev, right_mid, right_next = (edge(from_right, 128 * k) for k in range(3))
    right_far = edge(from_right, 384)
    winv_left = inverse(diag_row(left_mid, eye), has_left)
    winv_right = inverse(diag_row(right_mid, eye), has_right)
    a = [winv[b] * u[b] for b in range(mids)]
    a16 = {b: a[b].astype(BF16) for b in range(mids)}
    part = {}
    for b in range(mids):
        part[b] = a[b] + winv[b] * (u[b] - mid_product(mid_tiles, a16, b))
        u_out[b] = u[b]
        bpart_out[b] = part[b]
    part[-1] = -winv_left * dot_nt(a16[0], left_next)
    part[mids] = -winv_right * dot_nt(a16[mids - 1], right_prev)
    p16 = {b: v.astype(BF16) for b, v in part.items()}
    rest = {b: u[b] - mid_product(mid_tiles, p16, b) for b in range(mids)}
    rest[-1] = -(dot_nt(p16[-1], left_mid) + dot_nt(p16[0], left_next))
    rest[-2] = -dot_nt(p16[-1], left_far)
    rest[mids] = -(dot_nt(p16[mids], right_mid) + dot_nt(p16[mids - 1], right_prev))
    rest[mids + 1] = -dot_nt(p16[mids], right_far)
    start = me - 2 + me % 2
    order = list(range(-2, mids + 2))
    spreads, hots = [], []
    for b in order:
        if b < 0:
            at = MISC_AT + 2 + b
            hi, block = as_int(from_left[at : at + 1, :]), as_int(from_left[at + 2 : at + 3, :])
        elif b >= mids:
            at = MISC_AT + b - mids
            hi, block = as_int(from_right[at : at + 1, :]), as_int(from_right[at + 2 : at + 3, :])
        else:
            block, hi = split(mid_owner[b : b + 1, :], ext)
        spreads.append(spread(rest[b], block - start, 4))
        hots.append(one_hot(hi, ext))
    coarse = dot_nt(jnp.concatenate(spreads, axis=1), jnp.concatenate(hots, axis=1))
    coarse16 = coarse.astype(BF16)
    first, last = u[0].astype(BF16), u[mids - 1].astype(BF16)
    none = jnp.zeros_like(first)
    for d in range(send.shape[0]):
        for k in range(4):
            send[d, k] = coarse16[k * width : (k + 1) * width]
        send[d, 4] = jnp.where(me + 1 == d, last, jnp.where(me - 1 == d, first, none))


def coarse_kernel(place, got, inverse_rows, mid_tiles, u, bpart, from_left, from_right, fix_out, b_out):
    ext = mid_tiles.shape[2]
    mids = mid_tiles.shape[0]
    peers = got.shape[0]
    me = place[0]
    rhs = []
    for k in range(peers):
        terms = [
            got[s, k - (s - 2 + s % 2)].astype(F32)
            for s in range(peers)
            if 0 <= k - (s - 2 + s % 2) < 4
        ]
        rhs.append(sum(terms[1:], terms[0]))
    rhs16 = jnp.concatenate([r.astype(BF16) for r in rhs], axis=1)
    fix_out[...] = dot_nt(rhs16, inverse_rows[...].astype(BF16)).astype(BF16)
    eye = eye_mask(ext)
    winv_left = inverse(diag_row(edge(from_left, 128), eye), me > 0)
    winv_right = inverse(diag_row(edge(from_right, 128), eye), me < peers - 1)
    before = got[lax.rem(me + peers - 1, peers), 4].astype(F32)
    after = got[lax.rem(me + 1, peers), 4].astype(F32)
    a_before = (winv_left * before).astype(BF16)
    a_after = (winv_right * after).astype(BF16)
    for b in range(mids):
        value = bpart[b]
        if b == 0 or b == mids - 1:
            winv = DAMPING * (1.0 / diag_row(mid_tiles[b, 1], eye))
            if b == 0:
                value = value - winv * dot_nt(a_before, mid_tiles[b, 0])
            if b == mids - 1:
                value = value - winv * dot_nt(a_after, mid_tiles[b, 2])
        b_out[b] = value


def mid_kernel(place, fix, partner, mid_tiles, mid_owner, u, b_in, dpart_out, edges_out, send):
    ext = mid_tiles.shape[2]
    width = fix.shape[0]
    mids = mid_tiles.shape[0]
    me = place[0]
    odd = me % 2
    mine, other = fix[...], partner[...]
    pair = jnp.concatenate(
        [jnp.where(odd == 0, mine, other), jnp.where(odd == 0, other, mine)], axis=0
    )
    eye = eye_mask(ext)
    winv = mid_inverse(mid_tiles, eye)
    c, c16 = {}, {}
    for b in range(mids):
        block, hi = split(mid_owner[b : b + 1, :], ext)
        both = jnp.dot(pair, one_hot(hi, ext), preferred_element_type=F32)
        c[b] = b_in[b] + jnp.where(block - (me - odd) == 0, both[:width], both[width:])
        c16[b] = c[b].astype(BF16)
    d16 = []
    for b in range(mids):
        d = c[b] + winv[b] * (u[b] - mid_product(mid_tiles, c16, b))
        dpart_out[b] = d
        d16.append(d.astype(BF16))
    edges_out[0] = c16[0]
    edges_out[1] = c16[mids - 1]
    none = jnp.zeros_like(c16[0])
    for t in range(send.shape[0]):
        for b in range(mids):
            send[t, b] = d16[b]
        ahead = jnp.logical_or(me + 1 == t, me + 2 == t)
        behind = jnp.logical_or(me - 1 == t, me - 2 == t)
        send[t, mids] = jnp.where(ahead, c16[mids - 1], jnp.where(behind, c16[0], none))


def prolong(values, hi, lo, width, mids, ext):
    both = jnp.dot(values, one_hot(hi, ext), preferred_element_type=F32)
    result = jnp.where(lo == 0, both[:width], 0.0)
    for l in range(1, mids):
        result = jnp.where(lo == l, both[l * width : (l + 1) * width], result)
    return result


def last_kernel(
    index, place, tiles, got, dpart, c_edges, mid_tiles, owner, from_left, from_right, b_in, fres, winv,
    basis, out, gram_out, window, added, rounded,
):
    blocks, width, ext = b_in.shape
    mids = mid_tiles.shape[0]
    peers = got.shape[0]
    me = place[0]
    at = lambda shift: lax.rem(me + shift + peers, peers)
    eye = eye_mask(ext)
    left, right, far_left, far_right = (at(k) for k in (-1, 1, -2, 2))
    has_left, has_right = me > 0, me < peers - 1
    minv = lambda b: DAMPING * (1.0 / diag_row(mid_tiles[b, 1], eye))
    own = [dpart[b] for b in range(mids)]
    own[0] = own[0] - minv(0) * dot_nt(got[left, mids], mid_tiles[0, 0])
    own[-1] = own[-1] - minv(mids - 1) * dot_nt(got[right, mids], mid_tiles[mids - 1, 2])
    lefts = [got[left, b].astype(F32) for b in range(mids)]
    lefts[0] = lefts[0] - inverse(
        from_left[MISC_AT + 4 : MISC_AT + 5, :].astype(F32), has_left
    ) * dot_nt(got[far_left, mids], edge(from_left, 512))
    lefts[-1] = lefts[-1] - inverse(diag_row(edge(from_left, 128), eye), has_left) * dot_nt(
        c_edges[0], edge(from_left, 256)
    )
    rights = [got[right, b].astype(F32) for b in range(mids)]
    rights[0] = rights[0] - inverse(diag_row(edge(from_right, 128), eye), has_right) * dot_nt(
        c_edges[1], edge(from_right, 0)
    )
    rights[-1] = rights[-1] - inverse(
        from_right[MISC_AT + 4 : MISC_AT + 5, :].astype(F32), has_right
    ) * dot_nt(got[far_right, mids], edge(from_right, 512))
    own16, left16, right16 = (
        jnp.concatenate([v.astype(BF16) for v in side], axis=0) for side in (own, lefts, rights)
    )
    for g in range(blocks):
        lo, hi = split(owner[pl.ds(g, 1), :] - me * (mids * ext), ext)
        value = prolong(own16, hi, lo, width, mids, ext)
        added[g] = value
        window[blocks + g] = value.astype(BF16)
        for message, values, base in ((from_left, left16, 0), (from_right, right16, 2 * blocks)):
            hi = as_int(message[HI_AT + g : HI_AT + g + 1, :])
            lo = as_int(message[LO_AT + g : LO_AT + g + 1, :])
            window[base + g] = prolong(values, hi, lo, width, mids, ext).astype(BF16)
    offset = (me - 1) * blocks
    for g in range(blocks):
        product = fine_row(index, offset, tiles, window, g)
        value = b_in[g] + added[g] + winv[pl.ds(g, 1), :] * (fres[g] - product)
        cols = slice(g * ext, (g + 1) * ext)
        out[:, cols] = value
        rounded[:, cols] = value.astype(BF16)
    gram = dot_nt(rounded[...], basis[...])
    for d in range(gram_out.shape[0]):
        gram_out[d] = gram


def halo(value):
    peers = lax.axis_size("rows")
    odd = [(i, i + 1) for i in range(1, peers - 1, 2)]
    even = [(i, i + 1) for i in range(0, peers - 1, 2)]
    swap = lambda pairs: pairs + [(j, i) for i, j in pairs]
    far = lax.ppermute(value, "rows", swap(odd))
    near = lax.ppermute(value, "rows", swap(even))
    return near, far


def shifted(value):
    peers = lax.axis_size("rows")
    up = [(i, i + 1) for i in range(peers - 1)]
    down = [(j, i) for i, j in up]
    return up, down


def on_device(
    residual_block, basis, fine_tiles, fine_index, mid_tiles, fine_owner, mid_owner, coarse_inverse
):
    peers = lax.axis_size("rows")
    me = lax.axis_index("rows")
    blocks, slots, ext, _ = fine_tiles.shape
    mids = mid_tiles.shape[0]
    count = blocks * ext
    width = residual_block.shape[1]
    res = residual_block.T
    index = fine_index.T
    place = jnp.stack([me, jnp.int32(peers)])
    owner = fine_owner.reshape(blocks, ext)
    mid_rows = mid_owner.reshape(mids, ext)
    shape = jax.ShapeDtypeStruct
    tile_bytes = fine_tiles.size * 2
    fine_flops = 2 * fine_tiles.size * width

    hi = (owner % ext).astype(BF16)
    lo = (owner // ext - me * mids).astype(BF16)
    mid_hi = (mid_rows % ext).astype(BF16)
    mid_block = (mid_rows // ext).astype(BF16)
    diag = lambda b: jnp.diagonal(mid_tiles[b, 1])[None]

    def message(picks, pair, far):
        rows = [mid_tiles[b, k] for b, k in picks] + [hi, lo]
        rows += [mid_hi[pair[0] : pair[1]], mid_block[pair[0] : pair[1]], diag(far)]
        filled = MISC_AT + 5
        rows.append(jnp.zeros((MESSAGE - filled, ext), BF16))
        return jnp.concatenate(rows, axis=0)

    last = mids - 1
    to_right = message(
        [(last, 0), (last, 1), (last, 2), (last - 1, 2), (0, 0)], (last - 1, last + 1), 0
    )
    to_left = message([(0, 0), (0, 1), (0, 2), (1, 0), (last, 2)], (0, 2), last)
    shares = lax.axis_size("cols")
    share = MESSAGE // shares
    begin = lax.axis_index("cols") * share
    up, down = shifted(res)
    from_left = lax.ppermute(lax.dynamic_slice_in_dim(to_right, begin, share), "rows", up)
    from_right = lax.ppermute(lax.dynamic_slice_in_dim(to_left, begin, share), "rows", down)
    both = lax.all_gather(jnp.stack([from_left, from_right]), "cols", axis=1, tiled=True)
    from_left, from_right = both[0], both[1]
    all_basis = lax.all_gather(basis.T, "cols", axis=0, tiled=True)

    a16, winv = pl.pallas_call(
        first_kernel,
        in_specs=[VM, ANY],
        out_specs=[VM, VM],
        out_shape=[shape((blocks, width, ext), BF16), shape((blocks, ext), F32)],
        scratch_shapes=[pltpu.VMEM((blocks, ext, ext), BF16), pltpu.SemaphoreType.DMA((4,))],
        name="first_smoothing",
        **params(8, count * ext, tile_bytes // 4),
    )(res, fine_tiles)

    odd = me % 2

    def sides(value):
        near, far = halo(value)
        return (
            jnp.where(odd == 1, near, far),
            jnp.where(odd == 1, far, near),
        )

    left, right = sides(a16)
    b32, b16 = pl.pallas_call(
        second_kernel,
        in_specs=[SM, SM] + [VM] * 6,
        out_specs=[VM, VM],
        out_shape=[shape((blocks, width, ext), F32), shape((blocks, width, ext), BF16)],
        scratch_shapes=[pltpu.VMEM((3 * blocks, width, ext), BF16)],
        name="second_smoothing",
        **params(12, fine_flops, tile_bytes),
    )(index, place, fine_tiles, left, a16, right, res, winv)

    left, right = sides(b16)
    fres, u, bpart, send = pl.pallas_call(
        third_kernel,
        in_specs=[SM, SM] + [VM] * 11,
        out_specs=[VM] * 4,
        out_shape=[
            shape((blocks, width, ext), F32),
            shape((mids, width, ext), F32),
            shape((mids, width, ext), F32),
            shape((peers, 5, width, ext), BF16),
        ],
        scratch_shapes=[
            pltpu.VMEM((3 * blocks, width, ext), BF16),
            pltpu.VMEM((mids * width, count), BF16),
            pltpu.VMEM((ext, count), BF16),
        ],
        name="residual_and_restriction",
        **params(20, fine_flops, tile_bytes),
    )(
        index, place, fine_tiles, left, b16, right, res, b32, owner, mid_tiles, mid_rows,
        from_left, from_right,
    )

    got = lax.all_to_all(send, "rows", 0, 0)
    fix, mid_b = pl.pallas_call(
        coarse_kernel,
        in_specs=[SM] + [VM] * 7,
        out_specs=[VM, VM],
        out_shape=[shape((width, ext), BF16), shape((mids, width, ext), F32)],
        name="coarse_product",
        **params(16, 2 * width * coarse_inverse.size, coarse_inverse.size * 4),
    )(place, got, coarse_inverse, mid_tiles, u, bpart, from_left, from_right)

    partner = lax.ppermute(fix, "rows", [(i, i ^ 1) for i in range(peers)])
    dpart, c_edges, send = pl.pallas_call(
        mid_kernel,
        in_specs=[SM] + [VM] * 6,
        out_specs=[VM] * 3,
        out_shape=[
            shape((mids, width, ext), F32),
            shape((2, width, ext), BF16),
            shape((peers, mids + 1, width, ext), BF16),
        ],
        name="mid_level",
        **params(12, 2 * width * mid_tiles.size, mid_tiles.size * 2),
    )(place, fix, partner, mid_tiles, mid_rows, u, mid_b)

    return finish(
        place, index, fine_tiles, send, dpart, c_edges, mid_tiles, owner, from_left, from_right,
        b32, fres, winv, all_basis,
    )


def finish(
    place, index, fine_tiles, send, dpart, c_edges, mid_tiles, owner, from_left, from_right, b32,
    fres, winv, all_basis,
):
    peers = lax.axis_size("rows")
    blocks, width, ext = b32.shape
    mids = mid_tiles.shape[0]
    count = blocks * ext
    shape = jax.ShapeDtypeStruct
    got = lax.all_to_all(send, "rows", 0, 0)
    out, grams = pl.pallas_call(
        last_kernel,
        in_specs=[SM, SM] + [VM] * 12,
        out_specs=[VM, VM],
        out_shape=[
            shape((width, count), F32),
            shape((peers, width, all_basis.shape[0]), F32),
        ],
        scratch_shapes=[
            pltpu.VMEM((3 * blocks, width, ext), BF16),
            pltpu.VMEM((blocks, width, ext), F32),
            pltpu.VMEM((width, count), BF16),
        ],
        name="prolongation_and_last_smoothing",
        **params(16, 2 * fine_tiles.size * width, fine_tiles.size * 2),
    )(
        index, place, fine_tiles, got, dpart, c_edges, mid_tiles, owner, from_left, from_right,
        b32, fres, winv, all_basis,
    )
    gram = jnp.sum(lax.all_to_all(grams, "rows", 0, 0), axis=0)
    return out.T, gram.T


def solution(mesh):
    in_specs = (
        P("rows", "cols"),
        P("rows", "cols"),
        P("rows", None, None, None),
        P("rows", None),
        P("rows", None, None, None),
        P("rows"),
        P("rows"),
        P("rows", None),
    )
    out_specs = (P("rows", "cols"), P(None, "cols"))
    return jax.shard_map(
        on_device, mesh=mesh, in_specs=in_specs, out_specs=out_specs, check_vma=False
    )
```

```python
import jax
import jax.numpy as jnp
from jax import lax
from jax.experimental import pallas as pl
from jax.experimental.pallas import tpu as pltpu
from jax.sharding import PartitionSpec as P

DAMPING = 0.6666666666666666
F32 = jnp.float32
BF16 = jnp.bfloat16
NT = (((1,), (1,)), ((), ()))
VM = pl.BlockSpec(memory_space=pltpu.VMEM)
SM = pl.BlockSpec(memory_space=pltpu.SMEM)
ANY = pl.BlockSpec(memory_space=pl.ANY)
HBM = pl.BlockSpec(memory_space=pltpu.HBM)

HI_AT, LO_AT, MISC_AT = 512, 576, 640
MESSAGE = 704
FIRST_LIMIT = 52


def dot_nt(a, b):
    return lax.dot_general(a, b, NT, preferred_element_type=F32)


def eye_mask(n):
    return lax.broadcasted_iota(jnp.int32, (n, n), 0) == lax.broadcasted_iota(jnp.int32, (n, n), 1)


def diag_row(tile, eye):
    return jnp.sum(jnp.where(eye, tile.astype(F32), 0.0), axis=0, keepdims=True)


def params(mib, flops, size):
    return dict(
        compiler_params=pltpu.CompilerParams(vmem_limit_bytes=mib << 20),
        cost_estimate=pl.CostEstimate(flops=flops, bytes_accessed=size, transcendentals=0),
    )


def first_kernel(
    place, res, tiles, mid_tiles, owner, mid_owner, a_out, near_out, far_out, winv_out, res_out, flat,
    held, message, sems,
):
    blocks, ext = held.shape[0], held.shape[1]
    width = a_out.shape[1]
    parts = sems.shape[0] - 1
    per = blocks // parts

    def copy(part):
        rows = pl.ds(part * per, per)
        return pltpu.make_async_copy(tiles.at[rows, 0], held.at[rows], sems.at[part])

    whole = pltpu.make_async_copy(res, flat, sems.at[parts])
    whole.start()
    for part in range(parts):
        copy(part).start()
    eye = eye_mask(ext)

    mids = mid_tiles.shape[0]
    last = mids - 1
    lo, hi = split(owner[...] - place[0] * (mids * ext), ext)
    mid_block, mid_hi = split(mid_owner[...], ext)
    sides = (
        ([(last, 1), (last, 2), (last - 1, 2), (0, 0)], last - 1, 0),
        ([(0, 1), (0, 0), (1, 0), (last, 2)], 0, last),
    )
    for side, (picks, first, far) in enumerate(sides):
        for n, (b, k) in enumerate(picks):
            message[side, n * ext : (n + 1) * ext] = mid_tiles[b, k]
        message[side, HI_AT : HI_AT + blocks] = hi.astype(F32).astype(BF16)
        message[side, LO_AT : LO_AT + blocks] = lo.astype(F32).astype(BF16)
        rows = [
            mid_hi[first : first + 2].astype(F32),
            mid_block[first : first + 2].astype(F32),
            diag_row(mid_tiles[far, 1], eye),
            jnp.zeros((MESSAGE - MISC_AT - 5, ext), F32),
        ]
        message[side, MISC_AT:MESSAGE] = jnp.concatenate(rows, axis=0).astype(BF16)
    extra = near_out.shape[0] - blocks
    odd = place[0] % 2
    for n in range(extra):
        part = pl.ds(pl.multiple_of((place[2] * extra + n) * width, width), width)
        near_out[blocks + n] = message[odd, part]
        far_out[blocks + n] = message[1 - odd, part]

    for part in range(parts):
        copy(part).wait()
        if part == 0:
            whole.wait()
        for g in range(part * per, (part + 1) * per):
            winv = DAMPING * (1.0 / diag_row(held[g], eye))
            winv_out[pl.ds(g, 1), :] = winv
            r = flat[:, g * ext : (g + 1) * ext]
            res_out[g] = r
            value = (winv * r).astype(BF16)
            a_out[g] = value
            near_out[g] = value
            far_out[g] = value


def hot_kernel(after, owner, hot_out):
    del after
    blocks, ext = owner.shape
    _, hi = split(owner[...], ext)
    for g in range(blocks):
        hot_out[:, g * ext : (g + 1) * ext] = one_hot(hi[g : g + 1, :], ext)


def sides_kernel(place, a, b, c, d, left_out, right_out, hot_left, hot_right, buffer):
    extra, width, ext = a.shape[1:]
    for n, piece in enumerate((a, b, c, d)):
        at = place[2] ^ n
        buffer[0, at] = piece[0]
        buffer[1, at] = piece[1]
    for n in range(4):
        for k in range(extra):
            rows = slice((n * extra + k) * width, (n * extra + k + 1) * width)
            left_out[rows] = buffer[0, n, k]
            right_out[rows] = buffer[1, n, k]
    blocks = hot_left.shape[1] // ext
    for message, hot in ((left_out, hot_left), (right_out, hot_right)):
        hi = as_int(message[HI_AT : HI_AT + blocks, :])
        for g in range(blocks):
            hot[:, g * ext : (g + 1) * ext] = one_hot(hi[g : g + 1, :], ext)


def fill_window(window, near, own, far, me):
    blocks = own.shape[0]
    window[pl.ds((1 - me % 2) * (2 * blocks), blocks)] = near[0:blocks]
    window[blocks : 2 * blocks] = own[...]
    window[pl.ds((me % 2) * (2 * blocks), blocks)] = far[0:blocks]


def fine_row(index, offset, tiles, window, g):
    slots = tiles.shape[1]
    picked = [window[index[s, g] - offset] for s in range(slots)]
    return dot_nt(
        jnp.concatenate(picked, axis=1),
        jnp.concatenate([tiles[g, s] for s in range(slots)], axis=1),
    )


def second_kernel(
    index, place, tiles, near, own, far, res, winv, hot, basis_b, basis_c, basis_d, b_out, b16_out,
    mine_out, window,
):
    del hot, basis_b, basis_c, basis_d
    blocks, ext = own.shape[0], own.shape[2]
    offset = (place[0] - 1) * blocks
    fill_window(window, near, own, far, place[0])
    for g in range(blocks):
        product = fine_row(index, offset, tiles, window, g)
        w = winv[pl.ds(g, 1), :]
        r = res[g]
        b = w * r + w * (r - product)
        b_out[g] = b
        b16_out[g] = b.astype(BF16)
    odd = place[0] % 2
    mine_out[1 - odd] = near[blocks:]
    mine_out[odd] = far[blocks:]


def split(row, ext):
    return lax.shift_right_logical(row, ext.bit_length() - 1), row & (ext - 1)


def one_hot(row, n):
    ids = lax.broadcasted_iota(jnp.int32, (n, row.shape[1]), 0)
    return jnp.where(ids == row, 1.0, 0.0).astype(BF16)


def spread(value, row, n):
    return jnp.concatenate(
        [jnp.where(row == l, value, 0.0).astype(BF16) for l in range(n)], axis=0
    )


def edge(message, row, n=128):
    return message[row : row + n, :]


def as_int(row):
    return row.astype(F32).astype(jnp.int32)


def inverse(row, present):
    return DAMPING * (1.0 / jnp.where(present, row, 1.0))


def mid_inverse(mid_tiles, eye):
    return [
        DAMPING * (1.0 / diag_row(mid_tiles[b, 1], eye)) for b in range(mid_tiles.shape[0])
    ]


def mid_product(mid_tiles, v, b):
    ext = mid_tiles.shape[2]
    count = mid_tiles.shape[0]
    ks = [k for k in range(3) if v.get(b - 1 + k) is not None]
    return dot_nt(
        jnp.concatenate([v[b - 1 + k] for k in ks], axis=1),
        jnp.concatenate([mid_tiles[b, k] for k in ks], axis=1),
    )


def third_kernel(
    index, place, tiles, near, own, far, res, owner, hot, mid_tiles, mid_owner, from_left,
    from_right, fres_out, u_out, bpart_out, send, window, spread_rows,
):
    blocks, ext = own.shape[0], own.shape[2]
    width = own.shape[1]
    mids = mid_tiles.shape[0]
    me = place[0]
    peers = place[1]
    offset = (me - 1) * blocks
    fill_window(window, near, own, far, place[0])
    for g in range(blocks):
        product = fine_row(index, offset, tiles, window, g)
        r = res[g] - product
        fres_out[g] = r
        lo, _ = split(owner[pl.ds(g, 1), :] - me * (mids * ext), ext)
        spread_rows[:, g * ext : (g + 1) * ext] = spread(r, lo, mids)
    total = dot_nt(spread_rows[...], hot[...])
    u = [total[b * width : (b + 1) * width] for b in range(mids)]
    eye = eye_mask(ext)
    winv = mid_inverse(mid_tiles, eye)
    has_left, has_right = me > 0, me < peers - 1
    left_mid, left_next, left_far = (edge(from_left, 128 * k) for k in range(3))
    right_mid, right_prev, right_far = (edge(from_right, 128 * k) for k in range(3))
    winv_left = inverse(diag_row(left_mid, eye), has_left)
    winv_right = inverse(diag_row(right_mid, eye), has_right)
    a = [winv[b] * u[b] for b in range(mids)]
    a16 = {b: a[b].astype(BF16) for b in range(mids)}
    part = {}
    for b in range(mids):
        part[b] = a[b] + winv[b] * (u[b] - mid_product(mid_tiles, a16, b))
        u_out[b] = u[b]
        bpart_out[b] = part[b]
    part[-1] = -winv_left * dot_nt(a16[0], left_next)
    part[mids] = -winv_right * dot_nt(a16[mids - 1], right_prev)
    p16 = {b: v.astype(BF16) for b, v in part.items()}
    rest = {b: u[b] - mid_product(mid_tiles, p16, b) for b in range(mids)}
    rest[-1] = -(dot_nt(p16[-1], left_mid) + dot_nt(p16[0], left_next))
    rest[-2] = -dot_nt(p16[-1], left_far)
    rest[mids] = -(dot_nt(p16[mids], right_mid) + dot_nt(p16[mids - 1], right_prev))
    rest[mids + 1] = -dot_nt(p16[mids], right_far)
    start = me - 2 + me % 2
    order = list(range(-2, mids + 2))
    spreads, hots = [], []
    for b in order:
        if b < 0:
            at = MISC_AT + 2 + b
            hi, block = as_int(from_left[at : at + 1, :]), as_int(from_left[at + 2 : at + 3, :])
        elif b >= mids:
            at = MISC_AT + b - mids
            hi, block = as_int(from_right[at : at + 1, :]), as_int(from_right[at + 2 : at + 3, :])
        else:
            block, hi = split(mid_owner[b : b + 1, :], ext)
        spreads.append(spread(rest[b], block - start, 4))
        hots.append(one_hot(hi, ext))
    coarse = dot_nt(jnp.concatenate(spreads, axis=1), jnp.concatenate(hots, axis=1))
    coarse16 = coarse.astype(BF16)
    first, last = u[0].astype(BF16), u[mids - 1].astype(BF16)
    none = jnp.zeros_like(first)
    for d in range(send.shape[0]):
        for k in range(4):
            send[d, k] = coarse16[k * width : (k + 1) * width]
        send[d, 4] = jnp.where(me + 1 == d, last, jnp.where(me - 1 == d, first, none))


def coarse_kernel(place, got, inverse_rows, mid_tiles, u, bpart, from_left, from_right, fix_out, b_out):
    ext = mid_tiles.shape[2]
    mids = mid_tiles.shape[0]
    peers = got.shape[0]
    me = place[0]
    rhs = []
    for k in range(peers):
        terms = [
            got[s, k - (s - 2 + s % 2)].astype(F32)
            for s in range(peers)
            if 0 <= k - (s - 2 + s % 2) < 4
        ]
        rhs.append(sum(terms[1:], terms[0]))
    rhs16 = jnp.concatenate([r.astype(BF16) for r in rhs], axis=1)
    fix_out[...] = dot_nt(rhs16, inverse_rows[...].astype(BF16)).astype(BF16)
    eye = eye_mask(ext)
    winv_left = inverse(diag_row(edge(from_left, 0), eye), me > 0)
    winv_right = inverse(diag_row(edge(from_right, 0), eye), me < peers - 1)
    before = got[lax.rem(me + peers - 1, peers), 4].astype(F32)
    after = got[lax.rem(me + 1, peers), 4].astype(F32)
    a_before = (winv_left * before).astype(BF16)
    a_after = (winv_right * after).astype(BF16)
    for b in range(mids):
        value = bpart[b]
        if b == 0 or b == mids - 1:
            winv = DAMPING * (1.0 / diag_row(mid_tiles[b, 1], eye))
            if b == 0:
                value = value - winv * dot_nt(a_before, mid_tiles[b, 0])
            if b == mids - 1:
                value = value - winv * dot_nt(a_after, mid_tiles[b, 2])
        b_out[b] = value


def mid_kernel(place, fix, partner, mid_tiles, mid_owner, u, b_in, dpart_out, edges_out, send):
    ext = mid_tiles.shape[2]
    width = fix.shape[0]
    mids = mid_tiles.shape[0]
    me = place[0]
    odd = me % 2
    mine, other = fix[...], partner[...]
    pair = jnp.concatenate(
        [jnp.where(odd == 0, mine, other), jnp.where(odd == 0, other, mine)], axis=0
    )
    eye = eye_mask(ext)
    winv = mid_inverse(mid_tiles, eye)
    c, c16 = {}, {}
    for b in range(mids):
        block, hi = split(mid_owner[b : b + 1, :], ext)
        both = jnp.dot(pair, one_hot(hi, ext), preferred_element_type=F32)
        c[b] = b_in[b] + jnp.where(block - (me - odd) == 0, both[:width], both[width:])
        c16[b] = c[b].astype(BF16)
    d16 = []
    for b in range(mids):
        d = c[b] + winv[b] * (u[b] - mid_product(mid_tiles, c16, b))
        dpart_out[b] = d
        d16.append(d.astype(BF16))
    edges_out[0] = c16[0]
    edges_out[1] = c16[mids - 1]
    none = jnp.zeros_like(c16[0])
    for t in range(send.shape[0]):
        for b in range(mids):
            send[t, b] = d16[b]
        ahead = jnp.logical_or(me + 1 == t, me + 2 == t)
        behind = jnp.logical_or(me - 1 == t, me - 2 == t)
        send[t, mids] = jnp.where(ahead, c16[mids - 1], jnp.where(behind, c16[0], none))


def prolong(values, hot, lo, width, mids):
    both = jnp.dot(values, hot, preferred_element_type=F32)
    result = jnp.where(lo == 0, both[:width], 0.0)
    for l in range(1, mids):
        result = jnp.where(lo == l, both[l * width : (l + 1) * width], result)
    return result


def last_kernel(
    index, place, tiles, got, dpart, c_edges, mid_tiles, owner, hot_own, from_left, hot_left,
    from_right, hot_right, b_in, fres, winv, basis_a, basis_b, basis_c, basis_d, out, gram_out, window,
    added, rounded, grams,
):
    blocks, width, ext = b_in.shape
    mids = mid_tiles.shape[0]
    peers = got.shape[0]
    me = place[0]
    at = lambda shift: lax.rem(me + shift + peers, peers)
    eye = eye_mask(ext)
    left, right, far_left, far_right = (at(k) for k in (-1, 1, -2, 2))
    has_left, has_right = me > 0, me < peers - 1
    minv = lambda b: DAMPING * (1.0 / diag_row(mid_tiles[b, 1], eye))
    own = [dpart[b] for b in range(mids)]
    own[0] = own[0] - minv(0) * dot_nt(got[left, mids], mid_tiles[0, 0])
    own[-1] = own[-1] - minv(mids - 1) * dot_nt(got[right, mids], mid_tiles[mids - 1, 2])
    lefts = [got[left, b].astype(F32) for b in range(mids)]
    lefts[0] = lefts[0] - inverse(
        from_left[MISC_AT + 4 : MISC_AT + 5, :].astype(F32), has_left
    ) * dot_nt(got[far_left, mids], edge(from_left, 384))
    lefts[-1] = lefts[-1] - inverse(diag_row(edge(from_left, 0), eye), has_left) * dot_nt(
        c_edges[0], edge(from_left, 128)
    )
    rights = [got[right, b].astype(F32) for b in range(mids)]
    rights[0] = rights[0] - inverse(diag_row(edge(from_right, 0), eye), has_right) * dot_nt(
        c_edges[1], edge(from_right, 128)
    )
    rights[-1] = rights[-1] - inverse(
        from_right[MISC_AT + 4 : MISC_AT + 5, :].astype(F32), has_right
    ) * dot_nt(got[far_right, mids], edge(from_right, 384))
    own16, left16, right16 = (
        jnp.concatenate([v.astype(BF16) for v in side], axis=0) for side in (own, lefts, rights)
    )
    for g in range(blocks):
        cols = slice(g * ext, (g + 1) * ext)
        lo, _ = split(owner[pl.ds(g, 1), :] - me * (mids * ext), ext)
        value = prolong(own16, hot_own[:, cols], lo, width, mids)
        added[g] = value
        window[blocks + g] = value.astype(BF16)
        for message, hot, values, base in (
            (from_left, hot_left, left16, 0),
            (from_right, hot_right, right16, 2 * blocks),
        ):
            lo = as_int(message[LO_AT + g : LO_AT + g + 1, :])
            window[base + g] = prolong(values, hot[:, cols], lo, width, mids).astype(BF16)
    offset = (me - 1) * blocks
    for g in range(blocks):
        product = fine_row(index, offset, tiles, window, g)
        value = b_in[g] + added[g] + winv[pl.ds(g, 1), :] * (fres[g] - product)
        cols = slice(g * ext, (g + 1) * ext)
        out[:, cols] = value
        rounded[:, cols] = value.astype(BF16)
    for n, piece in enumerate((basis_a, basis_b, basis_c, basis_d)):
        grams[place[2] ^ n] = dot_nt(rounded[...], piece[...])
    gram = jnp.concatenate(
        [grams[n] for n in range(4)] + [jnp.zeros((width, ext - 4 * width), F32)], axis=1
    )
    for d in range(gram_out.shape[0]):
        gram_out[d] = gram


def sum_kernel(got, out):
    total = got[0]
    for s in range(1, got.shape[0]):
        total = total + got[s]
    out[...] = total[:, : out.shape[1]]


def halo(for_partner, for_other):
    peers = lax.axis_size("rows")
    odd = [(i, i + 1) for i in range(1, peers - 1, 2)]
    even = [(i, i + 1) for i in range(0, peers - 1, 2)]
    swap = lambda pairs: pairs + [(j, i) for i, j in pairs]
    near = lax.ppermute(for_partner, "rows", swap(even))
    far = lax.ppermute(for_other, "rows", swap(odd))
    return near, far


def from_columns(value):
    peers = lax.axis_size("cols")
    return [
        lax.ppermute(value, "cols", [(i, i ^ n) for i in range(peers)]) for n in range(1, peers)
    ]


def on_device(
    residual_block, basis, fine_tiles, fine_index, mid_tiles, fine_owner, mid_owner, coarse_inverse
):
    peers = lax.axis_size("rows")
    me = lax.axis_index("rows")
    blocks, slots, ext, _ = fine_tiles.shape
    mids = mid_tiles.shape[0]
    count = blocks * ext
    width = residual_block.shape[1]
    res = residual_block.T
    index = fine_index.T
    place = jnp.stack([me, jnp.int32(peers), lax.axis_index("cols")])
    owner = fine_owner.reshape(blocks, ext)
    mid_rows = mid_owner.reshape(mids, ext)
    shape = jax.ShapeDtypeStruct
    tile_bytes = fine_tiles.size * 2
    fine_flops = 2 * fine_tiles.size * width
    extra = MESSAGE // (lax.axis_size("cols") * width)

    a16, for_partner, for_other, winv, res_blocks = pl.pallas_call(
        first_kernel,
        in_specs=[SM, HBM, HBM, VM, VM, VM],
        out_specs=[VM] * 5,
        out_shape=[
            shape((blocks, width, ext), BF16),
            shape((blocks + extra, width, ext), BF16),
            shape((blocks + extra, width, ext), BF16),
            shape((blocks, ext), F32),
            shape((blocks, width, ext), F32),
        ],
        scratch_shapes=[
            pltpu.VMEM((width, count), F32),
            pltpu.VMEM((blocks, ext, ext), BF16),
            pltpu.VMEM((2, MESSAGE, ext), BF16),
            pltpu.SemaphoreType.DMA((5,)),
        ],
        name="first_smoothing",
        **params(FIRST_LIMIT, count * ext, tile_bytes // 4),
    )(place, res, fine_tiles, mid_tiles, owner, mid_rows)

    near, far = halo(for_partner, for_other)
    tiles = fine_tiles
    hot_own = pl.pallas_call(
        hot_kernel,
        in_specs=[ANY, VM],
        out_specs=VM,
        out_shape=shape((ext, count), BF16),
        name="one_hot_rows",
        **params(4, count * ext, 4 * tile_bytes),
    )(winv, owner)
    basis_pieces = [basis.T] + from_columns(basis.T)

    b32, b16, mine = pl.pallas_call(
        second_kernel,
        in_specs=[SM, SM] + [VM] * 6 + [ANY] * 4,
        out_specs=[VM] * 3,
        out_shape=[
            shape((blocks, width, ext), F32),
            shape((blocks, width, ext), BF16),
            shape((2, extra, width, ext), BF16),
        ],
        scratch_shapes=[pltpu.VMEM((3 * blocks, width, ext), BF16)],
        name="second_smoothing",
        **params(6, fine_flops, tile_bytes),
    )(index, place, tiles, near, a16, far, res_blocks, winv, hot_own, *basis_pieces[1:])

    near, far = halo(b16, b16)
    from_left, from_right, hot_left, hot_right = pl.pallas_call(
        sides_kernel,
        in_specs=[SM] + [VM] * 4,
        out_specs=[VM] * 4,
        out_shape=[
            shape((MESSAGE, ext), BF16),
            shape((MESSAGE, ext), BF16),
            shape((ext, count), BF16),
            shape((ext, count), BF16),
        ],
        scratch_shapes=[pltpu.VMEM((2, 4, extra, width, ext), BF16)],
        name="side_messages",
        **params(4, count * ext, tile_bytes),
    )(place, mine, *from_columns(mine))

    fres, u, bpart, send = pl.pallas_call(
        third_kernel,
        in_specs=[SM, SM] + [VM] * 11,
        out_specs=[VM] * 4,
        out_shape=[
            shape((blocks, width, ext), F32),
            shape((mids, width, ext), F32),
            shape((mids, width, ext), F32),
            shape((peers, 5, width, ext), BF16),
        ],
        scratch_shapes=[
            pltpu.VMEM((3 * blocks, width, ext), BF16),
            pltpu.VMEM((mids * width, count), BF16),
        ],
        name="residual_and_restriction",
        **params(10, fine_flops, tile_bytes),
    )(
        index, place, tiles, near, b16, far, res_blocks, owner, hot_own, mid_tiles, mid_rows,
        from_left, from_right,
    )

    got = lax.all_to_all(send, "rows", 0, 0)
    fix, mid_b = pl.pallas_call(
        coarse_kernel,
        in_specs=[SM] + [VM] * 7,
        out_specs=[VM, VM],
        out_shape=[shape((width, ext), BF16), shape((mids, width, ext), F32)],
        name="coarse_product",
        **params(4, 2 * width * coarse_inverse.size, coarse_inverse.size * 4),
    )(place, got, coarse_inverse, mid_tiles, u, bpart, from_left, from_right)

    partner = lax.ppermute(fix, "rows", [(i, i ^ 1) for i in range(peers)])
    dpart, c_edges, send = pl.pallas_call(
        mid_kernel,
        in_specs=[SM] + [VM] * 6,
        out_specs=[VM] * 3,
        out_shape=[
            shape((mids, width, ext), F32),
            shape((2, width, ext), BF16),
            shape((peers, mids + 1, width, ext), BF16),
        ],
        name="mid_level",
        **params(4, 2 * width * mid_tiles.size, mid_tiles.size * 2),
    )(place, fix, partner, mid_tiles, mid_rows, u, mid_b)

    return finish(
        place, index, tiles, send, dpart, c_edges, mid_tiles, owner, hot_own, from_left, hot_left,
        from_right, hot_right, b32, fres, winv, basis_pieces,
    )


def finish(
    place, index, tiles, send, dpart, c_edges, mid_tiles, owner, hot_own, from_left, hot_left,
    from_right, hot_right, b32, fres, winv, basis_pieces,
):
    peers = lax.axis_size("rows")
    blocks, width, ext = b32.shape
    mids = mid_tiles.shape[0]
    count = blocks * ext
    shape = jax.ShapeDtypeStruct
    got = lax.all_to_all(send, "rows", 0, 0)
    out, grams = pl.pallas_call(
        last_kernel,
        in_specs=[SM, SM] + [VM] * 18,
        out_specs=[VM, VM],
        out_shape=[
            shape((width, count), F32),
            shape((peers, width, ext), F32),
        ],
        scratch_shapes=[
            pltpu.VMEM((3 * blocks, width, ext), BF16),
            pltpu.VMEM((blocks, width, ext), F32),
            pltpu.VMEM((width, count), BF16),
            pltpu.VMEM((4, width, width), F32),
        ],
        name="prolongation_and_last_smoothing",
        **params(8, 2 * tiles.size * width, tiles.size * 2),
    )(
        index, place, tiles, got, dpart, c_edges, mid_tiles, owner, hot_own, from_left, hot_left,
        from_right, hot_right, b32, fres, winv, *basis_pieces,
    )
    gram = pl.pallas_call(
        sum_kernel,
        in_specs=[VM],
        out_specs=VM,
        out_shape=shape((width, 4 * width), F32),
        name="gram_sum",
        **params(4, 0, 0),
    )(lax.all_to_all(grams, "rows", 0, 0))
    return out.T, gram.T


def solution(mesh):
    in_specs = (
        P("rows", "cols"),
        P("rows", "cols"),
        P("rows", None, None, None),
        P("rows", None),
        P("rows", None, None, None),
        P("rows"),
        P("rows"),
        P("rows", None),
    )
    out_specs = (P("rows", "cols"), P(None, "cols"))
    return jax.shard_map(
        on_device, mesh=mesh, in_specs=in_specs, out_specs=out_specs, check_vma=False
    )
```

```python
import jax
import jax.numpy as jnp
from jax import lax
from jax.experimental import pallas as pl
from jax.experimental.pallas import tpu as pltpu
from jax.sharding import PartitionSpec as P

DAMPING = 0.6666666666666666
F32 = jnp.float32
BF16 = jnp.bfloat16
NT = (((1,), (1,)), ((), ()))
VM = pl.BlockSpec(memory_space=pltpu.VMEM)
SM = pl.BlockSpec(memory_space=pltpu.SMEM)
ANY = pl.BlockSpec(memory_space=pl.ANY)
HBM = pl.BlockSpec(memory_space=pltpu.HBM)

HI_AT, LO_AT, MISC_AT = 512, 576, 640
MESSAGE = 704
FIRST_LIMIT = 52
MID_LIMIT = 8


def dot_nt(a, b):
    return lax.dot_general(a, b, NT, preferred_element_type=F32)


def eye_mask(n):
    return lax.broadcasted_iota(jnp.int32, (n, n), 0) == lax.broadcasted_iota(jnp.int32, (n, n), 1)


def diag_row(tile, eye):
    return jnp.sum(jnp.where(eye, tile.astype(F32), 0.0), axis=0, keepdims=True)


def params(mib, flops, size):
    return dict(
        compiler_params=pltpu.CompilerParams(vmem_limit_bytes=mib << 20),
        cost_estimate=pl.CostEstimate(flops=flops, bytes_accessed=size, transcendentals=0),
    )


def first_kernel(
    place, res, tiles, mid_tiles, owner, mid_owner, inverse_rows, a_out, near_out, far_out, winv_out,
    res_out, flat, held, message, owned, mid_owned, inverse_part, sems, side_sems,
):
    blocks, ext = held.shape[0], held.shape[1]
    width = a_out.shape[1]
    parts = sems.shape[0] - 1
    per = blocks // parts

    def copy(part):
        rows = pl.ds(part * per, per)
        return pltpu.make_async_copy(tiles.at[rows, 0], held.at[rows], sems.at[part])

    whole = pltpu.make_async_copy(res, flat, sems.at[parts])
    mids = mid_tiles.shape[0]
    last = mids - 1
    picks = (
        [(last, 1), (last, 2), (last - 1, 2), (0, 0)],
        [(0, 1), (0, 0), (1, 0), (last, 2)],
    )
    share = inverse_part.shape[0]
    begin = pl.multiple_of(place[2] * share, share)
    smalls = [
        pltpu.make_async_copy(owner, owned, side_sems.at[0]),
        pltpu.make_async_copy(mid_owner, mid_owned, side_sems.at[1]),
        pltpu.make_async_copy(inverse_rows.at[pl.ds(begin, share)], inverse_part, side_sems.at[2]),
    ]
    for side in range(2):
        for n, (b, k) in enumerate(picks[side]):
            smalls.append(
                pltpu.make_async_copy(
                    mid_tiles.at[b, k],
                    message.at[side, pl.ds(n * ext, ext)],
                    side_sems.at[3 + 4 * side + n],
                )
            )
    whole.start()
    copy(0).start()
    for small in smalls:
        small.start()
    for part in range(1, parts):
        copy(part).start()
    eye = eye_mask(ext)
    for small in smalls:
        small.wait()
    lo, hi = split(owned[...] - place[0] * (mids * ext), ext)
    mid_block, mid_hi = split(mid_owned[...], ext)
    for side, first in enumerate((last - 1, 0)):
        message[side, HI_AT : HI_AT + blocks] = hi.astype(F32).astype(BF16)
        message[side, LO_AT : LO_AT + blocks] = lo.astype(F32).astype(BF16)
        rows = [
            mid_hi[first : first + 2].astype(F32),
            mid_block[first : first + 2].astype(F32),
            diag_row(message[1 - side, 0:ext], eye),
            jnp.zeros((MESSAGE - MISC_AT - 5, ext), F32),
        ]
        message[side, MISC_AT:MESSAGE] = jnp.concatenate(rows, axis=0).astype(BF16)
    extra = far_out.shape[0] - blocks
    odd = place[0] % 2
    for n in range(extra):
        part = pl.ds(pl.multiple_of((place[2] * extra + n) * width, width), width)
        near_out[blocks + n] = message[odd, part]
        far_out[blocks + n] = message[1 - odd, part]
    tall, wide = share // width, inverse_part.shape[1] // ext
    for i in range(tall):
        for k in range(wide):
            near_out[blocks + extra + i * wide + k] = inverse_part[
                i * width : (i + 1) * width, k * ext : (k + 1) * ext
            ].astype(BF16)

    for part in range(parts):
        copy(part).wait()
        if part == 0:
            whole.wait()
        for g in range(part * per, (part + 1) * per):
            winv = DAMPING * (1.0 / diag_row(held[g], eye))
            winv_out[pl.ds(g, 1), :] = winv
            r = flat[:, g * ext : (g + 1) * ext]
            res_out[g] = r
            value = (winv * r).astype(BF16)
            a_out[g] = value
            near_out[g] = value
            far_out[g] = value


def hot_kernel(after, owner, hot_out):
    del after
    blocks, ext = owner.shape
    _, hi = split(owner[...], ext)
    for g in range(blocks):
        hot_out[:, g * ext : (g + 1) * ext] = one_hot(hi[g : g + 1, :], ext)


def sides_kernel(
    place, a, b, c, d, left_out, right_out, inverse_out, hot_left, hot_right, buffer
):
    width, ext = a.shape[1:]
    extra = left_out.shape[0] // (4 * width)
    for n, piece in enumerate((a, b, c, d)):
        buffer[place[2] ^ n] = piece[...]
    share = inverse_out.shape[0] // 4
    wide = inverse_out.shape[1] // ext
    for n in range(4):
        for k in range(extra):
            rows = slice((n * extra + k) * width, (n * extra + k + 1) * width)
            left_out[rows] = buffer[n, k]
            right_out[rows] = buffer[n, extra + k]
        for i in range(share // width):
            rows = slice(n * share + i * width, n * share + (i + 1) * width)
            for k in range(wide):
                inverse_out[rows, k * ext : (k + 1) * ext] = buffer[n, 2 * extra + i * wide + k]
    blocks = hot_left.shape[1] // ext
    for message, hot in ((left_out, hot_left), (right_out, hot_right)):
        hi = as_int(message[HI_AT : HI_AT + blocks, :])
        for g in range(blocks):
            hot[:, g * ext : (g + 1) * ext] = one_hot(hi[g : g + 1, :], ext)


def fill_window(window, near, own, far, me):
    blocks = own.shape[0]
    window[pl.ds((1 - me % 2) * (2 * blocks), blocks)] = near[0:blocks]
    window[blocks : 2 * blocks] = own[...]
    window[pl.ds((me % 2) * (2 * blocks), blocks)] = far[0:blocks]


def fine_row(index, offset, tiles, window, g):
    slots = tiles.shape[1]
    picked = [window[index[s, g] - offset] for s in range(slots)]
    return dot_nt(
        jnp.concatenate(picked, axis=1),
        jnp.concatenate([tiles[g, s] for s in range(slots)], axis=1),
    )


def second_kernel(
    index, place, tiles, near, own, far, res, winv, hot, basis_b, basis_c, basis_d, b_out, b16_out,
    b16_too, mine_out, window,
):
    del hot, basis_b, basis_c, basis_d
    blocks, ext = own.shape[0], own.shape[2]
    offset = (place[0] - 1) * blocks
    fill_window(window, near, own, far, place[0])
    for g in range(blocks):
        product = fine_row(index, offset, tiles, window, g)
        w = winv[pl.ds(g, 1), :]
        r = res[g]
        b = w * r + w * (r - product)
        b_out[g] = b
        b16_out[g] = b.astype(BF16)
        b16_too[g] = b.astype(BF16)
    for n in range(blocks, b16_too.shape[0]):
        b16_too[n] = jnp.zeros_like(b16_too[n])
    odd = place[0] % 2
    extra = far.shape[0] - blocks
    mine_out[pl.ds((1 - odd) * extra, extra)] = near[blocks : blocks + extra]
    mine_out[pl.ds(odd * extra, extra)] = far[blocks:]
    mine_out[2 * extra :] = near[blocks + extra :]


def split(row, ext):
    return lax.shift_right_logical(row, ext.bit_length() - 1), row & (ext - 1)


def one_hot(row, n):
    ids = lax.broadcasted_iota(jnp.int32, (n, row.shape[1]), 0)
    return jnp.where(ids == row, 1.0, 0.0).astype(BF16)


def spread(value, row, n):
    return jnp.concatenate(
        [jnp.where(row == l, value, 0.0).astype(BF16) for l in range(n)], axis=0
    )


def edge(message, row, n=128):
    return message[row : row + n, :]


def as_int(row):
    return row.astype(F32).astype(jnp.int32)


def inverse(row, present):
    return DAMPING * (1.0 / jnp.where(present, row, 1.0))


def mid_inverse(mid_tiles, eye):
    return [
        DAMPING * (1.0 / diag_row(mid_tiles[b, 1], eye)) for b in range(mid_tiles.shape[0])
    ]


def mid_product(mid_tiles, v, b):
    ext = mid_tiles.shape[2]
    count = mid_tiles.shape[0]
    ks = [k for k in range(3) if v.get(b - 1 + k) is not None]
    return dot_nt(
        jnp.concatenate([v[b - 1 + k] for k in ks], axis=1),
        jnp.concatenate([mid_tiles[b, k] for k in ks], axis=1),
    )


def third_kernel(
    index, place, tiles, near, own, far, res, owner, hot, mid_tiles, mid_owner, from_left,
    from_right, fres_out, u_out, bpart_out, send, window, spread_rows,
):
    blocks, ext = own.shape[0], own.shape[2]
    width = own.shape[1]
    mids = mid_tiles.shape[0]
    me = place[0]
    peers = place[1]
    offset = (me - 1) * blocks
    fill_window(window, near, own, far, place[0])
    for g in range(blocks):
        product = fine_row(index, offset, tiles, window, g)
        r = res[g] - product
        fres_out[g] = r
        lo, _ = split(owner[pl.ds(g, 1), :] - me * (mids * ext), ext)
        spread_rows[:, g * ext : (g + 1) * ext] = spread(r, lo, mids)
    total = dot_nt(spread_rows[...], hot[...])
    u = [total[b * width : (b + 1) * width] for b in range(mids)]
    eye = eye_mask(ext)
    winv = mid_inverse(mid_tiles, eye)
    has_left, has_right = me > 0, me < peers - 1
    left_mid, left_next, left_far = (edge(from_left, 128 * k) for k in range(3))
    right_mid, right_prev, right_far = (edge(from_right, 128 * k) for k in range(3))
    winv_left = inverse(diag_row(left_mid, eye), has_left)
    winv_right = inverse(diag_row(right_mid, eye), has_right)
    a = [winv[b] * u[b] for b in range(mids)]
    a16 = {b: a[b].astype(BF16) for b in range(mids)}
    part = {}
    for b in range(mids):
        part[b] = a[b] + winv[b] * (u[b] - mid_product(mid_tiles, a16, b))
        u_out[b] = u[b]
        bpart_out[b] = part[b]
    part[-1] = -winv_left * dot_nt(a16[0], left_next)
    part[mids] = -winv_right * dot_nt(a16[mids - 1], right_prev)
    p16 = {b: v.astype(BF16) for b, v in part.items()}
    rest = {b: u[b] - mid_product(mid_tiles, p16, b) for b in range(mids)}
    rest[-1] = -(dot_nt(p16[-1], left_mid) + dot_nt(p16[0], left_next))
    rest[-2] = -dot_nt(p16[-1], left_far)
    rest[mids] = -(dot_nt(p16[mids], right_mid) + dot_nt(p16[mids - 1], right_prev))
    rest[mids + 1] = -dot_nt(p16[mids], right_far)
    start = me - 2 + me % 2
    order = list(range(-2, mids + 2))
    spreads, hots = [], []
    for b in order:
        if b < 0:
            at = MISC_AT + 2 + b
            hi, block = as_int(from_left[at : at + 1, :]), as_int(from_left[at + 2 : at + 3, :])
        elif b >= mids:
            at = MISC_AT + b - mids
            hi, block = as_int(from_right[at : at + 1, :]), as_int(from_right[at + 2 : at + 3, :])
        else:
            block, hi = split(mid_owner[b : b + 1, :], ext)
        spreads.append(spread(rest[b], block - start, 4))
        hots.append(one_hot(hi, ext))
    coarse = dot_nt(jnp.concatenate(spreads, axis=1), jnp.concatenate(hots, axis=1))
    coarse16 = coarse.astype(BF16)
    first, last = u[0].astype(BF16), u[mids - 1].astype(BF16)
    none = jnp.zeros_like(first)
    for d in range(send.shape[0]):
        for k in range(4):
            send[d, k] = coarse16[k * width : (k + 1) * width]
        send[d, 4] = jnp.where(me + 1 == d, last, jnp.where(me - 1 == d, first, none))


def mid_kernel(
    place, got, inverse_rows, partner_rows, mid_tiles, mid_owner, u, bpart, from_left, from_right,
    dpart_out, edges_out, near_out, far_out, next_out, beyond_out,
):
    ext = mid_tiles.shape[2]
    mids = mid_tiles.shape[0]
    peers = got.shape[0]
    width = got.shape[2]
    me = place[0]
    odd = me % 2
    rhs = []
    for k in range(peers):
        terms = [
            got[s, k - (s - 2 + s % 2)].astype(F32)
            for s in range(peers)
            if 0 <= k - (s - 2 + s % 2) < 4
        ]
        rhs.append(sum(terms[1:], terms[0]))
    rhs16 = jnp.concatenate([r.astype(BF16) for r in rhs], axis=1)
    mine = dot_nt(rhs16, inverse_rows[...].astype(BF16))
    other = dot_nt(rhs16, partner_rows[...])
    pair = jnp.concatenate(
        [jnp.where(odd == 0, mine, other), jnp.where(odd == 0, other, mine)], axis=0
    ).astype(BF16)
    eye = eye_mask(ext)
    winv = mid_inverse(mid_tiles, eye)
    winv_left = inverse(diag_row(edge(from_left, 0), eye), me > 0)
    winv_right = inverse(diag_row(edge(from_right, 0), eye), me < peers - 1)
    before = got[lax.rem(me + peers - 1, peers), 4].astype(F32)
    after = got[lax.rem(me + 1, peers), 4].astype(F32)
    a_before = (winv_left * before).astype(BF16)
    a_after = (winv_right * after).astype(BF16)
    c, c16 = {}, {}
    for b in range(mids):
        value = bpart[b]
        if b == 0:
            value = value - winv[b] * dot_nt(a_before, mid_tiles[b, 0])
        if b == mids - 1:
            value = value - winv[b] * dot_nt(a_after, mid_tiles[b, 2])
        block, hi = split(mid_owner[b : b + 1, :], ext)
        both = jnp.dot(pair, one_hot(hi, ext), preferred_element_type=F32)
        c[b] = value + jnp.where(block - (me - odd) == 0, both[:width], both[width:])
        c16[b] = c[b].astype(BF16)
    d16 = []
    for b in range(mids):
        d = c[b] + winv[b] * (u[b] - mid_product(mid_tiles, c16, b))
        dpart_out[b] = d
        d16.append(d.astype(BF16))
    edges_out[0] = c16[0]
    edges_out[1] = c16[mids - 1]
    for b in range(mids):
        near_out[b] = d16[b]
        far_out[b] = d16[b]
    first, last = c16[0], c16[mids - 1]
    low = me % 4 < 2
    near_out[mids] = jnp.where(odd == 0, last, first)
    far_out[mids] = jnp.where(odd == 0, first, last)
    next_out[...] = jnp.where(low, last, first)
    beyond_out[...] = jnp.where(low, first, last)


def prolong(values, hot, lo, width, mids):
    both = jnp.dot(values, hot, preferred_element_type=F32)
    result = jnp.where(lo == 0, both[:width], 0.0)
    for l in range(1, mids):
        result = jnp.where(lo == l, both[l * width : (l + 1) * width], result)
    return result


def last_kernel(
    index, place, tiles, near, far, nexts, beyond, dpart, c_edges, mid_tiles, owner, hot_own, from_left, hot_left,
    from_right, hot_right, b_in, fres, winv, basis_a, basis_b, basis_c, basis_d, out, gram_out, window,
    added, rounded, grams,
):
    blocks, width, ext = b_in.shape
    mids = mid_tiles.shape[0]
    me, peers = place[0], place[1]
    odd = me % 2
    low = me % 4 < 2
    eye = eye_mask(ext)
    has_left, has_right = me > 0, me < peers - 1
    left = [jnp.where(odd == 1, near[b], far[b]) for b in range(mids + 1)]
    right = [jnp.where(odd == 1, far[b], near[b]) for b in range(mids + 1)]
    far_left = jnp.where(low, beyond[...], nexts[...])
    far_right = jnp.where(low, nexts[...], beyond[...])
    minv = lambda b: DAMPING * (1.0 / diag_row(mid_tiles[b, 1], eye))
    own = [dpart[b] for b in range(mids)]
    own[0] = own[0] - minv(0) * dot_nt(left[mids], mid_tiles[0, 0])
    own[-1] = own[-1] - minv(mids - 1) * dot_nt(right[mids], mid_tiles[mids - 1, 2])
    lefts = [v.astype(F32) for v in left[:mids]]
    lefts[0] = lefts[0] - inverse(
        from_left[MISC_AT + 4 : MISC_AT + 5, :].astype(F32), has_left
    ) * dot_nt(far_left, edge(from_left, 384))
    lefts[-1] = lefts[-1] - inverse(diag_row(edge(from_left, 0), eye), has_left) * dot_nt(
        c_edges[0], edge(from_left, 128)
    )
    rights = [v.astype(F32) for v in right[:mids]]
    rights[0] = rights[0] - inverse(diag_row(edge(from_right, 0), eye), has_right) * dot_nt(
        c_edges[1], edge(from_right, 128)
    )
    rights[-1] = rights[-1] - inverse(
        from_right[MISC_AT + 4 : MISC_AT + 5, :].astype(F32), has_right
    ) * dot_nt(far_right, edge(from_right, 384))
    own16, left16, right16 = (
        jnp.concatenate([v.astype(BF16) for v in side], axis=0) for side in (own, lefts, rights)
    )
    own_lo, _ = split(owner[...] - me * (mids * ext), ext)
    left_lo, right_lo = (
        as_int(message[LO_AT : LO_AT + blocks, :]) for message in (from_left, from_right)
    )
    for g in range(0, blocks, 2):
        cols = slice(g * ext, (g + 2) * ext)
        for lo, hot, values, base in (
            (own_lo, hot_own, own16, blocks),
            (left_lo, hot_left, left16, 0),
            (right_lo, hot_right, right16, 2 * blocks),
        ):
            row = jnp.concatenate([lo[g : g + 1], lo[g + 1 : g + 2]], axis=1)
            value = prolong(values, hot[:, cols], row, width, mids)
            for n in range(2):
                half = value[:, n * ext : (n + 1) * ext]
                if base == blocks:
                    added[g + n] = half
                window[base + g + n] = half.astype(BF16)
    offset = (me - 1) * blocks
    for g in range(blocks):
        product = fine_row(index, offset, tiles, window, g)
        value = b_in[g] + added[g] + winv[pl.ds(g, 1), :] * (fres[g] - product)
        cols = slice(g * ext, (g + 1) * ext)
        out[:, cols] = value
        rounded[:, cols] = value.astype(BF16)
    for n, piece in enumerate((basis_a, basis_b, basis_c, basis_d)):
        grams[place[2] ^ n] = dot_nt(rounded[...], piece[...])
    gram = jnp.concatenate(
        [grams[n] for n in range(4)] + [jnp.zeros((width, ext - 4 * width), F32)], axis=1
    )
    for d in range(gram_out.shape[0]):
        gram_out[d] = gram


def sum_kernel(got, out):
    total = got[0]
    for s in range(1, got.shape[0]):
        total = total + got[s]
    out[...] = total[:, : out.shape[1]]


def halo(for_partner, for_other):
    peers = lax.axis_size("rows")
    odd = [(i, i + 1) for i in range(1, peers - 1, 2)]
    even = [(i, i + 1) for i in range(0, peers - 1, 2)]
    swap = lambda pairs: pairs + [(j, i) for i, j in pairs]
    near = lax.ppermute(for_partner, "rows", swap(even))
    far = lax.ppermute(for_other, "rows", swap(odd))
    return near, far


def from_columns(value):
    peers = lax.axis_size("cols")
    swap = lambda v, n: lax.ppermute(v, "cols", [(i, i ^ n) for i in range(peers)])
    across = swap(value, 2)
    return [swap(value, 1), across, swap(across, 1)]


def on_device(
    residual_block, basis, fine_tiles, fine_index, mid_tiles, fine_owner, mid_owner, coarse_inverse
):
    peers = lax.axis_size("rows")
    me = lax.axis_index("rows")
    blocks, slots, ext, _ = fine_tiles.shape
    mids = mid_tiles.shape[0]
    count = blocks * ext
    width = residual_block.shape[1]
    res = residual_block.T
    index = fine_index.T
    place = jnp.stack([me, jnp.int32(peers), lax.axis_index("cols")])
    owner = fine_owner.reshape(blocks, ext)
    mid_rows = mid_owner.reshape(mids, ext)
    shape = jax.ShapeDtypeStruct
    tile_bytes = fine_tiles.size * 2
    fine_flops = 2 * fine_tiles.size * width
    extra = MESSAGE // (lax.axis_size("cols") * width)

    columns = lax.axis_size("cols")
    share = coarse_inverse.shape[0] // columns
    whole_row = coarse_inverse.shape[1]
    quarter = (share // width) * (whole_row // ext)

    a16, for_partner, for_other, winv, res_blocks = pl.pallas_call(
        first_kernel,
        in_specs=[SM] + [HBM] * 6,
        out_specs=[VM] * 5,
        out_shape=[
            shape((blocks, width, ext), BF16),
            shape((blocks + extra + quarter, width, ext), BF16),
            shape((blocks + extra, width, ext), BF16),
            shape((blocks, ext), F32),
            shape((blocks, width, ext), F32),
        ],
        scratch_shapes=[
            pltpu.VMEM((width, count), F32),
            pltpu.VMEM((blocks, ext, ext), BF16),
            pltpu.VMEM((2, MESSAGE, ext), BF16),
            pltpu.VMEM((blocks, ext), jnp.int32),
            pltpu.VMEM((mids, ext), jnp.int32),
            pltpu.VMEM((share, whole_row), F32),
            pltpu.SemaphoreType.DMA((5,)),
            pltpu.SemaphoreType.DMA((11,)),
        ],
        name="first_smoothing",
        **params(FIRST_LIMIT, count * ext, tile_bytes // 4),
    )(place, res, fine_tiles, mid_tiles, owner, mid_rows, coarse_inverse)

    near, far = halo(for_partner, for_other)
    tiles = fine_tiles
    hot_own = pl.pallas_call(
        hot_kernel,
        in_specs=[ANY, VM],
        out_specs=VM,
        out_shape=shape((ext, count), BF16),
        name="one_hot_rows",
        **params(4, count * ext, 4 * tile_bytes),
    )(winv, owner)
    basis_pieces = [basis.T] + from_columns(basis.T)

    b32, b16, b16_too, mine = pl.pallas_call(
        second_kernel,
        in_specs=[SM, SM] + [VM] * 6 + [ANY] * 4,
        out_specs=[VM] * 4,
        out_shape=[
            shape((blocks, width, ext), F32),
            shape((blocks, width, ext), BF16),
            shape((blocks + 1, width, ext), BF16),
            shape((2 * extra + quarter, width, ext), BF16),
        ],
        scratch_shapes=[pltpu.VMEM((3 * blocks, width, ext), BF16)],
        name="second_smoothing",
        **params(6, fine_flops, tile_bytes),
    )(index, place, tiles, near, a16, far, res_blocks, winv, hot_own, *basis_pieces[1:])

    near, far = halo(b16_too, b16)
    from_left, from_right, partner_rows, hot_left, hot_right = pl.pallas_call(
        sides_kernel,
        in_specs=[SM] + [VM] * 4,
        out_specs=[VM] * 5,
        out_shape=[
            shape((MESSAGE, ext), BF16),
            shape((MESSAGE, ext), BF16),
            shape(coarse_inverse.shape, BF16),
            shape((ext, count), BF16),
            shape((ext, count), BF16),
        ],
        scratch_shapes=[pltpu.VMEM((4, 2 * extra + quarter, width, ext), BF16)],
        name="side_messages",
        **params(4, ext, ext),
    )(place, mine, *from_columns(mine))

    fres, u, bpart, send = pl.pallas_call(
        third_kernel,
        in_specs=[SM, SM] + [VM] * 11,
        out_specs=[VM] * 4,
        out_shape=[
            shape((blocks, width, ext), F32),
            shape((mids, width, ext), F32),
            shape((mids, width, ext), F32),
            shape((peers, 5, width, ext), BF16),
        ],
        scratch_shapes=[
            pltpu.VMEM((3 * blocks, width, ext), BF16),
            pltpu.VMEM((mids * width, count), BF16),
        ],
        name="residual_and_restriction",
        **params(10, fine_flops, tile_bytes),
    )(
        index, place, tiles, near, b16, far, res_blocks, owner, hot_own, mid_tiles, mid_rows,
        from_left, from_right,
    )

    got = lax.all_to_all(send, "rows", 0, 0)
    dpart, c_edges, *sends = pl.pallas_call(
        mid_kernel,
        in_specs=[SM] + [VM] * 9,
        out_specs=[VM] * 6,
        out_shape=[
            shape((mids, width, ext), F32),
            shape((2, width, ext), BF16),
            shape((mids + 1, width, ext), BF16),
            shape((mids + 1, width, ext), BF16),
            shape((width, ext), BF16),
            shape((width, ext), BF16),
        ],
        name="coarse_and_mid_level",
        **params(MID_LIMIT, 4 * width * coarse_inverse.size, coarse_inverse.size * 4),
    )(
        place, got, coarse_inverse, partner_rows, mid_tiles, mid_rows, u, bpart, from_left,
        from_right,
    )

    return finish(
        place, index, tiles, sends, dpart, c_edges, mid_tiles, owner, hot_own, from_left, hot_left,
        from_right, hot_right, b32, fres, winv, basis_pieces,
    )


def finish(
    place, index, tiles, sends, dpart, c_edges, mid_tiles, owner, hot_own, from_left, hot_left,
    from_right, hot_right, b32, fres, winv, basis_pieces,
):
    peers = lax.axis_size("rows")
    blocks, width, ext = b32.shape
    mids = mid_tiles.shape[0]
    count = blocks * ext
    shape = jax.ShapeDtypeStruct
    near, far = halo(*sends[:2])
    pairs = [(i, i + 2) for i in range(peers - 2) if i % 4 >= 2]
    pairs += [(j, i) for i, j in pairs]
    nexts = lax.ppermute(sends[2], "rows", [(i, i ^ 2) for i in range(peers)])
    beyond = lax.ppermute(sends[3], "rows", pairs)
    out, grams = pl.pallas_call(
        last_kernel,
        in_specs=[SM, SM] + [VM] * 21,
        out_specs=[VM, VM],
        out_shape=[
            shape((width, count), F32),
            shape((peers, width, ext), F32),
        ],
        scratch_shapes=[
            pltpu.VMEM((3 * blocks, width, ext), BF16),
            pltpu.VMEM((blocks, width, ext), F32),
            pltpu.VMEM((width, count), BF16),
            pltpu.VMEM((4, width, width), F32),
        ],
        name="prolongation_and_last_smoothing",
        **params(8, 2 * tiles.size * width, tiles.size * 2),
    )(
        index, place, tiles, near, far, nexts, beyond, dpart, c_edges, mid_tiles, owner, hot_own, from_left, hot_left,
        from_right, hot_right, b32, fres, winv, *basis_pieces,
    )
    gram = pl.pallas_call(
        sum_kernel,
        in_specs=[VM],
        out_specs=VM,
        out_shape=shape((width, 4 * width), F32),
        name="gram_sum",
        **params(4, 0, 0),
    )(lax.all_to_all(grams, "rows", 0, 0))
    return out.T, gram.T


def solution(mesh):
    in_specs = (
        P("rows", "cols"),
        P("rows", "cols"),
        P("rows", None, None, None),
        P("rows", None),
        P("rows", None, None, None),
        P("rows"),
        P("rows"),
        P("rows", None),
    )
    out_specs = (P("rows", "cols"), P(None, "cols"))
    return jax.shard_map(
        on_device, mesh=mesh, in_specs=in_specs, out_specs=out_specs, check_vma=False
    )
```

```python
import jax
import jax.numpy as jnp
from jax import lax
from jax.experimental import pallas as pl
from jax.experimental.pallas import tpu as pltpu
from jax.sharding import PartitionSpec as P

DAMPING = 0.6666666666666666
F32 = jnp.float32
BF16 = jnp.bfloat16
NT = (((1,), (1,)), ((), ()))
VM = pl.BlockSpec(memory_space=pltpu.VMEM)
SM = pl.BlockSpec(memory_space=pltpu.SMEM)
ANY = pl.BlockSpec(memory_space=pl.ANY)
HBM = pl.BlockSpec(memory_space=pltpu.HBM)

HI_AT, LO_AT, MISC_AT = 512, 576, 640
MESSAGE = 704
FIRST_LIMIT = 52
MID_LIMIT = 8


def dot_nn(a, b):
    return jnp.dot(a, b, preferred_element_type=F32)


def dot_nt(a, b):
    return lax.dot_general(a, b, NT, preferred_element_type=F32)


def eye_mask(n):
    return lax.broadcasted_iota(jnp.int32, (n, n), 0) == lax.broadcasted_iota(jnp.int32, (n, n), 1)


def diag_row(tile, eye):
    return jnp.sum(jnp.where(eye, tile.astype(F32), 0.0), axis=0, keepdims=True)


def params(mib, flops, size):
    return dict(
        compiler_params=pltpu.CompilerParams(vmem_limit_bytes=mib << 20),
        cost_estimate=pl.CostEstimate(flops=flops, bytes_accessed=size, transcendentals=0),
    )


def first_kernel(
    place, res, tiles, mid_tiles, owner, mid_owner, inverse_rows, a_out, near_out, far_out, winv_out,
    res_out, flat, held, message, owned, mid_owned, inverse_part, sems, side_sems,
):
    blocks, ext = held.shape[0], held.shape[1]
    width = a_out.shape[1]
    parts = sems.shape[0] - 1
    per = blocks // parts

    def copy(part):
        rows = pl.ds(part * per, per)
        return pltpu.make_async_copy(tiles.at[rows, 0], held.at[rows], sems.at[part])

    whole = pltpu.make_async_copy(res, flat, sems.at[parts])
    mids = mid_tiles.shape[0]
    last = mids - 1
    picks = (
        [(last, 1), (last, 2), (last - 1, 2), (0, 0)],
        [(0, 1), (0, 0), (1, 0), (last, 2)],
    )
    share = inverse_part.shape[0]
    begin = pl.multiple_of(place[2] * share, share)
    smalls = [
        pltpu.make_async_copy(owner, owned, side_sems.at[0]),
        pltpu.make_async_copy(mid_owner, mid_owned, side_sems.at[1]),
        pltpu.make_async_copy(inverse_rows.at[pl.ds(begin, share)], inverse_part, side_sems.at[2]),
    ]
    for side in range(2):
        for n, (b, k) in enumerate(picks[side]):
            smalls.append(
                pltpu.make_async_copy(
                    mid_tiles.at[b, k],
                    message.at[side, pl.ds(n * ext, ext)],
                    side_sems.at[3 + 4 * side + n],
                )
            )
    whole.start()
    for part in range(parts):
        copy(part).start()
    for small in smalls:
        small.start()
    eye = eye_mask(ext)
    for small in smalls:
        small.wait()
    lo, hi = split(owned[...] - place[0] * (mids * ext), ext)
    mid_block, mid_hi = split(mid_owned[...], ext)
    for side, first in enumerate((last - 1, 0)):
        message[side, HI_AT : HI_AT + blocks] = hi.astype(F32).astype(BF16)
        message[side, LO_AT : LO_AT + blocks] = lo.astype(F32).astype(BF16)
        rows = [
            mid_hi[first : first + 2].astype(F32),
            mid_block[first : first + 2].astype(F32),
            diag_row(message[1 - side, 0:ext], eye),
            jnp.zeros((MESSAGE - MISC_AT - 5, ext), F32),
        ]
        message[side, MISC_AT:MESSAGE] = jnp.concatenate(rows, axis=0).astype(BF16)
    extra = far_out.shape[0] - blocks
    odd = place[0] % 2
    for n in range(extra):
        part = pl.ds(pl.multiple_of((place[2] * extra + n) * width, width), width)
        near_out[blocks + n] = message[odd, part]
        far_out[blocks + n] = message[1 - odd, part]
    tall, wide = share // width, inverse_part.shape[1] // ext
    for i in range(tall):
        for k in range(wide):
            near_out[blocks + extra + i * wide + k] = inverse_part[
                i * width : (i + 1) * width, k * ext : (k + 1) * ext
            ].astype(BF16)

    for part in range(parts):
        copy(part).wait()
        if part == 0:
            whole.wait()
        for g in range(part * per, (part + 1) * per):
            winv = DAMPING * (1.0 / diag_row(held[g], eye))
            winv_out[pl.ds(g, 1), :] = winv
            r = flat[:, g * ext : (g + 1) * ext]
            res_out[g] = r
            value = (winv * r).astype(BF16)
            a_out[g] = value
            near_out[g] = value
            far_out[g] = value


def plan_kernel(place, index, after, owner, hot_out, plan):
    del after
    blocks, ext = owner.shape
    first = place[0] * blocks
    zero = 3 * blocks

    def row(g, most):
        away, block = [], []
        for s in range(1, 4):
            at = index[s, g] - first
            own = jnp.logical_and(at >= 0, at < blocks)
            away.append(jnp.where(own, 0, 1))
            block.append(at + blocks)
        count = away[0] + away[1] + away[2]
        one = jnp.where(away[0] == 1, 0, jnp.where(away[1] == 1, 1, 2))
        two = jnp.where(away[0] + away[1] == 2, 1, 2)
        pick = lambda k: jnp.where(k == 0, block[0], jnp.where(k == 1, block[1], block[2]))
        plan[0, g] = one + 1
        plan[1, g] = jnp.where(count >= 1, pick(one), zero)
        plan[2, g] = two + 1
        plan[3, g] = jnp.where(count >= 2, pick(two), zero)
        plan[4, g] = 0
        return jnp.maximum(most, count)

    plan[4, 0] = lax.fori_loop(0, blocks, row, 0)
    _, hi = split(owner[...], ext)
    for g in range(blocks):
        hot_out[:, g * ext : (g + 1) * ext] = one_hot(hi[g : g + 1, :], ext)


def own_rows(index, place, own, window, slots):
    blocks = own.shape[0]
    window[0:blocks] = own[...]
    window[blocks] = jnp.zeros_like(window[blocks])
    first = place[0] * blocks

    def local(s, g):
        at = index[s, g] - first
        return jnp.where(jnp.logical_and(at >= 0, at < blocks), at, blocks)

    def row(g):
        picked = [window[g]] + [window[local(s, g)] for s in range(1, slots)]
        return jnp.concatenate(picked, axis=1)

    return row


def own_first_kernel(index, place, tiles, own, out, turned_out, window):
    blocks, slots = tiles.shape[:2]
    row = own_rows(index, place, own, window, slots)
    for g in range(blocks):
        turned = [tiles[g, s].T for s in range(slots)]
        for s in range(slots):
            turned_out[g, s] = turned[s]
        out[g] = dot_nn(row(g), jnp.concatenate(turned, axis=0))


def own_kernel(index, place, turned, own, out, window):
    blocks, slots = turned.shape[:2]
    row = own_rows(index, place, own, window, slots)
    for g in range(blocks):
        out[g] = dot_nn(row(g), jnp.concatenate([turned[g, s] for s in range(slots)], axis=0))


def for_rows(index, plan, offset, tiles, window, part, blocks, then):
    window[3 * blocks] = jnp.zeros_like(window[3 * blocks])

    @pl.when(plan[4, 0] <= 2)
    def _():
        for g in range(blocks):
            picked = [window[plan[1, g]], window[plan[3, g]]]
            matched = [tiles[g, plan[0, g]], tiles[g, plan[2, g]]]
            added = dot_nn(jnp.concatenate(picked, axis=1), jnp.concatenate(matched, axis=0))
            then(g, part[g] + added)

    @pl.when(plan[4, 0] > 2)
    def _():
        @pl.loop(0, blocks)
        def _(g):
            then(g, fine_row(index, offset, tiles, window, g))


def sides_kernel(
    place, a, b, c, d, left_out, right_out, inverse_out, buffer
):
    width, ext = a.shape[1:]
    extra = left_out.shape[0] // (4 * width)
    for n, piece in enumerate((a, b, c, d)):
        buffer[place[2] ^ n] = piece[...]
    share = inverse_out.shape[0] // 4
    wide = inverse_out.shape[1] // ext
    for n in range(4):
        for k in range(extra):
            rows = slice((n * extra + k) * width, (n * extra + k + 1) * width)
            left_out[rows] = buffer[n, k]
            right_out[rows] = buffer[n, extra + k]
        for i in range(share // width):
            rows = slice(n * share + i * width, n * share + (i + 1) * width)
            for k in range(wide):
                inverse_out[rows, k * ext : (k + 1) * ext] = buffer[n, 2 * extra + i * wide + k]


def side_hot_kernel(after, from_left, from_right, hot_left, hot_right):
    del after
    ext = hot_left.shape[0]
    blocks = hot_left.shape[1] // ext
    for message, hot in ((from_left, hot_left), (from_right, hot_right)):
        hi = as_int(message[HI_AT : HI_AT + blocks, :])
        for g in range(blocks):
            hot[:, g * ext : (g + 1) * ext] = one_hot(hi[g : g + 1, :], ext)


def fill_window(window, near, own, far, me):
    blocks = own.shape[0]
    window[pl.ds((1 - me % 2) * (2 * blocks), blocks)] = near[0:blocks]
    window[blocks : 2 * blocks] = own[...]
    window[pl.ds((me % 2) * (2 * blocks), blocks)] = far[0:blocks]


def fine_row(index, offset, tiles, window, g):
    slots = tiles.shape[1]
    picked = [window[index[s, g] - offset] for s in range(slots)]
    return dot_nn(
        jnp.concatenate(picked, axis=1),
        jnp.concatenate([tiles[g, s] for s in range(slots)], axis=0),
    )


def second_kernel(
    index, plan, place, tiles, near, own, far, part, res, winv, hot, basis_b, basis_c, basis_d, b_out,
    b16_out, b16_too, mine_out, window,
):
    del hot, basis_b, basis_c, basis_d
    blocks, ext = own.shape[0], own.shape[2]
    offset = (place[0] - 1) * blocks
    fill_window(window, near, own, far, place[0])

    def finish_row(g, product):
        w = winv[pl.ds(g, 1), :]
        r = res[g]
        b = w * r + w * (r - product)
        b_out[g] = b
        b16_out[g] = b.astype(BF16)
        b16_too[g] = b.astype(BF16)

    for_rows(index, plan, offset, tiles, window, part, blocks, finish_row)
    for n in range(blocks, b16_too.shape[0]):
        b16_too[n] = jnp.zeros_like(b16_too[n])
    odd = place[0] % 2
    extra = far.shape[0] - blocks
    mine_out[pl.ds((1 - odd) * extra, extra)] = near[blocks : blocks + extra]
    mine_out[pl.ds(odd * extra, extra)] = far[blocks:]
    mine_out[2 * extra :] = near[blocks + extra :]


def split(row, ext):
    return lax.shift_right_logical(row, ext.bit_length() - 1), row & (ext - 1)


def one_hot(row, n):
    ids = lax.broadcasted_iota(jnp.int32, (n, row.shape[1]), 0)
    return jnp.where(ids == row, 1.0, 0.0).astype(BF16)


def spread(value, row, n):
    return jnp.concatenate(
        [jnp.where(row == l, value, 0.0).astype(BF16) for l in range(n)], axis=0
    )


def edge(message, row, n=128):
    return message[row : row + n, :]


def as_int(row):
    return row.astype(F32).astype(jnp.int32)


def inverse(row, present):
    return DAMPING * (1.0 / jnp.where(present, row, 1.0))


def mid_inverse(mid_tiles, eye):
    return [
        DAMPING * (1.0 / diag_row(mid_tiles[b, 1], eye)) for b in range(mid_tiles.shape[0])
    ]


def mid_product(mid_tiles, v, b):
    ext = mid_tiles.shape[2]
    count = mid_tiles.shape[0]
    ks = [k for k in range(3) if v.get(b - 1 + k) is not None]
    return dot_nt(
        jnp.concatenate([v[b - 1 + k] for k in ks], axis=1),
        jnp.concatenate([mid_tiles[b, k] for k in ks], axis=1),
    )


def third_kernel(
    index, plan, place, tiles, near, own, far, part, res, owner, hot, mid_tiles, mid_owner, from_left,
    from_right, fres_out, u_out, bpart_out, send, window, spread_rows,
):
    blocks, ext = own.shape[0], own.shape[2]
    width = own.shape[1]
    mids = mid_tiles.shape[0]
    me = place[0]
    peers = place[1]
    offset = (me - 1) * blocks
    fill_window(window, near, own, far, place[0])

    def finish_row(g, product):
        r = res[g] - product
        fres_out[g] = r
        lo, _ = split(owner[pl.ds(g, 1), :] - me * (mids * ext), ext)
        at = g * ext if isinstance(g, int) else pl.multiple_of(g * ext, ext)
        spread_rows[:, pl.ds(at, ext)] = spread(r, lo, mids)

    for_rows(index, plan, offset, tiles, window, part, blocks, finish_row)
    quarters = [slice(n * blocks // 4 * ext, (n + 1) * blocks // 4 * ext) for n in range(4)]
    total = sum(dot_nt(spread_rows[:, q], hot[:, q]) for q in quarters)
    u = [total[b * width : (b + 1) * width] for b in range(mids)]
    eye = eye_mask(ext)
    winv = mid_inverse(mid_tiles, eye)
    has_left, has_right = me > 0, me < peers - 1
    left_mid, left_next, left_far = (edge(from_left, 128 * k) for k in range(3))
    right_mid, right_prev, right_far = (edge(from_right, 128 * k) for k in range(3))
    winv_left = inverse(diag_row(left_mid, eye), has_left)
    winv_right = inverse(diag_row(right_mid, eye), has_right)
    a = [winv[b] * u[b] for b in range(mids)]
    a16 = {b: a[b].astype(BF16) for b in range(mids)}
    mine = {}
    for b in range(mids):
        mine[b] = a[b] + winv[b] * (u[b] - mid_product(mid_tiles, a16, b))
        u_out[b] = u[b]
        bpart_out[b] = mine[b]
    mine[-1] = -winv_left * dot_nt(a16[0], left_next)
    mine[mids] = -winv_right * dot_nt(a16[mids - 1], right_prev)
    p16 = {b: v.astype(BF16) for b, v in mine.items()}
    rest = {b: u[b] - mid_product(mid_tiles, p16, b) for b in range(mids)}
    rest[-1] = -(dot_nt(p16[-1], left_mid) + dot_nt(p16[0], left_next))
    rest[-2] = -dot_nt(p16[-1], left_far)
    rest[mids] = -(dot_nt(p16[mids], right_mid) + dot_nt(p16[mids - 1], right_prev))
    rest[mids + 1] = -dot_nt(p16[mids], right_far)
    start = me - 2 + me % 2
    order = list(range(-2, mids + 2))
    spreads, hots = [], []
    for b in order:
        if b < 0:
            at = MISC_AT + 2 + b
            hi, block = as_int(from_left[at : at + 1, :]), as_int(from_left[at + 2 : at + 3, :])
        elif b >= mids:
            at = MISC_AT + b - mids
            hi, block = as_int(from_right[at : at + 1, :]), as_int(from_right[at + 2 : at + 3, :])
        else:
            block, hi = split(mid_owner[b : b + 1, :], ext)
        spreads.append(spread(rest[b], block - start, 4))
        hots.append(one_hot(hi, ext))
    coarse = dot_nt(jnp.concatenate(spreads, axis=1), jnp.concatenate(hots, axis=1))
    coarse16 = coarse.astype(BF16)
    first, last = u[0].astype(BF16), u[mids - 1].astype(BF16)
    none = jnp.zeros_like(first)
    for d in range(send.shape[0]):
        for k in range(4):
            send[d, k] = coarse16[k * width : (k + 1) * width]
        send[d, 4] = jnp.where(me + 1 == d, last, jnp.where(me - 1 == d, first, none))


def mid_kernel(
    place, got, inverse_rows, partner_rows, mid_tiles, mid_owner, u, bpart, from_left, from_right,
    dpart_out, edges_out, near_out, far_out, next_out, beyond_out,
):
    ext = mid_tiles.shape[2]
    mids = mid_tiles.shape[0]
    peers = got.shape[0]
    width = got.shape[2]
    me = place[0]
    odd = me % 2
    rhs = []
    for k in range(peers):
        terms = [
            got[s, k - (s - 2 + s % 2)].astype(F32)
            for s in range(peers)
            if 0 <= k - (s - 2 + s % 2) < 4
        ]
        rhs.append(sum(terms[1:], terms[0]))
    rhs16 = jnp.concatenate([r.astype(BF16) for r in rhs], axis=1)
    mine = dot_nt(rhs16, inverse_rows[...].astype(BF16))
    other = dot_nt(rhs16, partner_rows[...])
    pair = jnp.concatenate(
        [jnp.where(odd == 0, mine, other), jnp.where(odd == 0, other, mine)], axis=0
    ).astype(BF16)
    eye = eye_mask(ext)
    winv = mid_inverse(mid_tiles, eye)
    winv_left = inverse(diag_row(edge(from_left, 0), eye), me > 0)
    winv_right = inverse(diag_row(edge(from_right, 0), eye), me < peers - 1)
    before = got[lax.rem(me + peers - 1, peers), 4].astype(F32)
    after = got[lax.rem(me + 1, peers), 4].astype(F32)
    a_before = (winv_left * before).astype(BF16)
    a_after = (winv_right * after).astype(BF16)
    c, c16 = {}, {}
    for b in range(mids):
        value = bpart[b]
        if b == 0:
            value = value - winv[b] * dot_nt(a_before, mid_tiles[b, 0])
        if b == mids - 1:
            value = value - winv[b] * dot_nt(a_after, mid_tiles[b, 2])
        block, hi = split(mid_owner[b : b + 1, :], ext)
        both = jnp.dot(pair, one_hot(hi, ext), preferred_element_type=F32)
        c[b] = value + jnp.where(block - (me - odd) == 0, both[:width], both[width:])
        c16[b] = c[b].astype(BF16)
    d16 = []
    for b in range(mids):
        d = c[b] + winv[b] * (u[b] - mid_product(mid_tiles, c16, b))
        dpart_out[b] = d
        d16.append(d.astype(BF16))
    edges_out[0] = c16[0]
    edges_out[1] = c16[mids - 1]
    for b in range(mids):
        near_out[b] = d16[b]
        far_out[b] = d16[b]
    first, last = c16[0], c16[mids - 1]
    low = me % 4 < 2
    near_out[mids] = jnp.where(odd == 0, last, first)
    far_out[mids] = jnp.where(odd == 0, first, last)
    next_out[...] = jnp.where(low, last, first)
    beyond_out[...] = jnp.where(low, first, last)


def prolong(values, hot, lo, width, mids):
    both = jnp.dot(values, hot, preferred_element_type=F32)
    result = jnp.where(lo == 0, both[:width], 0.0)
    for l in range(1, mids):
        result = jnp.where(lo == l, both[l * width : (l + 1) * width], result)
    return result


def last_kernel(
    index, place, tiles, near, far, nexts, beyond, dpart, c_edges, mid_tiles, owner, hot_own, from_left, hot_left,
    from_right, hot_right, b_in, fres, winv, basis_a, basis_b, basis_c, basis_d, out, gram_out, window,
    added, rounded, grams, result, sems,
):
    blocks, width, ext = b_in.shape
    mids = mid_tiles.shape[0]
    me, peers = place[0], place[1]
    odd = me % 2
    low = me % 4 < 2
    eye = eye_mask(ext)
    has_left, has_right = me > 0, me < peers - 1
    left = [jnp.where(odd == 1, near[b], far[b]) for b in range(mids + 1)]
    right = [jnp.where(odd == 1, far[b], near[b]) for b in range(mids + 1)]
    far_left = jnp.where(low, beyond[...], nexts[...])
    far_right = jnp.where(low, nexts[...], beyond[...])
    minv = lambda b: DAMPING * (1.0 / diag_row(mid_tiles[b, 1], eye))
    own = [dpart[b] for b in range(mids)]
    own[0] = own[0] - minv(0) * dot_nt(left[mids], mid_tiles[0, 0])
    own[-1] = own[-1] - minv(mids - 1) * dot_nt(right[mids], mid_tiles[mids - 1, 2])
    lefts = [v.astype(F32) for v in left[:mids]]
    lefts[0] = lefts[0] - inverse(
        from_left[MISC_AT + 4 : MISC_AT + 5, :].astype(F32), has_left
    ) * dot_nt(far_left, edge(from_left, 384))
    lefts[-1] = lefts[-1] - inverse(diag_row(edge(from_left, 0), eye), has_left) * dot_nt(
        c_edges[0], edge(from_left, 128)
    )
    rights = [v.astype(F32) for v in right[:mids]]
    rights[0] = rights[0] - inverse(diag_row(edge(from_right, 0), eye), has_right) * dot_nt(
        c_edges[1], edge(from_right, 128)
    )
    rights[-1] = rights[-1] - inverse(
        from_right[MISC_AT + 4 : MISC_AT + 5, :].astype(F32), has_right
    ) * dot_nt(far_right, edge(from_right, 384))
    own16, left16, right16 = (
        jnp.concatenate([v.astype(BF16) for v in side], axis=0) for side in (own, lefts, rights)
    )
    own_lo, _ = split(owner[...] - me * (mids * ext), ext)
    left_lo, right_lo = (
        as_int(message[LO_AT : LO_AT + blocks, :]) for message in (from_left, from_right)
    )
    for g in range(0, blocks, 2):
        cols = slice(g * ext, (g + 2) * ext)
        for lo, hot, values, base in (
            (own_lo, hot_own, own16, blocks),
            (left_lo, hot_left, left16, 0),
            (right_lo, hot_right, right16, 2 * blocks),
        ):
            row = jnp.concatenate([lo[g : g + 1], lo[g + 1 : g + 2]], axis=1)
            value = prolong(values, hot[:, cols], row, width, mids)
            for n in range(2):
                half = value[:, n * ext : (n + 1) * ext]
                if base == blocks:
                    added[g + n] = half
                window[base + g + n] = half.astype(BF16)
    offset = (me - 1) * blocks
    count = sems.shape[0]
    per = blocks // count

    def copy(part):
        cols = pl.ds(part * per * ext, per * ext)
        return pltpu.make_async_copy(result.at[:, cols], out.at[:, cols], sems.at[part])

    for g in range(blocks):
        product = fine_row(index, offset, tiles, window, g)
        value = b_in[g] + added[g] + winv[pl.ds(g, 1), :] * (fres[g] - product)
        cols = slice(g * ext, (g + 1) * ext)
        result[:, cols] = value
        rounded[:, cols] = value.astype(BF16)
        if (g + 1) % per == 0:
            copy((g + 1) // per - 1).start()
    for n, piece in enumerate((basis_a, basis_b, basis_c, basis_d)):
        grams[place[2] ^ n] = dot_nt(rounded[...], piece[...])
    gram = jnp.concatenate(
        [grams[n] for n in range(4)] + [jnp.zeros((width, ext - 4 * width), F32)], axis=1
    )
    for d in range(gram_out.shape[0]):
        gram_out[d] = gram
    for part in range(count):
        copy(part).wait()


def sum_kernel(got, out):
    total = got[0]
    for s in range(1, got.shape[0]):
        total = total + got[s]
    out[...] = total[:, : out.shape[1]]


def halo(for_partner, for_other):
    peers = lax.axis_size("rows")
    odd = [(i, i + 1) for i in range(1, peers - 1, 2)]
    even = [(i, i + 1) for i in range(0, peers - 1, 2)]
    swap = lambda pairs: pairs + [(j, i) for i, j in pairs]
    near = lax.ppermute(for_partner, "rows", swap(even))
    far = lax.ppermute(for_other, "rows", swap(odd))
    return near, far


def from_columns(value):
    peers = lax.axis_size("cols")
    swap = lambda v, n: lax.ppermute(v, "cols", [(i, i ^ n) for i in range(peers)])
    across = swap(value, 2)
    return [swap(value, 1), across, swap(across, 1)]


def on_device(
    residual_block, basis, fine_tiles, fine_index, mid_tiles, fine_owner, mid_owner, coarse_inverse
):
    peers = lax.axis_size("rows")
    me = lax.axis_index("rows")
    blocks, slots, ext, _ = fine_tiles.shape
    mids = mid_tiles.shape[0]
    count = blocks * ext
    width = residual_block.shape[1]
    res = residual_block.T
    index = fine_index.T
    place = jnp.stack([me, jnp.int32(peers), lax.axis_index("cols")])
    owner = fine_owner.reshape(blocks, ext)
    mid_rows = mid_owner.reshape(mids, ext)
    shape = jax.ShapeDtypeStruct
    tile_bytes = fine_tiles.size * 2
    fine_flops = 2 * fine_tiles.size * width
    extra = MESSAGE // (lax.axis_size("cols") * width)

    columns = lax.axis_size("cols")
    share = coarse_inverse.shape[0] // columns
    whole_row = coarse_inverse.shape[1]
    quarter = (share // width) * (whole_row // ext)

    a16, for_partner, for_other, winv, res_blocks = pl.pallas_call(
        first_kernel,
        in_specs=[SM] + [HBM] * 6,
        out_specs=[VM] * 5,
        out_shape=[
            shape((blocks, width, ext), BF16),
            shape((blocks + extra + quarter, width, ext), BF16),
            shape((blocks + extra, width, ext), BF16),
            shape((blocks, ext), F32),
            shape((blocks, width, ext), F32),
        ],
        scratch_shapes=[
            pltpu.VMEM((width, count), F32),
            pltpu.VMEM((blocks, ext, ext), BF16),
            pltpu.VMEM((2, MESSAGE, ext), BF16),
            pltpu.VMEM((blocks, ext), jnp.int32),
            pltpu.VMEM((mids, ext), jnp.int32),
            pltpu.VMEM((share, whole_row), F32),
            pltpu.SemaphoreType.DMA((5,)),
            pltpu.SemaphoreType.DMA((11,)),
        ],
        name="first_smoothing",
        **params(FIRST_LIMIT, count * ext, tile_bytes // 4),
    )(place, res, fine_tiles, mid_tiles, owner, mid_rows, coarse_inverse)

    near, far = halo(for_partner, for_other)
    hot_own, plan = pl.pallas_call(
        plan_kernel,
        in_specs=[SM, SM, ANY, VM],
        out_specs=[VM, SM],
        out_shape=[shape((ext, count), BF16), shape((5, blocks), jnp.int32)],
        name="one_hot_rows",
        **params(4, count * ext, 4 * tile_bytes),
    )(place, index, winv, owner)

    part_shape = shape((blocks, width, ext), F32)
    part, tiles = pl.pallas_call(
        own_first_kernel,
        in_specs=[SM, SM, VM, VM],
        out_specs=[VM, VM],
        out_shape=[part_shape, shape(fine_tiles.shape, BF16)],
        scratch_shapes=[pltpu.VMEM((blocks + 1, width, ext), BF16)],
        name="own_part_and_turned_tiles",
        **params(4, ext, ext),
    )(index, place, fine_tiles, a16)
    basis_pieces = [basis.T] + from_columns(basis.T)

    b32, b16, b16_too, mine = pl.pallas_call(
        second_kernel,
        in_specs=[SM] * 3 + [VM] * 7 + [ANY] * 4,
        out_specs=[VM] * 4,
        out_shape=[
            shape((blocks, width, ext), F32),
            shape((blocks, width, ext), BF16),
            shape((blocks + 1, width, ext), BF16),
            shape((2 * extra + quarter, width, ext), BF16),
        ],
        scratch_shapes=[pltpu.VMEM((3 * blocks + 1, width, ext), BF16)],
        name="second_smoothing",
        **params(6, fine_flops, tile_bytes),
    )(
        index, plan, place, tiles, near, a16, far, part, res_blocks, winv, hot_own,
        *basis_pieces[1:],
    )

    near, far = halo(b16_too, b16)
    part = pl.pallas_call(
        own_kernel,
        in_specs=[SM, SM, VM, VM],
        out_specs=VM,
        out_shape=part_shape,
        scratch_shapes=[pltpu.VMEM((blocks + 1, width, ext), BF16)],
        name="own_part_of_residual",
        **params(4, ext, ext),
    )(index, place, tiles, b16)
    from_left, from_right, partner_rows = pl.pallas_call(
        sides_kernel,
        in_specs=[SM] + [VM] * 4,
        out_specs=[VM] * 3,
        out_shape=[
            shape((MESSAGE, ext), BF16),
            shape((MESSAGE, ext), BF16),
            shape(coarse_inverse.shape, BF16),
        ],
        scratch_shapes=[pltpu.VMEM((4, 2 * extra + quarter, width, ext), BF16)],
        name="side_messages",
        **params(4, ext, ext),
    )(place, mine, *from_columns(mine))

    fres, u, bpart, send = pl.pallas_call(
        third_kernel,
        in_specs=[SM] * 3 + [VM] * 12,
        out_specs=[VM] * 4,
        out_shape=[
            shape((blocks, width, ext), F32),
            shape((mids, width, ext), F32),
            shape((mids, width, ext), F32),
            shape((peers, 5, width, ext), BF16),
        ],
        scratch_shapes=[
            pltpu.VMEM((3 * blocks + 1, width, ext), BF16),
            pltpu.VMEM((mids * width, count), BF16),
        ],
        name="residual_and_restriction",
        **params(10, fine_flops, tile_bytes),
    )(
        index, plan, place, tiles, near, b16, far, part, res_blocks, owner, hot_own, mid_tiles,
        mid_rows, from_left, from_right,
    )

    got = lax.all_to_all(send, "rows", 0, 0)
    dpart, c_edges, *sends = pl.pallas_call(
        mid_kernel,
        in_specs=[SM] + [VM] * 9,
        out_specs=[VM] * 6,
        out_shape=[
            shape((mids, width, ext), F32),
            shape((2, width, ext), BF16),
            shape((mids + 1, width, ext), BF16),
            shape((mids + 1, width, ext), BF16),
            shape((width, ext), BF16),
            shape((width, ext), BF16),
        ],
        name="coarse_and_mid_level",
        **params(MID_LIMIT, 4 * width * coarse_inverse.size, coarse_inverse.size * 4),
    )(
        place, got, coarse_inverse, partner_rows, mid_tiles, mid_rows, u, bpart, from_left,
        from_right,
    )

    return finish(
        place, index, tiles, sends, dpart, c_edges, mid_tiles, owner, hot_own, from_left, from_right,
        b32, fres, winv, basis_pieces,
    )


def finish(
    place, index, tiles, sends, dpart, c_edges, mid_tiles, owner, hot_own, from_left, from_right, b32,
    fres, winv, basis_pieces,
):
    peers = lax.axis_size("rows")
    blocks, width, ext = b32.shape
    mids = mid_tiles.shape[0]
    count = blocks * ext
    shape = jax.ShapeDtypeStruct
    near, far = halo(*sends[:2])
    pairs = [(i, i + 2) for i in range(peers - 2) if i % 4 >= 2]
    pairs += [(j, i) for i, j in pairs]
    nexts = lax.ppermute(sends[2], "rows", [(i, i ^ 2) for i in range(peers)])
    beyond = lax.ppermute(sends[3], "rows", pairs)
    hot_left, hot_right = pl.pallas_call(
        side_hot_kernel,
        in_specs=[ANY, VM, VM],
        out_specs=[VM] * 2,
        out_shape=[shape((ext, count), BF16)] * 2,
        name="side_one_hot_rows",
        **params(4, ext, ext),
    )(c_edges, from_left, from_right)
    out, grams = pl.pallas_call(
        last_kernel,
        in_specs=[SM, SM] + [VM] * 21,
        out_specs=[HBM, VM],
        out_shape=[
            shape((width, count), F32),
            shape((peers, width, ext), F32),
        ],
        scratch_shapes=[
            pltpu.VMEM((3 * blocks, width, ext), BF16),
            pltpu.VMEM((blocks, width, ext), F32),
            pltpu.VMEM((width, count), BF16),
            pltpu.VMEM((4, width, width), F32),
            pltpu.VMEM((width, count), F32),
            pltpu.SemaphoreType.DMA((4,)),
        ],
        name="prolongation_and_last_smoothing",
        **params(8, 2 * tiles.size * width, tiles.size * 2),
    )(
        index, place, tiles, near, far, nexts, beyond, dpart, c_edges, mid_tiles, owner, hot_own, from_left, hot_left,
        from_right, hot_right, b32, fres, winv, *basis_pieces,
    )
    gram = pl.pallas_call(
        sum_kernel,
        in_specs=[VM],
        out_specs=VM,
        out_shape=shape((width, 4 * width), F32),
        name="gram_sum",
        **params(4, 0, 0),
    )(lax.all_to_all(grams, "rows", 0, 0))
    return out.T, gram.T


def solution(mesh):
    in_specs = (
        P("rows", "cols"),
        P("rows", "cols"),
        P("rows", None, None, None),
        P("rows", None),
        P("rows", None, None, None),
        P("rows"),
        P("rows"),
        P("rows", None),
    )
    out_specs = (P("rows", "cols"), P(None, "cols"))
    return jax.shard_map(
        on_device, mesh=mesh, in_specs=in_specs, out_specs=out_specs, check_vma=False
    )
```

```python
import jax
import jax.numpy as jnp
from jax import lax
from jax.experimental import pallas as pl
from jax.experimental.pallas import tpu as pltpu
from jax.sharding import PartitionSpec as P

DAMPING = 0.6666666666666666
F32 = jnp.float32
BF16 = jnp.bfloat16
NT = (((1,), (1,)), ((), ()))
VM = pl.BlockSpec(memory_space=pltpu.VMEM)
SM = pl.BlockSpec(memory_space=pltpu.SMEM)
ANY = pl.BlockSpec(memory_space=pl.ANY)
HBM = pl.BlockSpec(memory_space=pltpu.HBM)

HI_AT, LO_AT, MISC_AT = 512, 576, 640
MESSAGE = 656
FIRST_LIMIT = 52
MID_LIMIT = 8


def dot_nn(a, b):
    return jnp.dot(a, b, preferred_element_type=F32)


def dot_nt(a, b):
    return lax.dot_general(a, b, NT, preferred_element_type=F32)


def eye_mask(n):
    return lax.broadcasted_iota(jnp.int32, (n, n), 0) == lax.broadcasted_iota(jnp.int32, (n, n), 1)


def diag_row(tile, eye):
    return jnp.sum(jnp.where(eye, tile.astype(F32), 0.0), axis=0, keepdims=True)


def params(mib, flops, size):
    return dict(
        compiler_params=pltpu.CompilerParams(vmem_limit_bytes=mib << 20),
        cost_estimate=pl.CostEstimate(flops=flops, bytes_accessed=size, transcendentals=0),
    )


def first_kernel(
    place, res, tiles, mid_tiles, owner, inverse_rows, a_out, near_out, far_out, winv_out,
    res_out, flat, held, picked, inverse_part, sems, side_sems,
):
    blocks, ext = held.shape[0], held.shape[1]
    width = a_out.shape[1]
    parts = sems.shape[0] - 1
    per = blocks // parts

    def copy(part):
        rows = pl.ds(part * per, per)
        return pltpu.make_async_copy(tiles.at[rows, 0], held.at[rows], sems.at[part])

    whole = pltpu.make_async_copy(res, flat, sems.at[parts])
    mids = mid_tiles.shape[0]
    last = mids - 1
    column = place[2]
    odd = place[0] % 2
    choose = lambda *values: jnp.where(
        column < 2,
        jnp.where(column == 0, values[0], values[1]),
        jnp.where(column == 2, values[2], values[3]),
    )
    up = choose(last, last, last - 1, 0), choose(1, 2, 2, 0)
    down = choose(0, 0, 1, last), choose(1, 0, 0, 2)
    tiles_at = [
        [jnp.where(odd == side, one, two) for one, two in zip(up, down)] for side in range(2)
    ] + [(0, 1), (last, 1)]
    share = inverse_part.shape[0]
    begin = pl.multiple_of(column * share, share)
    smalls = [
        pltpu.make_async_copy(inverse_rows.at[pl.ds(begin, share)], inverse_part, side_sems.at[4])
    ] + [
        pltpu.make_async_copy(mid_tiles.at[b, k], picked.at[n], side_sems.at[n])
        for n, (b, k) in enumerate(tiles_at)
    ]
    whole.start()
    for part in range(parts):
        copy(part).start()
    for small in smalls:
        small.start()
    eye = eye_mask(ext)
    quarter = blocks // 4
    rows = pl.ds(pl.multiple_of(column * quarter, quarter), quarter)
    lo, hi = split(owner[rows] - place[0] * (mids * ext), ext)
    mid_block, mid_hi = split(owner[blocks:], ext)
    for small in smalls:
        small.wait()
    extra = far_out.shape[0] - blocks
    singles = [
        jnp.concatenate(
            [
                mid_hi[first : first + 2].astype(F32),
                mid_block[first : first + 2].astype(F32),
                diag_row(picked[2 + side], eye),
                jnp.zeros((width - 5, ext), F32),
            ],
            axis=0,
        )
        for side, first in enumerate((last - 1, 0))
    ]
    tile_blocks = ext // width
    for n, (to, single) in enumerate(
        (
            (near_out, jnp.where(odd == 0, singles[0], singles[1])),
            (far_out, jnp.where(odd == 0, singles[1], singles[0])),
        )
    ):
        for k in range(tile_blocks):
            to[blocks + k] = picked[n, k * width : (k + 1) * width]
        to[blocks + tile_blocks] = hi.astype(F32).astype(BF16)
        to[blocks + tile_blocks + 1] = lo.astype(F32).astype(BF16)
        to[blocks + tile_blocks + 2] = single.astype(BF16)
    tall, wide = share // width, inverse_part.shape[1] // ext
    for i in range(tall):
        for k in range(wide):
            near_out[blocks + extra + i * wide + k] = inverse_part[
                i * width : (i + 1) * width, k * ext : (k + 1) * ext
            ].astype(BF16)

    for part in range(parts):
        copy(part).wait()
        if part == 0:
            whole.wait()
        for g in range(part * per, (part + 1) * per):
            winv = DAMPING * (1.0 / diag_row(held[g], eye))
            winv_out[pl.ds(g, 1), :] = winv
            r = flat[:, g * ext : (g + 1) * ext]
            res_out[g] = r
            value = (winv * r).astype(BF16)
            a_out[g] = value
            near_out[g] = value
            far_out[g] = value


def plan_kernel(place, index, after, owner, hot_out, plan):
    del after
    blocks, ext = index.shape[1], owner.shape[1]
    first = place[0] * blocks
    zero = 3 * blocks

    def row(g, most):
        away, block = [], []
        for s in range(1, 4):
            at = index[s, g] - first
            own = jnp.logical_and(at >= 0, at < blocks)
            away.append(jnp.where(own, 0, 1))
            block.append(at + blocks)
        count = away[0] + away[1] + away[2]
        one = jnp.where(away[0] == 1, 0, jnp.where(away[1] == 1, 1, 2))
        two = jnp.where(away[0] + away[1] == 2, 1, 2)
        pick = lambda k: jnp.where(k == 0, block[0], jnp.where(k == 1, block[1], block[2]))
        plan[0, g] = one + 1
        plan[1, g] = jnp.where(count >= 1, pick(one), zero)
        plan[2, g] = two + 1
        plan[3, g] = jnp.where(count >= 2, pick(two), zero)
        plan[4, g] = 0
        return jnp.maximum(most, count)

    plan[4, 0] = lax.fori_loop(0, blocks, row, 0, unroll=8)
    _, hi = split(owner[0:blocks], ext)
    for g in range(blocks):
        hot_out[:, g * ext : (g + 1) * ext] = one_hot(hi[g : g + 1, :], ext)


def own_rows(index, place, own, window, slots):
    blocks = own.shape[0]
    window[0:blocks] = own[...]
    window[blocks] = jnp.zeros_like(window[blocks])
    first = place[0] * blocks

    def local(s, g):
        at = index[s, g] - first
        return jnp.where(jnp.logical_and(at >= 0, at < blocks), at, blocks)

    def row(g):
        picked = [window[g]] + [window[local(s, g)] for s in range(1, slots)]
        return jnp.concatenate(picked, axis=1)

    return row


def own_first_kernel(index, place, tiles, own, out, turned_out, window):
    blocks, slots = tiles.shape[:2]
    row = own_rows(index, place, own, window, slots)
    for g in range(blocks):
        turned = [tiles[g, s].T for s in range(slots)]
        for s in range(slots):
            turned_out[g, s] = turned[s]
        out[g] = dot_nn(row(g), jnp.concatenate(turned, axis=0))


def own_kernel(index, place, turned, own, out, window):
    blocks, slots = turned.shape[:2]
    row = own_rows(index, place, own, window, slots)
    for g in range(blocks):
        out[g] = dot_nn(row(g), jnp.concatenate([turned[g, s] for s in range(slots)], axis=0))


def for_rows(index, plan, offset, tiles, window, part, blocks, then):
    window[3 * blocks] = jnp.zeros_like(window[3 * blocks])

    @pl.when(plan[4, 0] <= 2)
    def _():
        for g in range(blocks):
            picked = [window[plan[1, g]], window[plan[3, g]]]
            matched = [tiles[g, plan[0, g]], tiles[g, plan[2, g]]]
            added = dot_nn(jnp.concatenate(picked, axis=1), jnp.concatenate(matched, axis=0))
            then(g, part[g] + added)

    @pl.when(plan[4, 0] > 2)
    def _():
        @pl.loop(0, blocks)
        def _(g):
            then(g, fine_row(index, offset, tiles, window, g))


def sides_kernel(
    place, a, b, c, d, mid_tiles, owner, left_out, right_out, inverse_out, scale_out, mid_hot,
    mid_block, buffer,
):
    width, ext = a.shape[1:]
    tile_blocks = ext // width
    extra = tile_blocks + 3
    for n, piece in enumerate((a, b, c, d)):
        buffer[place[2] ^ n] = piece[...]
    share = inverse_out.shape[0] // 4
    wide = inverse_out.shape[1] // ext
    for out, first in ((left_out, 0), (right_out, extra)):
        for n in range(4):
            for k in range(tile_blocks):
                at = n * ext + k * width
                out[at : at + width] = buffer[n, first + k]
            out[HI_AT + n * width : HI_AT + (n + 1) * width] = buffer[n, first + tile_blocks]
            out[LO_AT + n * width : LO_AT + (n + 1) * width] = buffer[n, first + tile_blocks + 1]
        out[MISC_AT:MESSAGE] = buffer[0, first + tile_blocks + 2]
    for n in range(4):
        for i in range(share // width):
            rows = slice(n * share + i * width, n * share + (i + 1) * width)
            for k in range(wide):
                inverse_out[rows, k * ext : (k + 1) * ext] = buffer[n, 2 * extra + i * wide + k]
    mids = mid_tiles.shape[0]
    eye = eye_mask(ext)
    has_left, has_right = place[0] > 0, place[0] < place[1] - 1
    left_single, right_single = (m[MISC_AT:MESSAGE].astype(F32) for m in (left_out, right_out))
    scales = [DAMPING * (1.0 / diag_row(mid_tiles[b, 1], eye)) for b in range(mids)] + [
        inverse(diag_row(left_out[0:ext], eye), has_left),
        inverse(diag_row(right_out[0:ext], eye), has_right),
        inverse(left_single[4:5], has_left),
        inverse(right_single[4:5], has_right),
    ]
    scale_out[...] = jnp.concatenate(
        scales + [jnp.zeros((scale_out.shape[0] - len(scales), ext), F32)], axis=0
    )
    blocks = owner.shape[0] - mids
    own_block, own_hi = split(owner[blocks:], ext)
    block = [left_single[2:4].astype(jnp.int32), own_block, right_single[2:4].astype(jnp.int32)]
    hi = [left_single[0:2].astype(jnp.int32), own_hi, right_single[0:2].astype(jnp.int32)]
    hi = jnp.concatenate(hi, axis=0)
    start = place[0] - 2 + place[0] % 2
    mid_block[0 : mids + 4] = jnp.concatenate(block, axis=0) - start
    for b in range(mids + 4):
        mid_hot[:, b * ext : (b + 1) * ext] = one_hot(hi[b : b + 1], ext)


def side_hot_kernel(after, from_left, from_right, hot_left, hot_right):
    del after
    ext = hot_left.shape[0]
    blocks = hot_left.shape[1] // ext
    for message, hot in ((from_left, hot_left), (from_right, hot_right)):
        hi = as_int(message[HI_AT : HI_AT + blocks, :])
        for g in range(blocks):
            hot[:, g * ext : (g + 1) * ext] = one_hot(hi[g : g + 1, :], ext)


def fill_window(window, near, own, far, me):
    blocks = own.shape[0]
    window[pl.ds((1 - me % 2) * (2 * blocks), blocks)] = near[0:blocks]
    window[blocks : 2 * blocks] = own[...]
    window[pl.ds((me % 2) * (2 * blocks), blocks)] = far[0:blocks]


def fine_row(index, offset, tiles, window, g):
    slots = tiles.shape[1]
    picked = [window[index[s, g] - offset] for s in range(slots)]
    return dot_nn(
        jnp.concatenate(picked, axis=1),
        jnp.concatenate([tiles[g, s] for s in range(slots)], axis=0),
    )


def second_kernel(
    index, plan, place, tiles, near, own, far, part, res, winv, hot, basis_b, basis_c, basis_d, b_out,
    b16_out, b16_too, mine_out, window,
):
    del hot, basis_b, basis_c, basis_d
    blocks, ext = own.shape[0], own.shape[2]
    offset = (place[0] - 1) * blocks
    fill_window(window, near, own, far, place[0])

    def finish_row(g, product):
        w = winv[pl.ds(g, 1), :]
        r = res[g]
        b = w * r + w * (r - product)
        b_out[g] = b
        b16_out[g] = b.astype(BF16)
        b16_too[g] = b.astype(BF16)

    for_rows(index, plan, offset, tiles, window, part, blocks, finish_row)
    for n in range(blocks, b16_too.shape[0]):
        b16_too[n] = jnp.zeros_like(b16_too[n])
    odd = place[0] % 2
    extra = far.shape[0] - blocks
    mine_out[pl.ds((1 - odd) * extra, extra)] = near[blocks : blocks + extra]
    mine_out[pl.ds(odd * extra, extra)] = far[blocks:]
    mine_out[2 * extra :] = near[blocks + extra :]


def split(row, ext):
    return lax.shift_right_logical(row, ext.bit_length() - 1), row & (ext - 1)


def one_hot(row, n):
    ids = lax.broadcasted_iota(jnp.int32, (n, row.shape[1]), 0)
    return jnp.where(ids == row, 1.0, 0.0).astype(BF16)


def spread(value, row, n):
    return jnp.concatenate(
        [jnp.where(row == l, value, 0.0).astype(BF16) for l in range(n)], axis=0
    )


def edge(message, row, n=128):
    return message[row : row + n, :]


def as_int(row):
    return row.astype(F32).astype(jnp.int32)


def inverse(row, present):
    return DAMPING * (1.0 / jnp.where(present, row, 1.0))


def mid_product(mid_tiles, v, b):
    ext = mid_tiles.shape[2]
    count = mid_tiles.shape[0]
    ks = [k for k in range(3) if v.get(b - 1 + k) is not None]
    return dot_nt(
        jnp.concatenate([v[b - 1 + k] for k in ks], axis=1),
        jnp.concatenate([mid_tiles[b, k] for k in ks], axis=1),
    )


def third_kernel(
    index, plan, place, tiles, near, own, far, part, res, owner, hot, mid_tiles, from_left,
    from_right, scale, mid_hot, mid_block, fres_out, u_out, bpart_out, send, window, spread_rows,
):
    blocks, ext = own.shape[0], own.shape[2]
    width = own.shape[1]
    mids = mid_tiles.shape[0]
    me = place[0]
    offset = (me - 1) * blocks
    fill_window(window, near, own, far, place[0])

    def finish_row(g, product):
        r = res[g] - product
        fres_out[g] = r
        lo, _ = split(owner[pl.ds(g, 1), :] - me * (mids * ext), ext)
        at = g * ext if isinstance(g, int) else pl.multiple_of(g * ext, ext)
        spread_rows[:, pl.ds(at, ext)] = spread(r, lo, mids)

    for_rows(index, plan, offset, tiles, window, part, blocks, finish_row)
    quarters = [slice(n * blocks // 4 * ext, (n + 1) * blocks // 4 * ext) for n in range(4)]
    total = sum(dot_nt(spread_rows[:, q], hot[:, q]) for q in quarters)
    u = [total[b * width : (b + 1) * width] for b in range(mids)]
    winv = [scale[b : b + 1, :] for b in range(mids)]
    winv_left, winv_right = scale[mids : mids + 1, :], scale[mids + 1 : mids + 2, :]
    left_mid, left_next, left_far = (edge(from_left, 128 * k) for k in range(3))
    right_mid, right_prev, right_far = (edge(from_right, 128 * k) for k in range(3))
    a = [winv[b] * u[b] for b in range(mids)]
    a16 = {b: a[b].astype(BF16) for b in range(mids)}
    mine = {}
    for b in range(mids):
        mine[b] = a[b] + winv[b] * (u[b] - mid_product(mid_tiles, a16, b))
        u_out[b] = u[b]
        bpart_out[b] = mine[b]
    mine[-1] = -winv_left * dot_nt(a16[0], left_next)
    mine[mids] = -winv_right * dot_nt(a16[mids - 1], right_prev)
    p16 = {b: v.astype(BF16) for b, v in mine.items()}
    rest = {b: u[b] - mid_product(mid_tiles, p16, b) for b in range(mids)}
    rest[-1] = -(dot_nt(p16[-1], left_mid) + dot_nt(p16[0], left_next))
    rest[-2] = -dot_nt(p16[-1], left_far)
    rest[mids] = -(dot_nt(p16[mids], right_mid) + dot_nt(p16[mids - 1], right_prev))
    rest[mids + 1] = -dot_nt(p16[mids], right_far)
    spreads = [
        spread(rest[b], mid_block[b + 2 : b + 3, :], 4) for b in range(-2, mids + 2)
    ]
    coarse = dot_nt(jnp.concatenate(spreads, axis=1), mid_hot[...])
    coarse16 = coarse.astype(BF16)
    first, last = u[0].astype(BF16), u[mids - 1].astype(BF16)
    none = jnp.zeros_like(first)
    for d in range(send.shape[0]):
        for k in range(4):
            send[d, k] = coarse16[k * width : (k + 1) * width]
        send[d, 4] = jnp.where(me + 1 == d, last, jnp.where(me - 1 == d, first, none))


def mid_kernel(
    place, got, inverse_rows, partner_rows, mid_tiles, scale, mid_hot, mid_block, u, bpart,
    dpart_out, edges_out, near_out, far_out, next_out, beyond_out,
):
    ext = mid_tiles.shape[2]
    mids = mid_tiles.shape[0]
    peers = got.shape[0]
    width = got.shape[2]
    me = place[0]
    odd = me % 2
    rhs = []
    for k in range(peers):
        terms = [
            got[s, k - (s - 2 + s % 2)].astype(F32)
            for s in range(peers)
            if 0 <= k - (s - 2 + s % 2) < 4
        ]
        rhs.append(sum(terms[1:], terms[0]))
    rhs16 = jnp.concatenate([r.astype(BF16) for r in rhs], axis=1)
    mine = dot_nt(rhs16, inverse_rows[...].astype(BF16))
    other = dot_nt(rhs16, partner_rows[...])
    pair = jnp.concatenate(
        [jnp.where(odd == 0, mine, other), jnp.where(odd == 0, other, mine)], axis=0
    ).astype(BF16)
    winv = [scale[b : b + 1, :] for b in range(mids)]
    winv_left, winv_right = scale[mids : mids + 1, :], scale[mids + 1 : mids + 2, :]
    before = got[lax.rem(me + peers - 1, peers), 4].astype(F32)
    after = got[lax.rem(me + 1, peers), 4].astype(F32)
    a_before = (winv_left * before).astype(BF16)
    a_after = (winv_right * after).astype(BF16)
    c, c16 = {}, {}
    for b in range(mids):
        value = bpart[b]
        if b == 0:
            value = value - winv[b] * dot_nt(a_before, mid_tiles[b, 0])
        if b == mids - 1:
            value = value - winv[b] * dot_nt(a_after, mid_tiles[b, 2])
        hot = mid_hot[:, (b + 2) * ext : (b + 3) * ext]
        both = jnp.dot(pair, hot, preferred_element_type=F32)
        second = mid_block[b + 2 : b + 3, :] == 3 - 2 * odd
        c[b] = value + jnp.where(second, both[width:], both[:width])
        c16[b] = c[b].astype(BF16)
    d16 = []
    for b in range(mids):
        d = c[b] + winv[b] * (u[b] - mid_product(mid_tiles, c16, b))
        dpart_out[b] = d
        d16.append(d.astype(BF16))
    edges_out[0] = c16[0]
    edges_out[1] = c16[mids - 1]
    for b in range(mids):
        near_out[b] = d16[b]
        far_out[b] = d16[b]
    first, last = c16[0], c16[mids - 1]
    low = me % 4 < 2
    near_out[mids] = jnp.where(odd == 0, last, first)
    far_out[mids] = jnp.where(odd == 0, first, last)
    next_out[...] = jnp.where(low, last, first)
    beyond_out[...] = jnp.where(low, first, last)


def prolong(values, hot, lo, width, mids):
    both = jnp.dot(values, hot, preferred_element_type=F32)
    result = jnp.where(lo == 0, both[:width], 0.0)
    for l in range(1, mids):
        result = jnp.where(lo == l, both[l * width : (l + 1) * width], result)
    return result


def last_kernel(
    index, place, tiles, near, far, other, nexts, beyond, dpart, c_edges, mid_tiles, scale, owner, hot_own, from_left, hot_left,
    from_right, hot_right, b_in, fres, winv, basis_a, basis_b, basis_c, basis_d, out, gram_out, window,
    added, rounded, grams, result, sems,
):
    blocks, width, ext = b_in.shape
    mids = mid_tiles.shape[0]
    me, peers = place[0], place[1]
    odd = me % 2
    low = me % 4 < 2
    middle = jnp.logical_or(me % 4 == 1, me % 4 == 2)
    present = jnp.logical_and(me > 0, me < peers - 1)
    none = jnp.zeros_like(nexts[...])
    away = [
        jnp.where(middle, other[b], jnp.where(present, far[b], none)) for b in range(mids + 1)
    ]
    left = [jnp.where(odd == 1, near[b], away[b]) for b in range(mids + 1)]
    right = [jnp.where(odd == 1, away[b], near[b]) for b in range(mids + 1)]
    outer = jnp.where(jnp.logical_and(me > 1, me < peers - 2), beyond[...], none)
    far_left = jnp.where(low, outer, nexts[...])
    far_right = jnp.where(low, nexts[...], outer)
    row = lambda n: scale[n : n + 1, :]
    own = [dpart[b] for b in range(mids)]
    own[0] = own[0] - row(0) * dot_nt(left[mids], mid_tiles[0, 0])
    own[-1] = own[-1] - row(mids - 1) * dot_nt(right[mids], mid_tiles[mids - 1, 2])
    lefts = [v.astype(F32) for v in left[:mids]]
    lefts[0] = lefts[0] - row(mids + 2) * dot_nt(far_left, edge(from_left, 384))
    lefts[-1] = lefts[-1] - row(mids) * dot_nt(c_edges[0], edge(from_left, 128))
    rights = [v.astype(F32) for v in right[:mids]]
    rights[0] = rights[0] - row(mids + 1) * dot_nt(c_edges[1], edge(from_right, 128))
    rights[-1] = rights[-1] - row(mids + 3) * dot_nt(far_right, edge(from_right, 384))
    own16, left16, right16 = (
        jnp.concatenate([v.astype(BF16) for v in side], axis=0) for side in (own, lefts, rights)
    )
    own_lo, _ = split(owner[0:blocks] - me * (mids * ext), ext)
    left_lo, right_lo = (
        as_int(message[LO_AT : LO_AT + blocks, :]) for message in (from_left, from_right)
    )
    for g in range(0, blocks, 2):
        cols = slice(g * ext, (g + 2) * ext)
        for lo, hot, values, base in (
            (own_lo, hot_own, own16, blocks),
            (left_lo, hot_left, left16, 0),
            (right_lo, hot_right, right16, 2 * blocks),
        ):
            row = jnp.concatenate([lo[g : g + 1], lo[g + 1 : g + 2]], axis=1)
            value = prolong(values, hot[:, cols], row, width, mids)
            for n in range(2):
                half = value[:, n * ext : (n + 1) * ext]
                if base == blocks:
                    added[g + n] = half
                window[base + g + n] = half.astype(BF16)
    offset = (me - 1) * blocks
    count = sems.shape[0]
    per = blocks // count

    def copy(part):
        cols = pl.ds(part * per * ext, per * ext)
        return pltpu.make_async_copy(result.at[:, cols], out.at[:, cols], sems.at[part])

    for g in range(blocks):
        product = fine_row(index, offset, tiles, window, g)
        value = b_in[g] + added[g] + winv[pl.ds(g, 1), :] * (fres[g] - product)
        cols = slice(g * ext, (g + 1) * ext)
        result[:, cols] = value
        rounded[:, cols] = value.astype(BF16)
        if (g + 1) % per == 0:
            copy((g + 1) // per - 1).start()
    for n, piece in enumerate((basis_a, basis_b, basis_c, basis_d)):
        grams[place[2] ^ n] = dot_nt(rounded[...], piece[...])
    gram = jnp.concatenate([grams[n] for n in range(4)], axis=1)
    gram = jnp.concatenate([gram[: width // 2], gram[width // 2 :]], axis=1)
    for d in range(gram_out.shape[0]):
        gram_out[d] = gram
    for part in range(count):
        copy(part).wait()


def sum_kernel(got, out):
    total = got[0]
    for s in range(1, got.shape[0]):
        total = total + got[s]
    half, wide = out.shape[0] // 2, out.shape[1]
    out[0:half] = total[:, :wide]
    out[half:] = total[:, wide:]


def halo(for_partner, for_other):
    peers = lax.axis_size("rows")
    odd = [(i, i + 1) for i in range(1, peers - 1, 2)]
    even = [(i, i + 1) for i in range(0, peers - 1, 2)]
    swap = lambda pairs: pairs + [(j, i) for i, j in pairs]
    near = lax.ppermute(for_partner, "rows", swap(even))
    far = lax.ppermute(for_other, "rows", swap(odd))
    return near, far


def from_columns(value):
    peers = lax.axis_size("cols")
    swap = lambda v, n: lax.ppermute(v, "cols", [(i, i ^ n) for i in range(peers)])
    across = swap(value, 2)
    return [swap(value, 1), across, swap(across, 1)]


def on_device(
    residual_block, basis, fine_tiles, fine_index, mid_tiles, fine_owner, mid_owner, coarse_inverse
):
    peers = lax.axis_size("rows")
    me = lax.axis_index("rows")
    blocks, slots, ext, _ = fine_tiles.shape
    mids = mid_tiles.shape[0]
    count = blocks * ext
    width = residual_block.shape[1]
    res = residual_block.T
    index = fine_index.T
    place = jnp.stack([me, jnp.int32(peers), lax.axis_index("cols")])
    owner = jnp.concatenate([fine_owner, mid_owner]).reshape(blocks + mids, ext)
    shape = jax.ShapeDtypeStruct
    tile_bytes = fine_tiles.size * 2
    fine_flops = 2 * fine_tiles.size * width
    extra = ext // width + 3

    columns = lax.axis_size("cols")
    share = coarse_inverse.shape[0] // columns
    whole_row = coarse_inverse.shape[1]
    quarter = (share // width) * (whole_row // ext)

    a16, for_partner, for_other, winv, res_blocks = pl.pallas_call(
        first_kernel,
        in_specs=[SM] + [HBM] * 3 + [VM, HBM],
        out_specs=[VM] * 5,
        out_shape=[
            shape((blocks, width, ext), BF16),
            shape((blocks + extra + quarter, width, ext), BF16),
            shape((blocks + extra, width, ext), BF16),
            shape((blocks, ext), F32),
            shape((blocks, width, ext), F32),
        ],
        scratch_shapes=[
            pltpu.VMEM((width, count), F32),
            pltpu.VMEM((blocks, ext, ext), BF16),
            pltpu.VMEM((4, ext, ext), BF16),
            pltpu.VMEM((share, whole_row), F32),
            pltpu.SemaphoreType.DMA((5,)),
            pltpu.SemaphoreType.DMA((5,)),
        ],
        name="first_smoothing",
        **params(FIRST_LIMIT, count * ext, tile_bytes // 4),
    )(place, res, fine_tiles, mid_tiles, owner, coarse_inverse)

    near, far = halo(for_partner, for_other)
    hot_own, plan = pl.pallas_call(
        plan_kernel,
        in_specs=[SM, SM, ANY, VM],
        out_specs=[VM, SM],
        out_shape=[shape((ext, count), BF16), shape((5, blocks), jnp.int32)],
        name="one_hot_rows",
        **params(4, count * ext, 4 * tile_bytes),
    )(place, index, winv, owner)

    part_shape = shape((blocks, width, ext), F32)
    part, tiles = pl.pallas_call(
        own_first_kernel,
        in_specs=[SM, SM, VM, VM],
        out_specs=[VM, VM],
        out_shape=[part_shape, shape(fine_tiles.shape, BF16)],
        scratch_shapes=[pltpu.VMEM((blocks + 1, width, ext), BF16)],
        name="own_part_and_turned_tiles",
        **params(4, ext, ext),
    )(index, place, fine_tiles, a16)
    basis_pieces = [basis.T] + from_columns(basis.T)

    b32, b16, b16_too, mine = pl.pallas_call(
        second_kernel,
        in_specs=[SM] * 3 + [VM] * 7 + [ANY] * 4,
        out_specs=[VM] * 4,
        out_shape=[
            shape((blocks, width, ext), F32),
            shape((blocks, width, ext), BF16),
            shape((blocks + 1, width, ext), BF16),
            shape((2 * extra + quarter, width, ext), BF16),
        ],
        scratch_shapes=[pltpu.VMEM((3 * blocks + 1, width, ext), BF16)],
        name="second_smoothing",
        **params(6, fine_flops, tile_bytes),
    )(
        index, plan, place, tiles, near, a16, far, part, res_blocks, winv, hot_own,
        *basis_pieces[1:],
    )

    near, far = halo(b16_too, b16)
    part = pl.pallas_call(
        own_kernel,
        in_specs=[SM, SM, VM, VM],
        out_specs=VM,
        out_shape=part_shape,
        scratch_shapes=[pltpu.VMEM((blocks + 1, width, ext), BF16)],
        name="own_part_of_residual",
        **params(4, ext, ext),
    )(index, place, tiles, b16)
    from_left, from_right, partner_rows, scale, mid_hot, mid_block = pl.pallas_call(
        sides_kernel,
        in_specs=[SM] + [VM] * 6,
        out_specs=[VM] * 6,
        out_shape=[
            shape((MESSAGE, ext), BF16),
            shape((MESSAGE, ext), BF16),
            shape(coarse_inverse.shape, BF16),
            shape((16, ext), F32),
            shape((ext, (mids + 4) * ext), BF16),
            shape((16, ext), jnp.int32),
        ],
        scratch_shapes=[pltpu.VMEM((4, 2 * extra + quarter, width, ext), BF16)],
        name="side_messages",
        **params(4, ext, ext),
    )(place, mine, *from_columns(mine), mid_tiles, owner)

    fres, u, bpart, send = pl.pallas_call(
        third_kernel,
        in_specs=[SM] * 3 + [VM] * 14,
        out_specs=[VM] * 4,
        out_shape=[
            shape((blocks, width, ext), F32),
            shape((mids, width, ext), F32),
            shape((mids, width, ext), F32),
            shape((peers, 5, width, ext), BF16),
        ],
        scratch_shapes=[
            pltpu.VMEM((3 * blocks + 1, width, ext), BF16),
            pltpu.VMEM((mids * width, count), BF16),
        ],
        name="residual_and_restriction",
        **params(10, fine_flops, tile_bytes),
    )(
        index, plan, place, tiles, near, b16, far, part, res_blocks, owner, hot_own, mid_tiles,
        from_left, from_right, scale, mid_hot, mid_block,
    )

    got = lax.all_to_all(send, "rows", 0, 0)
    dpart, c_edges, *sends = pl.pallas_call(
        mid_kernel,
        in_specs=[SM] + [VM] * 9,
        out_specs=[VM] * 6,
        out_shape=[
            shape((mids, width, ext), F32),
            shape((2, width, ext), BF16),
            shape((mids + 1, width, ext), BF16),
            shape((mids + 1, width, ext), BF16),
            shape((width, ext), BF16),
            shape((width, ext), BF16),
        ],
        name="coarse_and_mid_level",
        **params(MID_LIMIT, 4 * width * coarse_inverse.size, coarse_inverse.size * 4),
    )(
        place, got, coarse_inverse, partner_rows, mid_tiles, scale, mid_hot, mid_block, u, bpart,
    )

    return finish(
        place, index, tiles, sends, dpart, c_edges, mid_tiles, scale, owner, hot_own, from_left, from_right,
        b32, fres, winv, basis_pieces,
    )


def finish(
    place, index, tiles, sends, dpart, c_edges, mid_tiles, scale, owner, hot_own, from_left, from_right, b32,
    fres, winv, basis_pieces,
):
    peers = lax.axis_size("rows")
    blocks, width, ext = b32.shape
    mids = mid_tiles.shape[0]
    count = blocks * ext
    shape = jax.ShapeDtypeStruct
    swap = lambda v, pairs: lax.ppermute(v, "rows", pairs + [(j, i) for i, j in pairs])
    flip = lambda v, n: lax.ppermute(v, "rows", [(i, i ^ n) for i in range(peers)])
    ends = [(0, 1), (peers - 2, peers - 1)] if peers > 4 else [(0, 1), (2, 3)]
    inner = range(2, peers - 4, 4)
    far = swap(sends[1], [(i + 1, i + 2) for i in inner] + [(i, i + 3) for i in inner] + ends)
    beyond = swap(sends[3], [(i + n, i + 2 + n) for i in inner for n in range(2)] + ends)
    near = flip(sends[0], 1)
    other = flip(sends[1], 3)
    nexts = flip(sends[2], 2)
    hot_left, hot_right = pl.pallas_call(
        side_hot_kernel,
        in_specs=[ANY, VM, VM],
        out_specs=[VM] * 2,
        out_shape=[shape((ext, count), BF16)] * 2,
        name="side_one_hot_rows",
        **params(4, ext, ext),
    )(c_edges, from_left, from_right)
    out, grams = pl.pallas_call(
        last_kernel,
        in_specs=[SM, SM] + [VM] * 23,
        out_specs=[HBM, VM],
        out_shape=[
            shape((width, count), F32),
            shape((peers, width // 2, 8 * width), F32),
        ],
        scratch_shapes=[
            pltpu.VMEM((3 * blocks, width, ext), BF16),
            pltpu.VMEM((blocks, width, ext), F32),
            pltpu.VMEM((width, count), BF16),
            pltpu.VMEM((4, width, width), F32),
            pltpu.VMEM((width, count), F32),
            pltpu.SemaphoreType.DMA((4,)),
        ],
        name="prolongation_and_last_smoothing",
        **params(8, 2 * tiles.size * width, tiles.size * 2),
    )(
        index, place, tiles, near, far, other, nexts, beyond, dpart, c_edges, mid_tiles, scale, owner, hot_own, from_left, hot_left,
        from_right, hot_right, b32, fres, winv, *basis_pieces,
    )
    gram = pl.pallas_call(
        sum_kernel,
        in_specs=[VM],
        out_specs=VM,
        out_shape=shape((width, 4 * width), F32),
        name="gram_sum",
        **params(4, 0, 0),
    )(lax.all_to_all(grams, "rows", 0, 0))
    return out.T, gram.T


def solution(mesh):
    in_specs = (
        P("rows", "cols"),
        P("rows", "cols"),
        P("rows", None, None, None),
        P("rows", None),
        P("rows", None, None, None),
        P("rows"),
        P("rows"),
        P("rows", None),
    )
    out_specs = (P("rows", "cols"), P(None, "cols"))
    return jax.shard_map(
        on_device, mesh=mesh, in_specs=in_specs, out_specs=out_specs, check_vma=False
    )
```

```python
import jax
import jax.numpy as jnp
from jax import lax
from jax.experimental import pallas as pl
from jax.experimental.pallas import tpu as pltpu
from jax.sharding import PartitionSpec as P

DAMPING = 0.6666666666666666
F32 = jnp.float32
BF16 = jnp.bfloat16
NT = (((1,), (1,)), ((), ()))
VM = pl.BlockSpec(memory_space=pltpu.VMEM)
SM = pl.BlockSpec(memory_space=pltpu.SMEM)
ANY = pl.BlockSpec(memory_space=pl.ANY)
HBM = pl.BlockSpec(memory_space=pltpu.HBM)

HI_AT, LO_AT, MISC_AT = 512, 576, 640
MESSAGE = 656
FIRST_LIMIT = 52
MID_LIMIT = 8


def dot_nn(a, b):
    return jnp.dot(a, b, preferred_element_type=F32)


def dot_nt(a, b):
    return lax.dot_general(a, b, NT, preferred_element_type=F32)


def eye_mask(n):
    return lax.broadcasted_iota(jnp.int32, (n, n), 0) == lax.broadcasted_iota(jnp.int32, (n, n), 1)


def diag_row(tile, eye):
    return jnp.sum(jnp.where(eye, tile.astype(F32), 0.0), axis=0, keepdims=True)


def params(mib, flops, size):
    return dict(
        compiler_params=pltpu.CompilerParams(vmem_limit_bytes=mib << 20),
        cost_estimate=pl.CostEstimate(flops=flops, bytes_accessed=size, transcendentals=0),
    )


def first_kernel(
    place, res, tiles, mid_tiles, owner, inverse_rows, a_out, near_out, far_out, winv_out,
    res_out, flat, held, picked, inverse_part, sems, side_sems,
):
    blocks, ext = held.shape[0], held.shape[1]
    width = a_out.shape[1]
    parts = sems.shape[0] - 1
    per = blocks // parts

    def copy(part):
        rows = pl.ds(part * per, per)
        return pltpu.make_async_copy(tiles.at[rows, 0], held.at[rows], sems.at[part])

    whole = pltpu.make_async_copy(res, flat, sems.at[parts])
    mids = mid_tiles.shape[0]
    last = mids - 1
    column = place[2]
    odd = place[0] % 2
    choose = lambda *values: jnp.where(
        column < 2,
        jnp.where(column == 0, values[0], values[1]),
        jnp.where(column == 2, values[2], values[3]),
    )
    up = choose(last, last, last - 1, 0), choose(1, 2, 2, 0)
    down = choose(0, 0, 1, last), choose(1, 0, 0, 2)
    tiles_at = [
        [jnp.where(odd == side, one, two) for one, two in zip(up, down)] for side in range(2)
    ] + [(0, 1), (last, 1)]
    share = inverse_part.shape[0]
    begin = pl.multiple_of(column * share, share)
    smalls = [
        pltpu.make_async_copy(inverse_rows.at[pl.ds(begin, share)], inverse_part, side_sems.at[4])
    ] + [
        pltpu.make_async_copy(mid_tiles.at[b, k], picked.at[n], side_sems.at[n])
        for n, (b, k) in enumerate(tiles_at)
    ]
    whole.start()
    for part in range(parts):
        copy(part).start()
    for small in smalls:
        small.start()
    eye = eye_mask(ext)
    quarter = blocks // 4
    rows = pl.ds(pl.multiple_of(column * quarter, quarter), quarter)
    lo, hi = split(owner[rows] - place[0] * (mids * ext), ext)
    mid_block, mid_hi = split(owner[blocks:], ext)
    for small in smalls:
        small.wait()
    extra = far_out.shape[0] - blocks
    singles = [
        jnp.concatenate(
            [
                mid_hi[first : first + 2].astype(F32),
                mid_block[first : first + 2].astype(F32),
                diag_row(picked[2 + side], eye),
                jnp.zeros((width - 5, ext), F32),
            ],
            axis=0,
        )
        for side, first in enumerate((last - 1, 0))
    ]
    tile_blocks = ext // width
    for n, (to, single) in enumerate(
        (
            (near_out, jnp.where(odd == 0, singles[0], singles[1])),
            (far_out, jnp.where(odd == 0, singles[1], singles[0])),
        )
    ):
        for k in range(tile_blocks):
            to[blocks + k] = picked[n, k * width : (k + 1) * width]
        to[blocks + tile_blocks] = hi.astype(F32).astype(BF16)
        to[blocks + tile_blocks + 1] = lo.astype(F32).astype(BF16)
        to[blocks + tile_blocks + 2] = single.astype(BF16)
    tall, wide = share // width, inverse_part.shape[1] // ext
    for i in range(tall):
        for k in range(wide):
            near_out[blocks + extra + i * wide + k] = inverse_part[
                i * width : (i + 1) * width, k * ext : (k + 1) * ext
            ].astype(BF16)

    for part in range(parts):
        copy(part).wait()
        if part == 0:
            whole.wait()
        for g in range(part * per, (part + 1) * per):
            winv = DAMPING * (1.0 / diag_row(held[g], eye))
            winv_out[pl.ds(g, 1), :] = winv
            r = flat[:, g * ext : (g + 1) * ext]
            res_out[g] = r
            value = (winv * r).astype(BF16)
            a_out[g] = value
            near_out[g] = value
            far_out[g] = value


def plan_kernel(place, index, after, owner, hot_out, plan):
    del after
    blocks, ext = index.shape[1], owner.shape[1]
    first = place[0] * blocks
    zero = 3 * blocks

    def row(g, most):
        away, block = [], []
        for s in range(1, 4):
            at = index[s, g] - first
            own = jnp.logical_and(at >= 0, at < blocks)
            away.append(jnp.where(own, 0, 1))
            block.append(at + blocks)
        count = away[0] + away[1] + away[2]
        one = jnp.where(away[0] == 1, 0, jnp.where(away[1] == 1, 1, 2))
        two = jnp.where(away[0] + away[1] == 2, 1, 2)
        pick = lambda k: jnp.where(k == 0, block[0], jnp.where(k == 1, block[1], block[2]))
        plan[0, g] = one + 1
        plan[1, g] = jnp.where(count >= 1, pick(one), zero)
        plan[2, g] = two + 1
        plan[3, g] = jnp.where(count >= 2, pick(two), zero)
        plan[4, g] = 0
        return jnp.maximum(most, count)

    plan[4, 0] = lax.fori_loop(0, blocks, row, 0, unroll=8)
    _, hi = split(owner[0:blocks], ext)
    for g in range(blocks):
        hot_out[:, g * ext : (g + 1) * ext] = one_hot(hi[g : g + 1, :], ext)


def own_rows(index, place, own, window, slots):
    blocks = own.shape[0]
    window[0:blocks] = own[...]
    window[blocks] = jnp.zeros_like(window[blocks])
    first = place[0] * blocks

    def local(s, g):
        at = index[s, g] - first
        return jnp.where(jnp.logical_and(at >= 0, at < blocks), at, blocks)

    def row(g):
        picked = [window[g]] + [window[local(s, g)] for s in range(1, slots)]
        return jnp.concatenate(picked, axis=1)

    return row


def own_first_kernel(index, place, plan, tiles, own, out, turned_out, window):
    del plan
    blocks, slots = tiles.shape[:2]
    row = own_rows(index, place, own, window, slots)
    for g in range(blocks):
        turned = [tiles[g, s].T for s in range(slots)]
        for s in range(slots):
            turned_out[g, s] = turned[s]
        out[g] = dot_nn(row(g), jnp.concatenate(turned, axis=0))


def own_kernel(index, place, turned, own, out, window):
    blocks, slots = turned.shape[:2]
    row = own_rows(index, place, own, window, slots)
    for g in range(blocks):
        out[g] = dot_nn(row(g), jnp.concatenate([turned[g, s] for s in range(slots)], axis=0))


def for_rows(index, plan, offset, tiles, window, part, blocks, then):
    window[3 * blocks] = jnp.zeros_like(window[3 * blocks])

    @pl.when(plan[4, 0] <= 2)
    def _():
        for g in range(blocks):
            picked = [window[plan[1, g]], window[plan[3, g]]]
            matched = [tiles[g, plan[0, g]], tiles[g, plan[2, g]]]
            added = dot_nn(jnp.concatenate(picked, axis=1), jnp.concatenate(matched, axis=0))
            then(g, part[g] + added)

    @pl.when(plan[4, 0] > 2)
    def _():
        @pl.loop(0, blocks)
        def _(g):
            then(g, fine_row(index, offset, tiles, window, g))


def sides_kernel(
    place, a, b, c, d, rows_a, rows_b, rows_c, rows_d, mid_tiles, owner, left_out, right_out,
    inverse_out, scale_out, mid_hot, mid_block, buffer, rows_buffer,
):
    width, ext = a.shape[1:]
    tile_blocks = ext // width
    extra = tile_blocks + 3
    for n, piece in enumerate((a, b, c, d)):
        buffer[place[2] ^ n] = piece[...]
    for n, piece in enumerate((rows_a, rows_b, rows_c, rows_d)):
        rows_buffer[place[2] ^ n] = piece[...]
    share = inverse_out.shape[0] // 4
    wide = inverse_out.shape[1] // ext
    for out, first in ((left_out, 0), (right_out, extra)):
        for n in range(4):
            for k in range(tile_blocks):
                at = n * ext + k * width
                out[at : at + width] = buffer[n, first + k]
            out[HI_AT + n * width : HI_AT + (n + 1) * width] = buffer[n, first + tile_blocks]
            out[LO_AT + n * width : LO_AT + (n + 1) * width] = buffer[n, first + tile_blocks + 1]
        out[MISC_AT:MESSAGE] = buffer[0, first + tile_blocks + 2]
    for n in range(4):
        for i in range(share // width):
            rows = slice(n * share + i * width, n * share + (i + 1) * width)
            for k in range(wide):
                inverse_out[rows, k * ext : (k + 1) * ext] = rows_buffer[n, i * wide + k]
    mids = mid_tiles.shape[0]
    eye = eye_mask(ext)
    has_left, has_right = place[0] > 0, place[0] < place[1] - 1
    left_single, right_single = (m[MISC_AT:MESSAGE].astype(F32) for m in (left_out, right_out))
    scales = [DAMPING * (1.0 / diag_row(mid_tiles[b, 1], eye)) for b in range(mids)] + [
        inverse(diag_row(left_out[0:ext], eye), has_left),
        inverse(diag_row(right_out[0:ext], eye), has_right),
        inverse(left_single[4:5], has_left),
        inverse(right_single[4:5], has_right),
    ]
    scale_out[...] = jnp.concatenate(
        scales + [jnp.zeros((scale_out.shape[0] - len(scales), ext), F32)], axis=0
    )
    blocks = owner.shape[0] - mids
    own_block, own_hi = split(owner[blocks:], ext)
    block = [left_single[2:4].astype(jnp.int32), own_block, right_single[2:4].astype(jnp.int32)]
    hi = [left_single[0:2].astype(jnp.int32), own_hi, right_single[0:2].astype(jnp.int32)]
    hi = jnp.concatenate(hi, axis=0)
    start = place[0] - 2 + place[0] % 2
    mid_block[0 : mids + 4] = jnp.concatenate(block, axis=0) - start
    for b in range(mids + 4):
        mid_hot[:, b * ext : (b + 1) * ext] = one_hot(hi[b : b + 1], ext)


def side_hot_kernel(after, from_left, from_right, hot_left, hot_right):
    del after
    ext = hot_left.shape[0]
    blocks = hot_left.shape[1] // ext
    for message, hot in ((from_left, hot_left), (from_right, hot_right)):
        hi = as_int(message[HI_AT : HI_AT + blocks, :])
        for g in range(blocks):
            hot[:, g * ext : (g + 1) * ext] = one_hot(hi[g : g + 1, :], ext)


def fill_window(window, near, own, far, me):
    blocks = own.shape[0]
    window[pl.ds((1 - me % 2) * (2 * blocks), blocks)] = near[0:blocks]
    window[blocks : 2 * blocks] = own[...]
    window[pl.ds((me % 2) * (2 * blocks), blocks)] = far[0:blocks]


def fine_row(index, offset, tiles, window, g):
    slots = tiles.shape[1]
    picked = [window[index[s, g] - offset] for s in range(slots)]
    return dot_nn(
        jnp.concatenate(picked, axis=1),
        jnp.concatenate([tiles[g, s] for s in range(slots)], axis=0),
    )


def second_kernel(
    index, plan, place, tiles, near, own, far, part, res, winv, hot, basis_b, basis_c, basis_d, b_out,
    b16_out, b16_too, mine_out, rows_out, window,
):
    del hot, basis_b, basis_c, basis_d
    blocks, ext = own.shape[0], own.shape[2]
    offset = (place[0] - 1) * blocks
    fill_window(window, near, own, far, place[0])

    def finish_row(g, product):
        w = winv[pl.ds(g, 1), :]
        r = res[g]
        b = w * r + w * (r - product)
        b_out[g] = b
        b16_out[g] = b.astype(BF16)
        b16_too[g] = b.astype(BF16)

    for_rows(index, plan, offset, tiles, window, part, blocks, finish_row)
    for n in range(blocks, b16_too.shape[0]):
        b16_too[n] = jnp.zeros_like(b16_too[n])
    odd = place[0] % 2
    extra = far.shape[0] - blocks
    mine_out[pl.ds((1 - odd) * extra, extra)] = near[blocks : blocks + extra]
    mine_out[pl.ds(odd * extra, extra)] = far[blocks:]
    rows_out[...] = near[blocks + extra :]


def split(row, ext):
    return lax.shift_right_logical(row, ext.bit_length() - 1), row & (ext - 1)


def one_hot(row, n):
    ids = lax.broadcasted_iota(jnp.int32, (n, row.shape[1]), 0)
    return jnp.where(ids == row, 1.0, 0.0).astype(BF16)


def spread(value, row, n):
    return jnp.concatenate(
        [jnp.where(row == l, value, 0.0).astype(BF16) for l in range(n)], axis=0
    )


def edge(message, row, n=128):
    return message[row : row + n, :]


def as_int(row):
    return row.astype(F32).astype(jnp.int32)


def inverse(row, present):
    return DAMPING * (1.0 / jnp.where(present, row, 1.0))


def mid_product(mid_tiles, v, b):
    ext = mid_tiles.shape[2]
    count = mid_tiles.shape[0]
    ks = [k for k in range(3) if v.get(b - 1 + k) is not None]
    return dot_nt(
        jnp.concatenate([v[b - 1 + k] for k in ks], axis=1),
        jnp.concatenate([mid_tiles[b, k] for k in ks], axis=1),
    )


def third_kernel(
    index, plan, place, tiles, near, own, far, part, res, owner, hot, mid_tiles, from_left,
    from_right, scale, mid_hot, mid_block, fres_out, u_out, bpart_out, send, window, spread_rows,
):
    blocks, ext = own.shape[0], own.shape[2]
    width = own.shape[1]
    mids = mid_tiles.shape[0]
    me = place[0]
    offset = (me - 1) * blocks
    fill_window(window, near, own, far, place[0])

    def finish_row(g, product):
        r = res[g] - product
        fres_out[g] = r
        lo, _ = split(owner[pl.ds(g, 1), :] - me * (mids * ext), ext)
        at = g * ext if isinstance(g, int) else pl.multiple_of(g * ext, ext)
        spread_rows[:, pl.ds(at, ext)] = spread(r, lo, mids)

    for_rows(index, plan, offset, tiles, window, part, blocks, finish_row)
    quarters = [slice(n * blocks // 4 * ext, (n + 1) * blocks // 4 * ext) for n in range(4)]
    total = sum(dot_nt(spread_rows[:, q], hot[:, q]) for q in quarters)
    u = [total[b * width : (b + 1) * width] for b in range(mids)]
    winv = [scale[b : b + 1, :] for b in range(mids)]
    winv_left, winv_right = scale[mids : mids + 1, :], scale[mids + 1 : mids + 2, :]
    left_mid, left_next, left_far = (edge(from_left, 128 * k) for k in range(3))
    right_mid, right_prev, right_far = (edge(from_right, 128 * k) for k in range(3))
    a = [winv[b] * u[b] for b in range(mids)]
    a16 = {b: a[b].astype(BF16) for b in range(mids)}
    mine = {}
    for b in range(mids):
        mine[b] = a[b] + winv[b] * (u[b] - mid_product(mid_tiles, a16, b))
        u_out[b] = u[b]
        bpart_out[b] = mine[b]
    mine[-1] = -winv_left * dot_nt(a16[0], left_next)
    mine[mids] = -winv_right * dot_nt(a16[mids - 1], right_prev)
    p16 = {b: v.astype(BF16) for b, v in mine.items()}
    rest = {b: u[b] - mid_product(mid_tiles, p16, b) for b in range(mids)}
    rest[-1] = -(dot_nt(p16[-1], left_mid) + dot_nt(p16[0], left_next))
    rest[-2] = -dot_nt(p16[-1], left_far)
    rest[mids] = -(dot_nt(p16[mids], right_mid) + dot_nt(p16[mids - 1], right_prev))
    rest[mids + 1] = -dot_nt(p16[mids], right_far)
    spreads = [
        spread(rest[b], mid_block[b + 2 : b + 3, :], 4) for b in range(-2, mids + 2)
    ]
    coarse = dot_nt(jnp.concatenate(spreads, axis=1), mid_hot[...])
    coarse16 = coarse.astype(BF16)
    first, last = u[0].astype(BF16), u[mids - 1].astype(BF16)
    none = jnp.zeros_like(first)
    for d in range(send.shape[0]):
        for k in range(4):
            send[d, k] = coarse16[k * width : (k + 1) * width]
        send[d, 4] = jnp.where(me + 1 == d, last, jnp.where(me - 1 == d, first, none))


def mid_kernel(
    place, got, inverse_rows, partner_rows, mid_tiles, scale, mid_hot, mid_block, u, bpart,
    dpart_out, edges_out, near_out, far_out, next_out, beyond_out,
):
    ext = mid_tiles.shape[2]
    mids = mid_tiles.shape[0]
    peers = got.shape[0]
    width = got.shape[2]
    me = place[0]
    odd = me % 2
    rhs = []
    for k in range(peers):
        terms = [
            got[s, k - (s - 2 + s % 2)].astype(F32)
            for s in range(peers)
            if 0 <= k - (s - 2 + s % 2) < 4
        ]
        rhs.append(sum(terms[1:], terms[0]))
    rhs16 = jnp.concatenate([r.astype(BF16) for r in rhs], axis=1)
    mine = dot_nt(rhs16, inverse_rows[...].astype(BF16))
    other = dot_nt(rhs16, partner_rows[...])
    pair = jnp.concatenate(
        [jnp.where(odd == 0, mine, other), jnp.where(odd == 0, other, mine)], axis=0
    ).astype(BF16)
    winv = [scale[b : b + 1, :] for b in range(mids)]
    winv_left, winv_right = scale[mids : mids + 1, :], scale[mids + 1 : mids + 2, :]
    before = got[lax.rem(me + peers - 1, peers), 4].astype(F32)
    after = got[lax.rem(me + 1, peers), 4].astype(F32)
    a_before = (winv_left * before).astype(BF16)
    a_after = (winv_right * after).astype(BF16)
    c, c16 = {}, {}
    for b in range(mids):
        value = bpart[b]
        if b == 0:
            value = value - winv[b] * dot_nt(a_before, mid_tiles[b, 0])
        if b == mids - 1:
            value = value - winv[b] * dot_nt(a_after, mid_tiles[b, 2])
        hot = mid_hot[:, (b + 2) * ext : (b + 3) * ext]
        both = jnp.dot(pair, hot, preferred_element_type=F32)
        second = mid_block[b + 2 : b + 3, :] == 3 - 2 * odd
        c[b] = value + jnp.where(second, both[width:], both[:width])
        c16[b] = c[b].astype(BF16)
    d16 = []
    for b in range(mids):
        d = c[b] + winv[b] * (u[b] - mid_product(mid_tiles, c16, b))
        dpart_out[b] = d
        d16.append(d.astype(BF16))
    edges_out[0] = c16[0]
    edges_out[1] = c16[mids - 1]
    for b in range(mids):
        near_out[b] = d16[b]
        far_out[b] = d16[b]
    first, last = c16[0], c16[mids - 1]
    low = me % 4 < 2
    near_out[mids] = jnp.where(odd == 0, last, first)
    far_out[mids] = jnp.where(odd == 0, first, last)
    next_out[...] = jnp.where(low, last, first)
    beyond_out[...] = jnp.where(low, first, last)


def prolong(values, hot, lo, width, mids):
    both = jnp.dot(values, hot, preferred_element_type=F32)
    result = jnp.where(lo == 0, both[:width], 0.0)
    for l in range(1, mids):
        result = jnp.where(lo == l, both[l * width : (l + 1) * width], result)
    return result


def last_kernel(
    index, place, tiles, near, far, other, nexts, beyond, dpart, c_edges, mid_tiles, scale, owner, hot_own, from_left, hot_left,
    from_right, hot_right, b_in, fres, winv, basis_a, basis_b, basis_c, basis_d, out, gram_out, window,
    added, rounded, grams, result, sems,
):
    blocks, width, ext = b_in.shape
    mids = mid_tiles.shape[0]
    me, peers = place[0], place[1]
    odd = me % 2
    low = me % 4 < 2
    middle = jnp.logical_or(me % 4 == 1, me % 4 == 2)
    present = jnp.logical_and(me > 0, me < peers - 1)
    none = jnp.zeros_like(nexts[...])
    away = [
        jnp.where(middle, other[b], jnp.where(present, far[b], none)) for b in range(mids + 1)
    ]
    left = [jnp.where(odd == 1, near[b], away[b]) for b in range(mids + 1)]
    right = [jnp.where(odd == 1, away[b], near[b]) for b in range(mids + 1)]
    outer = jnp.where(jnp.logical_and(me > 1, me < peers - 2), beyond[...], none)
    far_left = jnp.where(low, outer, nexts[...])
    far_right = jnp.where(low, nexts[...], outer)
    row = lambda n: scale[n : n + 1, :]
    own = [dpart[b] for b in range(mids)]
    own[0] = own[0] - row(0) * dot_nt(left[mids], mid_tiles[0, 0])
    own[-1] = own[-1] - row(mids - 1) * dot_nt(right[mids], mid_tiles[mids - 1, 2])
    lefts = [v.astype(F32) for v in left[:mids]]
    lefts[0] = lefts[0] - row(mids + 2) * dot_nt(far_left, edge(from_left, 384))
    lefts[-1] = lefts[-1] - row(mids) * dot_nt(c_edges[0], edge(from_left, 128))
    rights = [v.astype(F32) for v in right[:mids]]
    rights[0] = rights[0] - row(mids + 1) * dot_nt(c_edges[1], edge(from_right, 128))
    rights[-1] = rights[-1] - row(mids + 3) * dot_nt(far_right, edge(from_right, 384))
    own16, left16, right16 = (
        jnp.concatenate([v.astype(BF16) for v in side], axis=0) for side in (own, lefts, rights)
    )
    own_lo, _ = split(owner[0:blocks] - me * (mids * ext), ext)
    left_lo, right_lo = (
        as_int(message[LO_AT : LO_AT + blocks, :]) for message in (from_left, from_right)
    )
    for g in range(0, blocks, 2):
        cols = slice(g * ext, (g + 2) * ext)
        for lo, hot, values, base in (
            (own_lo, hot_own, own16, blocks),
            (left_lo, hot_left, left16, 0),
            (right_lo, hot_right, right16, 2 * blocks),
        ):
            row = jnp.concatenate([lo[g : g + 1], lo[g + 1 : g + 2]], axis=1)
            value = prolong(values, hot[:, cols], row, width, mids)
            for n in range(2):
                half = value[:, n * ext : (n + 1) * ext]
                if base == blocks:
                    added[g + n] = half
                window[base + g + n] = half.astype(BF16)
    offset = (me - 1) * blocks
    count = sems.shape[0]
    per = blocks // count

    def copy(part):
        cols = pl.ds(part * per * ext, per * ext)
        return pltpu.make_async_copy(result.at[:, cols], out.at[:, cols], sems.at[part])

    for g in range(blocks):
        product = fine_row(index, offset, tiles, window, g)
        value = b_in[g] + added[g] + winv[pl.ds(g, 1), :] * (fres[g] - product)
        cols = slice(g * ext, (g + 1) * ext)
        result[:, cols] = value
        rounded[:, cols] = value.astype(BF16)
        if (g + 1) % per == 0:
            copy((g + 1) // per - 1).start()
    for n, piece in enumerate((basis_a, basis_b, basis_c, basis_d)):
        grams[place[2] ^ n] = dot_nt(rounded[...], piece[...])
    gram = jnp.concatenate([grams[n] for n in range(4)], axis=1)
    gram = jnp.concatenate([gram[: width // 2], gram[width // 2 :]], axis=1)
    for d in range(gram_out.shape[0]):
        gram_out[d] = gram
    for part in range(count):
        copy(part).wait()


def sum_kernel(got, out):
    total = got[0]
    for s in range(1, got.shape[0]):
        total = total + got[s]
    half, wide = out.shape[0] // 2, out.shape[1]
    out[0:half] = total[:, :wide]
    out[half:] = total[:, wide:]


def halo(for_partner, for_other):
    peers = lax.axis_size("rows")
    odd = [(i, i + 1) for i in range(1, peers - 1, 2)]
    even = [(i, i + 1) for i in range(0, peers - 1, 2)]
    swap = lambda pairs: pairs + [(j, i) for i, j in pairs]
    near = lax.ppermute(for_partner, "rows", swap(even))
    far = lax.ppermute(for_other, "rows", swap(odd))
    return near, far


def relay_kernel(value, after, out):
    del after
    out[...] = value[...]


def from_columns(value, relay=lambda v: v):
    peers = lax.axis_size("cols")
    swap = lambda v, n: lax.ppermute(v, "cols", [(i, i ^ n) for i in range(peers)])
    across = swap(value, 2)
    return [swap(value, 1), across, swap(relay(across), 1)]


def on_device(
    residual_block, basis, fine_tiles, fine_index, mid_tiles, fine_owner, mid_owner, coarse_inverse
):
    peers = lax.axis_size("rows")
    me = lax.axis_index("rows")
    blocks, slots, ext, _ = fine_tiles.shape
    mids = mid_tiles.shape[0]
    count = blocks * ext
    width = residual_block.shape[1]
    res = residual_block.T
    index = fine_index.T
    place = jnp.stack([me, jnp.int32(peers), lax.axis_index("cols")])
    owner = jnp.concatenate([fine_owner, mid_owner]).reshape(blocks + mids, ext)
    shape = jax.ShapeDtypeStruct
    tile_bytes = fine_tiles.size * 2
    fine_flops = 2 * fine_tiles.size * width
    extra = ext // width + 3

    columns = lax.axis_size("cols")
    share = coarse_inverse.shape[0] // columns
    whole_row = coarse_inverse.shape[1]
    quarter = (share // width) * (whole_row // ext)

    a16, for_partner, for_other, winv, res_blocks = pl.pallas_call(
        first_kernel,
        in_specs=[SM] + [HBM] * 3 + [VM, HBM],
        out_specs=[VM] * 5,
        out_shape=[
            shape((blocks, width, ext), BF16),
            shape((blocks + extra + quarter, width, ext), BF16),
            shape((blocks + extra, width, ext), BF16),
            shape((blocks, ext), F32),
            shape((blocks, width, ext), F32),
        ],
        scratch_shapes=[
            pltpu.VMEM((width, count), F32),
            pltpu.VMEM((blocks, ext, ext), BF16),
            pltpu.VMEM((4, ext, ext), BF16),
            pltpu.VMEM((share, whole_row), F32),
            pltpu.SemaphoreType.DMA((5,)),
            pltpu.SemaphoreType.DMA((5,)),
        ],
        name="first_smoothing",
        **params(FIRST_LIMIT, count * ext, tile_bytes // 4),
    )(place, res, fine_tiles, mid_tiles, owner, coarse_inverse)

    near, far = halo(for_partner, for_other)
    hot_own, plan = pl.pallas_call(
        plan_kernel,
        in_specs=[SM, SM, ANY, VM],
        out_specs=[VM, SM],
        out_shape=[shape((ext, count), BF16), shape((5, blocks), jnp.int32)],
        name="one_hot_rows",
        **params(4, count * ext, 4 * tile_bytes),
    )(place, index, winv, owner)

    part_shape = shape((blocks, width, ext), F32)
    part, tiles = pl.pallas_call(
        own_first_kernel,
        in_specs=[SM, SM, SM, VM, VM],
        out_specs=[VM, VM],
        out_shape=[part_shape, shape(fine_tiles.shape, BF16)],
        scratch_shapes=[pltpu.VMEM((blocks + 1, width, ext), BF16)],
        name="own_part_and_turned_tiles",
        **params(4, ext, ext),
    )(index, place, plan, fine_tiles, a16)
    basis_pieces = [basis.T] + from_columns(basis.T)

    b32, b16, b16_too, mine, mine_rows = pl.pallas_call(
        second_kernel,
        in_specs=[SM] * 3 + [VM] * 7 + [ANY] * 4,
        out_specs=[VM] * 5,
        out_shape=[
            shape((blocks, width, ext), F32),
            shape((blocks, width, ext), BF16),
            shape((blocks + 1, width, ext), BF16),
            shape((2 * extra, width, ext), BF16),
            shape((quarter, width, ext), BF16),
        ],
        scratch_shapes=[pltpu.VMEM((3 * blocks + 1, width, ext), BF16)],
        name="second_smoothing",
        **params(6, fine_flops, tile_bytes),
    )(
        index, plan, place, tiles, near, a16, far, part, res_blocks, winv, hot_own,
        *basis_pieces[1:],
    )

    near, far = halo(b16_too, b16)
    part = pl.pallas_call(
        own_kernel,
        in_specs=[SM, SM, VM, VM],
        out_specs=VM,
        out_shape=part_shape,
        scratch_shapes=[pltpu.VMEM((blocks + 1, width, ext), BF16)],
        name="own_part_of_residual",
        **params(4, ext, ext),
    )(index, place, tiles, b16)
    def relay(value):
        return pl.pallas_call(
            relay_kernel,
            in_specs=[VM, ANY],
            out_specs=VM,
            out_shape=shape(value.shape, value.dtype),
            name="relay",
            **params(4, ext, ext),
        )(value, part)

    from_left, from_right, partner_rows, scale, mid_hot, mid_block = pl.pallas_call(
        sides_kernel,
        in_specs=[SM] + [VM] * 10,
        out_specs=[VM] * 6,
        out_shape=[
            shape((MESSAGE, ext), BF16),
            shape((MESSAGE, ext), BF16),
            shape(coarse_inverse.shape, BF16),
            shape((16, ext), F32),
            shape((ext, (mids + 4) * ext), BF16),
            shape((16, ext), jnp.int32),
        ],
        scratch_shapes=[
            pltpu.VMEM((4, 2 * extra, width, ext), BF16),
            pltpu.VMEM((4, quarter, width, ext), BF16),
        ],
        name="side_messages",
        **params(4, ext, ext),
    )(
        place, mine, *from_columns(mine, relay), mine_rows, *from_columns(mine_rows, relay), mid_tiles, owner,
    )

    fres, u, bpart, send = pl.pallas_call(
        third_kernel,
        in_specs=[SM] * 3 + [VM] * 14,
        out_specs=[VM] * 4,
        out_shape=[
            shape((blocks, width, ext), F32),
            shape((mids, width, ext), F32),
            shape((mids, width, ext), F32),
            shape((peers, 5, width, ext), BF16),
        ],
        scratch_shapes=[
            pltpu.VMEM((3 * blocks + 1, width, ext), BF16),
            pltpu.VMEM((mids * width, count), BF16),
        ],
        name="residual_and_restriction",
        **params(10, fine_flops, tile_bytes),
    )(
        index, plan, place, tiles, near, b16, far, part, res_blocks, owner, hot_own, mid_tiles,
        from_left, from_right, scale, mid_hot, mid_block,
    )

    got = lax.all_to_all(send, "rows", 0, 0)
    dpart, c_edges, *sends = pl.pallas_call(
        mid_kernel,
        in_specs=[SM] + [VM] * 9,
        out_specs=[VM] * 6,
        out_shape=[
            shape((mids, width, ext), F32),
            shape((2, width, ext), BF16),
            shape((mids + 1, width, ext), BF16),
            shape((mids + 1, width, ext), BF16),
            shape((width, ext), BF16),
            shape((width, ext), BF16),
        ],
        name="coarse_and_mid_level",
        **params(MID_LIMIT, 4 * width * coarse_inverse.size, coarse_inverse.size * 4),
    )(
        place, got, coarse_inverse, partner_rows, mid_tiles, scale, mid_hot, mid_block, u, bpart,
    )

    return finish(
        place, index, tiles, sends, dpart, c_edges, mid_tiles, scale, owner, hot_own, from_left, from_right,
        b32, fres, winv, basis_pieces,
    )


def finish(
    place, index, tiles, sends, dpart, c_edges, mid_tiles, scale, owner, hot_own, from_left, from_right, b32,
    fres, winv, basis_pieces,
):
    peers = lax.axis_size("rows")
    blocks, width, ext = b32.shape
    mids = mid_tiles.shape[0]
    count = blocks * ext
    shape = jax.ShapeDtypeStruct
    swap = lambda v, pairs: lax.ppermute(v, "rows", pairs + [(j, i) for i, j in pairs])
    flip = lambda v, n: lax.ppermute(v, "rows", [(i, i ^ n) for i in range(peers)])
    ends = [(0, 1), (peers - 2, peers - 1)] if peers > 4 else [(0, 1), (2, 3)]
    inner = range(2, peers - 4, 4)
    far = swap(sends[1], [(i + 1, i + 2) for i in inner] + [(i, i + 3) for i in inner] + ends)
    beyond = swap(sends[3], [(i + n, i + 2 + n) for i in inner for n in range(2)] + ends)
    near = flip(sends[0], 1)
    other = flip(sends[1], 3)
    nexts = flip(sends[2], 2)
    hot_left, hot_right = pl.pallas_call(
        side_hot_kernel,
        in_specs=[ANY, VM, VM],
        out_specs=[VM] * 2,
        out_shape=[shape((ext, count), BF16)] * 2,
        name="side_one_hot_rows",
        **params(4, ext, ext),
    )(c_edges, from_left, from_right)
    out, grams = pl.pallas_call(
        last_kernel,
        in_specs=[SM, SM] + [VM] * 23,
        out_specs=[HBM, VM],
        out_shape=[
            shape((width, count), F32),
            shape((peers, width // 2, 8 * width), F32),
        ],
        scratch_shapes=[
            pltpu.VMEM((3 * blocks, width, ext), BF16),
            pltpu.VMEM((blocks, width, ext), F32),
            pltpu.VMEM((width, count), BF16),
            pltpu.VMEM((4, width, width), F32),
            pltpu.VMEM((width, count), F32),
            pltpu.SemaphoreType.DMA((2,)),
        ],
        name="prolongation_and_last_smoothing",
        **params(8, 2 * tiles.size * width, tiles.size * 2),
    )(
        index, place, tiles, near, far, other, nexts, beyond, dpart, c_edges, mid_tiles, scale, owner, hot_own, from_left, hot_left,
        from_right, hot_right, b32, fres, winv, *basis_pieces,
    )
    gram = pl.pallas_call(
        sum_kernel,
        in_specs=[VM],
        out_specs=VM,
        out_shape=shape((width, 4 * width), F32),
        name="gram_sum",
        **params(4, 0, 0),
    )(lax.all_to_all(grams, "rows", 0, 0))
    return out.T, gram.T


def solution(mesh):
    in_specs = (
        P("rows", "cols"),
        P("rows", "cols"),
        P("rows", None, None, None),
        P("rows", None),
        P("rows", None, None, None),
        P("rows"),
        P("rows"),
        P("rows", None),
    )
    out_specs = (P("rows", "cols"), P(None, "cols"))
    return jax.shard_map(
        on_device, mesh=mesh, in_specs=in_specs, out_specs=out_specs, check_vma=False
    )
```

```python
import jax
import jax.numpy as jnp
from jax import lax
from jax.experimental import pallas as pl
from jax.experimental.pallas import tpu as pltpu
from jax.sharding import PartitionSpec as P

DAMPING = 0.6666666666666666
F32 = jnp.float32
BF16 = jnp.bfloat16
NT = (((1,), (1,)), ((), ()))
VM = pl.BlockSpec(memory_space=pltpu.VMEM)
SM = pl.BlockSpec(memory_space=pltpu.SMEM)
ANY = pl.BlockSpec(memory_space=pl.ANY)
HBM = pl.BlockSpec(memory_space=pltpu.HBM)

HI_AT, LO_AT, MISC_AT = 512, 576, 640
MESSAGE = 656
FIRST_LIMIT = 52
MID_LIMIT = 8


def dot_nn(a, b):
    return jnp.dot(a, b, preferred_element_type=F32)


def dot_nt(a, b):
    return lax.dot_general(a, b, NT, preferred_element_type=F32)


def eye_mask(n):
    return lax.broadcasted_iota(jnp.int32, (n, n), 0) == lax.broadcasted_iota(jnp.int32, (n, n), 1)


def diag_row(tile, eye):
    return jnp.sum(jnp.where(eye, tile.astype(F32), 0.0), axis=0, keepdims=True)


def params(mib, flops, size):
    return dict(
        compiler_params=pltpu.CompilerParams(vmem_limit_bytes=mib << 20),
        cost_estimate=pl.CostEstimate(flops=flops, bytes_accessed=size, transcendentals=0),
    )


def first_kernel(
    place, res, tiles, mid_tiles, owner, inverse_rows, a_out, near_out, far_out, winv_out,
    res_out, flat, held, picked, inverse_part, sems, side_sems,
):
    blocks, ext = held.shape[0], held.shape[1]
    width = a_out.shape[1]
    parts = sems.shape[0] - 1
    per = blocks // parts

    def copy(part):
        rows = pl.ds(part * per, per)
        return pltpu.make_async_copy(tiles.at[rows, 0], held.at[rows], sems.at[part])

    whole = pltpu.make_async_copy(res, flat, sems.at[parts])
    mids = mid_tiles.shape[0]
    last = mids - 1
    column = place[2]
    odd = place[0] % 2
    choose = lambda *values: jnp.where(
        column < 2,
        jnp.where(column == 0, values[0], values[1]),
        jnp.where(column == 2, values[2], values[3]),
    )
    up = choose(last, last, last - 1, 0), choose(1, 2, 2, 0)
    down = choose(0, 0, 1, last), choose(1, 0, 0, 2)
    tiles_at = [
        [jnp.where(odd == side, one, two) for one, two in zip(up, down)] for side in range(2)
    ] + [(0, 1), (last, 1)]
    share = inverse_part.shape[0]
    begin = pl.multiple_of(column * share, share)
    smalls = [
        pltpu.make_async_copy(inverse_rows.at[pl.ds(begin, share)], inverse_part, side_sems.at[4])
    ] + [
        pltpu.make_async_copy(mid_tiles.at[b, k], picked.at[n], side_sems.at[n])
        for n, (b, k) in enumerate(tiles_at)
    ]
    whole.start()
    for part in range(parts):
        copy(part).start()
    for small in smalls:
        small.start()
    eye = eye_mask(ext)
    quarter = blocks // 4
    rows = pl.ds(pl.multiple_of(column * quarter, quarter), quarter)
    lo, hi = split(owner[rows] - place[0] * (mids * ext), ext)
    mid_block, mid_hi = split(owner[blocks:], ext)
    for small in smalls:
        small.wait()
    extra = far_out.shape[0] - blocks
    singles = [
        jnp.concatenate(
            [
                mid_hi[first : first + 2].astype(F32),
                mid_block[first : first + 2].astype(F32),
                diag_row(picked[2 + side], eye),
                jnp.zeros((width - 5, ext), F32),
            ],
            axis=0,
        )
        for side, first in enumerate((last - 1, 0))
    ]
    tile_blocks = ext // width
    for n, (to, single) in enumerate(
        (
            (near_out, jnp.where(odd == 0, singles[0], singles[1])),
            (far_out, jnp.where(odd == 0, singles[1], singles[0])),
        )
    ):
        for k in range(tile_blocks):
            to[blocks + k] = picked[n, k * width : (k + 1) * width]
        to[blocks + tile_blocks] = hi.astype(F32).astype(BF16)
        to[blocks + tile_blocks + 1] = lo.astype(F32).astype(BF16)
        to[blocks + tile_blocks + 2] = single.astype(BF16)
    tall, wide = share // width, inverse_part.shape[1] // ext
    for i in range(tall):
        for k in range(wide):
            near_out[blocks + extra + i * wide + k] = inverse_part[
                i * width : (i + 1) * width, k * ext : (k + 1) * ext
            ].astype(BF16)

    for part in range(parts):
        copy(part).wait()
        if part == 0:
            whole.wait()
        for g in range(part * per, (part + 1) * per):
            winv = DAMPING * (1.0 / diag_row(held[g], eye))
            winv_out[pl.ds(g, 1), :] = winv
            r = flat[:, g * ext : (g + 1) * ext]
            res_out[g] = r
            value = (winv * r).astype(BF16)
            a_out[g] = value
            near_out[g] = value
            far_out[g] = value


def plan_kernel(place, index, after, owner, hot_out, plan):
    del after
    blocks, ext = index.shape[1], owner.shape[1]
    first = place[0] * blocks
    zero = 3 * blocks

    def row(g, most):
        away, block = [], []
        for s in range(1, 4):
            at = index[s, g] - first
            own = jnp.logical_and(at >= 0, at < blocks)
            away.append(jnp.where(own, 0, 1))
            block.append(at + blocks)
        count = away[0] + away[1] + away[2]
        one = jnp.where(away[0] == 1, 0, jnp.where(away[1] == 1, 1, 2))
        two = jnp.where(away[0] + away[1] == 2, 1, 2)
        pick = lambda k: jnp.where(k == 0, block[0], jnp.where(k == 1, block[1], block[2]))
        plan[0, g] = one + 1
        plan[1, g] = jnp.where(count >= 1, pick(one), zero)
        plan[2, g] = two + 1
        plan[3, g] = jnp.where(count >= 2, pick(two), zero)
        plan[4, g] = 0
        return jnp.maximum(most, count)

    plan[4, 0] = lax.fori_loop(0, blocks, row, 0, unroll=8)
    _, hi = split(owner[0:blocks], ext)
    for g in range(blocks):
        hot_out[:, g * ext : (g + 1) * ext] = one_hot(hi[g : g + 1, :], ext)


def own_rows(index, place, own, window, slots):
    blocks = own.shape[0]
    window[0:blocks] = own[...]
    window[blocks] = jnp.zeros_like(window[blocks])
    first = place[0] * blocks

    def local(s, g):
        at = index[s, g] - first
        return jnp.where(jnp.logical_and(at >= 0, at < blocks), at, blocks)

    def row(g):
        picked = [window[g]] + [window[local(s, g)] for s in range(1, slots)]
        return jnp.concatenate(picked, axis=1)

    return row


def own_first_kernel(index, place, plan, tiles, own, out, turned_out, window):
    del plan
    blocks, slots = tiles.shape[:2]
    row = own_rows(index, place, own, window, slots)
    for g in range(blocks):
        turned = [tiles[g, s].T for s in range(slots)]
        for s in range(slots):
            turned_out[g, s] = turned[s]
        out[g] = dot_nn(row(g), jnp.concatenate(turned, axis=0))


def own_kernel(index, place, turned, own, out, window):
    blocks, slots = turned.shape[:2]
    row = own_rows(index, place, own, window, slots)
    for g in range(blocks):
        out[g] = dot_nn(row(g), jnp.concatenate([turned[g, s] for s in range(slots)], axis=0))


def for_rows(index, plan, offset, tiles, window, part, blocks, then):
    window[3 * blocks] = jnp.zeros_like(window[3 * blocks])

    @pl.when(plan[4, 0] <= 2)
    def _():
        for g in range(blocks):
            picked = [window[plan[1, g]], window[plan[3, g]]]
            matched = [tiles[g, plan[0, g]], tiles[g, plan[2, g]]]
            added = dot_nn(jnp.concatenate(picked, axis=1), jnp.concatenate(matched, axis=0))
            then(g, part[g] + added)

    @pl.when(plan[4, 0] > 2)
    def _():
        @pl.loop(0, blocks)
        def _(g):
            then(g, fine_row(index, offset, tiles, window, g))


def sides_kernel(
    place, a, b, c, d, rows_a, rows_b, rows_c, rows_d, mid_tiles, owner, left_out, right_out,
    inverse_out, scale_out, mid_hot, mid_block, buffer, rows_buffer,
):
    width, ext = a.shape[1:]
    tile_blocks = ext // width
    extra = tile_blocks + 3
    for n, piece in enumerate((a, b, c, d)):
        buffer[place[2] ^ n] = piece[...]
    for n, piece in enumerate((rows_a, rows_b, rows_c, rows_d)):
        rows_buffer[place[2] ^ n] = piece[...]
    share = inverse_out.shape[0] // 4
    wide = inverse_out.shape[1] // ext
    for out, first in ((left_out, 0), (right_out, extra)):
        for n in range(4):
            for k in range(tile_blocks):
                at = n * ext + k * width
                out[at : at + width] = buffer[n, first + k]
            out[HI_AT + n * width : HI_AT + (n + 1) * width] = buffer[n, first + tile_blocks]
            out[LO_AT + n * width : LO_AT + (n + 1) * width] = buffer[n, first + tile_blocks + 1]
        out[MISC_AT:MESSAGE] = buffer[0, first + tile_blocks + 2]
    for n in range(4):
        for i in range(share // width):
            rows = slice(n * share + i * width, n * share + (i + 1) * width)
            for k in range(wide):
                inverse_out[rows, k * ext : (k + 1) * ext] = rows_buffer[n, i * wide + k]
    mids = mid_tiles.shape[0]
    eye = eye_mask(ext)
    has_left, has_right = place[0] > 0, place[0] < place[1] - 1
    left_single, right_single = (m[MISC_AT:MESSAGE].astype(F32) for m in (left_out, right_out))
    scales = [DAMPING * (1.0 / diag_row(mid_tiles[b, 1], eye)) for b in range(mids)] + [
        inverse(diag_row(left_out[0:ext], eye), has_left),
        inverse(diag_row(right_out[0:ext], eye), has_right),
        inverse(left_single[4:5], has_left),
        inverse(right_single[4:5], has_right),
    ]
    scale_out[...] = jnp.concatenate(
        scales + [jnp.zeros((scale_out.shape[0] - len(scales), ext), F32)], axis=0
    )
    blocks = owner.shape[0] - mids
    own_block, own_hi = split(owner[blocks:], ext)
    block = [left_single[2:4].astype(jnp.int32), own_block, right_single[2:4].astype(jnp.int32)]
    hi = [left_single[0:2].astype(jnp.int32), own_hi, right_single[0:2].astype(jnp.int32)]
    hi = jnp.concatenate(hi, axis=0)
    start = place[0] - 2 + place[0] % 2
    mid_block[0 : mids + 4] = jnp.concatenate(block, axis=0) - start
    for b in range(mids + 4):
        mid_hot[:, b * ext : (b + 1) * ext] = one_hot(hi[b : b + 1], ext)


def side_hot_kernel(after, from_left, from_right, hot_left, hot_right):
    del after
    ext = hot_left.shape[0]
    blocks = hot_left.shape[1] // ext
    for message, hot in ((from_left, hot_left), (from_right, hot_right)):
        hi = as_int(message[HI_AT : HI_AT + blocks, :])
        for g in range(blocks):
            hot[:, g * ext : (g + 1) * ext] = one_hot(hi[g : g + 1, :], ext)


def fill_window(window, near, own, far, me):
    blocks = own.shape[0]
    window[pl.ds((1 - me % 2) * (2 * blocks), blocks)] = near[0:blocks]
    window[blocks : 2 * blocks] = own[...]
    window[pl.ds((me % 2) * (2 * blocks), blocks)] = far[0:blocks]


def fine_row(index, offset, tiles, window, g):
    slots = tiles.shape[1]
    picked = [window[index[s, g] - offset] for s in range(slots)]
    return dot_nn(
        jnp.concatenate(picked, axis=1),
        jnp.concatenate([tiles[g, s] for s in range(slots)], axis=0),
    )


def second_kernel(
    index, plan, place, tiles, near, own, far, part, res, winv, hot, basis_b, basis_c, basis_d, b_out,
    b16_out, b16_too, mine_out, rows_out, window,
):
    del hot, basis_b, basis_c, basis_d
    blocks, ext = own.shape[0], own.shape[2]
    offset = (place[0] - 1) * blocks
    fill_window(window, near, own, far, place[0])

    def finish_row(g, product):
        w = winv[pl.ds(g, 1), :]
        r = res[g]
        b = w * r + w * (r - product)
        b_out[g] = b
        b16_out[g] = b.astype(BF16)
        b16_too[g] = b.astype(BF16)

    for_rows(index, plan, offset, tiles, window, part, blocks, finish_row)
    for n in range(blocks, b16_too.shape[0]):
        b16_too[n] = jnp.zeros_like(b16_too[n])
    odd = place[0] % 2
    extra = far.shape[0] - blocks
    mine_out[pl.ds((1 - odd) * extra, extra)] = near[blocks : blocks + extra]
    mine_out[pl.ds(odd * extra, extra)] = far[blocks:]
    rows_out[...] = near[blocks + extra :]


def split(row, ext):
    return lax.shift_right_logical(row, ext.bit_length() - 1), row & (ext - 1)


def one_hot(row, n):
    ids = lax.broadcasted_iota(jnp.int32, (n, row.shape[1]), 0)
    return jnp.where(ids == row, 1.0, 0.0).astype(BF16)


def spread(value, row, n):
    return jnp.concatenate(
        [jnp.where(row == l, value, 0.0).astype(BF16) for l in range(n)], axis=0
    )


def edge(message, row, n=128):
    return message[row : row + n, :]


def as_int(row):
    return row.astype(F32).astype(jnp.int32)


def inverse(row, present):
    return DAMPING * (1.0 / jnp.where(present, row, 1.0))


def mid_product(mid_tiles, v, b):
    ext = mid_tiles.shape[2]
    count = mid_tiles.shape[0]
    ks = [k for k in range(3) if v.get(b - 1 + k) is not None]
    return dot_nt(
        jnp.concatenate([v[b - 1 + k] for k in ks], axis=1),
        jnp.concatenate([mid_tiles[b, k] for k in ks], axis=1),
    )


def third_kernel(
    index, plan, place, tiles, near, own, far, part, res, owner, hot, mid_tiles, from_left,
    from_right, scale, mid_hot, mid_block, fres_out, u_out, bpart_out, send, window, spread_rows,
):
    blocks, ext = own.shape[0], own.shape[2]
    width = own.shape[1]
    mids = mid_tiles.shape[0]
    me = place[0]
    offset = (me - 1) * blocks
    fill_window(window, near, own, far, place[0])

    def finish_row(g, product):
        r = res[g] - product
        fres_out[g] = r
        lo, _ = split(owner[pl.ds(g, 1), :] - me * (mids * ext), ext)
        at = g * ext if isinstance(g, int) else pl.multiple_of(g * ext, ext)
        spread_rows[:, pl.ds(at, ext)] = spread(r, lo, mids)

    for_rows(index, plan, offset, tiles, window, part, blocks, finish_row)
    quarters = [slice(n * blocks // 4 * ext, (n + 1) * blocks // 4 * ext) for n in range(4)]
    total = sum(dot_nt(spread_rows[:, q], hot[:, q]) for q in quarters)
    u = [total[b * width : (b + 1) * width] for b in range(mids)]
    winv = [scale[b : b + 1, :] for b in range(mids)]
    winv_left, winv_right = scale[mids : mids + 1, :], scale[mids + 1 : mids + 2, :]
    left_mid, left_next, left_far = (edge(from_left, 128 * k) for k in range(3))
    right_mid, right_prev, right_far = (edge(from_right, 128 * k) for k in range(3))
    a = [winv[b] * u[b] for b in range(mids)]
    a16 = {b: a[b].astype(BF16) for b in range(mids)}
    mine = {}
    for b in range(mids):
        mine[b] = a[b] + winv[b] * (u[b] - mid_product(mid_tiles, a16, b))
        u_out[b] = u[b]
        bpart_out[b] = mine[b]
    mine[-1] = -winv_left * dot_nt(a16[0], left_next)
    mine[mids] = -winv_right * dot_nt(a16[mids - 1], right_prev)
    p16 = {b: v.astype(BF16) for b, v in mine.items()}
    rest = {b: u[b] - mid_product(mid_tiles, p16, b) for b in range(mids)}
    rest[-1] = -(dot_nt(p16[-1], left_mid) + dot_nt(p16[0], left_next))
    rest[-2] = -dot_nt(p16[-1], left_far)
    rest[mids] = -(dot_nt(p16[mids], right_mid) + dot_nt(p16[mids - 1], right_prev))
    rest[mids + 1] = -dot_nt(p16[mids], right_far)
    spreads = [
        spread(rest[b], mid_block[b + 2 : b + 3, :], 4) for b in range(-2, mids + 2)
    ]
    coarse = dot_nt(jnp.concatenate(spreads, axis=1), mid_hot[...])
    coarse16 = coarse.astype(BF16)
    first, last = u[0].astype(BF16), u[mids - 1].astype(BF16)
    none = jnp.zeros_like(first)
    for d in range(send.shape[0]):
        for k in range(4):
            send[d, k] = coarse16[k * width : (k + 1) * width]
        send[d, 4] = jnp.where(me + 1 == d, last, jnp.where(me - 1 == d, first, none))


def mid_kernel(
    place, got, inverse_rows, partner_rows, mid_tiles, scale, mid_hot, mid_block, u, bpart,
    dpart_out, edges_out, near_out, far_out, next_out, beyond_out,
):
    ext = mid_tiles.shape[2]
    mids = mid_tiles.shape[0]
    peers = got.shape[0]
    width = got.shape[2]
    me = place[0]
    odd = me % 2
    rhs = []
    for k in range(peers):
        terms = [
            got[s, k - (s - 2 + s % 2)].astype(F32)
            for s in range(peers)
            if 0 <= k - (s - 2 + s % 2) < 4
        ]
        rhs.append(sum(terms[1:], terms[0]))
    rhs16 = jnp.concatenate([r.astype(BF16) for r in rhs], axis=1)
    mine = dot_nt(rhs16, inverse_rows[...].astype(BF16))
    other = dot_nt(rhs16, partner_rows[...])
    pair = jnp.concatenate(
        [jnp.where(odd == 0, mine, other), jnp.where(odd == 0, other, mine)], axis=0
    ).astype(BF16)
    winv = [scale[b : b + 1, :] for b in range(mids)]
    winv_left, winv_right = scale[mids : mids + 1, :], scale[mids + 1 : mids + 2, :]
    before = got[lax.rem(me + peers - 1, peers), 4].astype(F32)
    after = got[lax.rem(me + 1, peers), 4].astype(F32)
    a_before = (winv_left * before).astype(BF16)
    a_after = (winv_right * after).astype(BF16)
    c, c16 = {}, {}
    for b in range(mids):
        value = bpart[b]
        if b == 0:
            value = value - winv[b] * dot_nt(a_before, mid_tiles[b, 0])
        if b == mids - 1:
            value = value - winv[b] * dot_nt(a_after, mid_tiles[b, 2])
        hot = mid_hot[:, (b + 2) * ext : (b + 3) * ext]
        both = jnp.dot(pair, hot, preferred_element_type=F32)
        second = mid_block[b + 2 : b + 3, :] == 3 - 2 * odd
        c[b] = value + jnp.where(second, both[width:], both[:width])
        c16[b] = c[b].astype(BF16)
    d16 = []
    for b in range(mids):
        d = c[b] + winv[b] * (u[b] - mid_product(mid_tiles, c16, b))
        dpart_out[b] = d
        d16.append(d.astype(BF16))
    edges_out[0] = c16[0]
    edges_out[1] = c16[mids - 1]
    for b in range(mids):
        near_out[b] = d16[b]
        far_out[b] = d16[b]
    first, last = c16[0], c16[mids - 1]
    low = me % 4 < 2
    near_out[mids] = jnp.where(odd == 0, last, first)
    far_out[mids] = jnp.where(odd == 0, first, last)
    next_out[...] = jnp.where(low, last, first)
    beyond_out[...] = jnp.where(low, first, last)


def prolong(values, hot, lo, width, mids):
    both = jnp.dot(values, hot, preferred_element_type=F32)
    result = jnp.where(lo == 0, both[:width], 0.0)
    for l in range(1, mids):
        result = jnp.where(lo == l, both[l * width : (l + 1) * width], result)
    return result


def last_kernel(
    index, place, tiles, near, far, other, nexts, beyond, dpart, c_edges, mid_tiles, scale, owner, hot_own, from_left, hot_left,
    from_right, hot_right, b_in, fres, winv, basis_a, basis_b, basis_c, basis_d, out, gram_out, window,
    added, rounded, grams, result, sems,
):
    blocks, width, ext = b_in.shape
    mids = mid_tiles.shape[0]
    me, peers = place[0], place[1]
    odd = me % 2
    low = me % 4 < 2
    middle = jnp.logical_or(me % 4 == 1, me % 4 == 2)
    present = jnp.logical_and(me > 0, me < peers - 1)
    none = jnp.zeros_like(nexts[...])
    away = [
        jnp.where(middle, other[b], jnp.where(present, far[b], none)) for b in range(mids + 1)
    ]
    left = [jnp.where(odd == 1, near[b], away[b]) for b in range(mids + 1)]
    right = [jnp.where(odd == 1, away[b], near[b]) for b in range(mids + 1)]
    outer = jnp.where(jnp.logical_and(me > 1, me < peers - 2), beyond[...], none)
    far_left = jnp.where(low, outer, nexts[...])
    far_right = jnp.where(low, nexts[...], outer)
    row = lambda n: scale[n : n + 1, :]
    own = [dpart[b] for b in range(mids)]
    own[0] = own[0] - row(0) * dot_nt(left[mids], mid_tiles[0, 0])
    own[-1] = own[-1] - row(mids - 1) * dot_nt(right[mids], mid_tiles[mids - 1, 2])
    lefts = [v.astype(F32) for v in left[:mids]]
    lefts[0] = lefts[0] - row(mids + 2) * dot_nt(far_left, edge(from_left, 384))
    lefts[-1] = lefts[-1] - row(mids) * dot_nt(c_edges[0], edge(from_left, 128))
    rights = [v.astype(F32) for v in right[:mids]]
    rights[0] = rights[0] - row(mids + 1) * dot_nt(c_edges[1], edge(from_right, 128))
    rights[-1] = rights[-1] - row(mids + 3) * dot_nt(far_right, edge(from_right, 384))
    own16, left16, right16 = (
        jnp.concatenate([v.astype(BF16) for v in side], axis=0) for side in (own, lefts, rights)
    )
    own_lo, _ = split(owner[0:blocks] - me * (mids * ext), ext)
    left_lo, right_lo = (
        as_int(message[LO_AT : LO_AT + blocks, :]) for message in (from_left, from_right)
    )
    for g in range(0, blocks, 2):
        cols = slice(g * ext, (g + 2) * ext)
        for lo, hot, values, base in (
            (own_lo, hot_own, own16, blocks),
            (left_lo, hot_left, left16, 0),
            (right_lo, hot_right, right16, 2 * blocks),
        ):
            row = jnp.concatenate([lo[g : g + 1], lo[g + 1 : g + 2]], axis=1)
            value = prolong(values, hot[:, cols], row, width, mids)
            for n in range(2):
                half = value[:, n * ext : (n + 1) * ext]
                if base == blocks:
                    added[g + n] = half
                window[base + g + n] = half.astype(BF16)
    offset = (me - 1) * blocks
    count = sems.shape[0]
    per = blocks // count

    def copy(part):
        cols = pl.ds(part * per * ext, per * ext)
        return pltpu.make_async_copy(result.at[:, cols], out.at[:, cols], sems.at[part])

    for g in range(blocks):
        product = fine_row(index, offset, tiles, window, g)
        value = b_in[g] + added[g] + winv[pl.ds(g, 1), :] * (fres[g] - product)
        cols = slice(g * ext, (g + 1) * ext)
        result[:, cols] = value
        rounded[:, cols] = value.astype(BF16)
        if (g + 1) % per == 0:
            copy((g + 1) // per - 1).start()
    for n, piece in enumerate((basis_a, basis_b, basis_c, basis_d)):
        grams[place[2] ^ n] = dot_nt(rounded[...], piece[...])
    gram = jnp.concatenate([grams[n] for n in range(4)], axis=1)
    gram = jnp.concatenate([gram[: width // 2], gram[width // 2 :]], axis=1)
    for d in range(gram_out.shape[0]):
        gram_out[d] = gram
    for part in range(count):
        copy(part).wait()


def sum_kernel(got, out):
    total = got[0]
    for s in range(1, got.shape[0]):
        total = total + got[s]
    half, wide = out.shape[0] // 2, out.shape[1]
    out[0:half] = total[:, :wide]
    out[half:] = total[:, wide:]


def halo(for_partner, for_other):
    peers = lax.axis_size("rows")
    odd = [(i, i + 1) for i in range(1, peers - 1, 2)]
    even = [(i, i + 1) for i in range(0, peers - 1, 2)]
    swap = lambda pairs: pairs + [(j, i) for i, j in pairs]
    near = lax.ppermute(for_partner, "rows", swap(even))
    far = lax.ppermute(for_other, "rows", swap(odd))
    return near, far


def relay_kernel(one, two, after, one_out, two_out):
    del after
    one_out[...] = one[...]
    two_out[...] = two[...]


def from_columns(values, relay=lambda *v: v):
    peers = lax.axis_size("cols")
    swap = lambda v, n: lax.ppermute(v, "cols", [(i, i ^ n) for i in range(peers)])
    across = [swap(v, 2) for v in values]
    sent_on = relay(*across)
    return [[swap(v, 1), a, swap(r, 1)] for v, a, r in zip(values, across, sent_on)]


def on_device(
    residual_block, basis, fine_tiles, fine_index, mid_tiles, fine_owner, mid_owner, coarse_inverse
):
    peers = lax.axis_size("rows")
    me = lax.axis_index("rows")
    blocks, slots, ext, _ = fine_tiles.shape
    mids = mid_tiles.shape[0]
    count = blocks * ext
    width = residual_block.shape[1]
    res = residual_block.T
    index = fine_index.T
    place = jnp.stack([me, jnp.int32(peers), lax.axis_index("cols")])
    owner = jnp.concatenate([fine_owner, mid_owner]).reshape(blocks + mids, ext)
    shape = jax.ShapeDtypeStruct
    tile_bytes = fine_tiles.size * 2
    fine_flops = 2 * fine_tiles.size * width
    extra = ext // width + 3

    columns = lax.axis_size("cols")
    share = coarse_inverse.shape[0] // columns
    whole_row = coarse_inverse.shape[1]
    quarter = (share // width) * (whole_row // ext)

    a16, for_partner, for_other, winv, res_blocks = pl.pallas_call(
        first_kernel,
        in_specs=[SM] + [HBM] * 3 + [VM, HBM],
        out_specs=[VM] * 5,
        out_shape=[
            shape((blocks, width, ext), BF16),
            shape((blocks + extra + quarter, width, ext), BF16),
            shape((blocks + extra, width, ext), BF16),
            shape((blocks, ext), F32),
            shape((blocks, width, ext), F32),
        ],
        scratch_shapes=[
            pltpu.VMEM((width, count), F32),
            pltpu.VMEM((blocks, ext, ext), BF16),
            pltpu.VMEM((4, ext, ext), BF16),
            pltpu.VMEM((share, whole_row), F32),
            pltpu.SemaphoreType.DMA((5,)),
            pltpu.SemaphoreType.DMA((5,)),
        ],
        name="first_smoothing",
        **params(FIRST_LIMIT, count * ext, tile_bytes // 4),
    )(place, res, fine_tiles, mid_tiles, owner, coarse_inverse)

    near, far = halo(for_partner, for_other)
    hot_own, plan = pl.pallas_call(
        plan_kernel,
        in_specs=[SM, SM, ANY, VM],
        out_specs=[VM, SM],
        out_shape=[shape((ext, count), BF16), shape((5, blocks), jnp.int32)],
        name="one_hot_rows",
        **params(4, count * ext, 4 * tile_bytes),
    )(place, index, winv, owner)

    part_shape = shape((blocks, width, ext), F32)
    part, tiles = pl.pallas_call(
        own_first_kernel,
        in_specs=[SM, SM, SM, VM, VM],
        out_specs=[VM, VM],
        out_shape=[part_shape, shape(fine_tiles.shape, BF16)],
        scratch_shapes=[pltpu.VMEM((blocks + 1, width, ext), BF16)],
        name="own_part_and_turned_tiles",
        **params(4, ext, ext),
    )(index, place, plan, fine_tiles, a16)
    basis_pieces = [basis.T] + from_columns([basis.T])[0]

    b32, b16, b16_too, mine, mine_rows = pl.pallas_call(
        second_kernel,
        in_specs=[SM] * 3 + [VM] * 7 + [ANY] * 4,
        out_specs=[VM] * 5,
        out_shape=[
            shape((blocks, width, ext), F32),
            shape((blocks, width, ext), BF16),
            shape((blocks + 1, width, ext), BF16),
            shape((2 * extra, width, ext), BF16),
            shape((quarter, width, ext), BF16),
        ],
        scratch_shapes=[pltpu.VMEM((3 * blocks + 1, width, ext), BF16)],
        name="second_smoothing",
        **params(6, fine_flops, tile_bytes),
    )(
        index, plan, place, tiles, near, a16, far, part, res_blocks, winv, hot_own,
        *basis_pieces[1:],
    )

    near, far = halo(b16_too, b16)
    part = pl.pallas_call(
        own_kernel,
        in_specs=[SM, SM, VM, VM],
        out_specs=VM,
        out_shape=part_shape,
        scratch_shapes=[pltpu.VMEM((blocks + 1, width, ext), BF16)],
        name="own_part_of_residual",
        **params(4, ext, ext),
    )(index, place, tiles, b16)
    def relay(one, two):
        return pl.pallas_call(
            relay_kernel,
            in_specs=[VM, VM, ANY],
            out_specs=[VM, VM],
            out_shape=[shape(one.shape, BF16), shape(two.shape, BF16)],
            name="relay",
            **params(4, ext, ext),
        )(one, two, part)

    mine_pieces, rows_pieces = from_columns([mine, mine_rows], relay)
    from_left, from_right, partner_rows, scale, mid_hot, mid_block = pl.pallas_call(
        sides_kernel,
        in_specs=[SM] + [VM] * 10,
        out_specs=[VM] * 6,
        out_shape=[
            shape((MESSAGE, ext), BF16),
            shape((MESSAGE, ext), BF16),
            shape(coarse_inverse.shape, BF16),
            shape((16, ext), F32),
            shape((ext, (mids + 4) * ext), BF16),
            shape((16, ext), jnp.int32),
        ],
        scratch_shapes=[
            pltpu.VMEM((4, 2 * extra, width, ext), BF16),
            pltpu.VMEM((4, quarter, width, ext), BF16),
        ],
        name="side_messages",
        **params(4, ext, ext),
    )(
        place, mine, *mine_pieces, mine_rows, *rows_pieces, mid_tiles, owner,
    )

    fres, u, bpart, send = pl.pallas_call(
        third_kernel,
        in_specs=[SM] * 3 + [VM] * 14,
        out_specs=[VM] * 4,
        out_shape=[
            shape((blocks, width, ext), F32),
            shape((mids, width, ext), F32),
            shape((mids, width, ext), F32),
            shape((peers, 5, width, ext), BF16),
        ],
        scratch_shapes=[
            pltpu.VMEM((3 * blocks + 1, width, ext), BF16),
            pltpu.VMEM((mids * width, count), BF16),
        ],
        name="residual_and_restriction",
        **params(10, fine_flops, tile_bytes),
    )(
        index, plan, place, tiles, near, b16, far, part, res_blocks, owner, hot_own, mid_tiles,
        from_left, from_right, scale, mid_hot, mid_block,
    )

    got = lax.all_to_all(send, "rows", 0, 0)
    dpart, c_edges, *sends = pl.pallas_call(
        mid_kernel,
        in_specs=[SM] + [VM] * 9,
        out_specs=[VM] * 6,
        out_shape=[
            shape((mids, width, ext), F32),
            shape((2, width, ext), BF16),
            shape((mids + 1, width, ext), BF16),
            shape((mids + 1, width, ext), BF16),
            shape((width, ext), BF16),
            shape((width, ext), BF16),
        ],
        name="coarse_and_mid_level",
        **params(MID_LIMIT, 4 * width * coarse_inverse.size, coarse_inverse.size * 4),
    )(
        place, got, coarse_inverse, partner_rows, mid_tiles, scale, mid_hot, mid_block, u, bpart,
    )

    return finish(
        place, index, tiles, sends, dpart, c_edges, mid_tiles, scale, owner, hot_own, from_left, from_right,
        b32, fres, winv, basis_pieces,
    )


def finish(
    place, index, tiles, sends, dpart, c_edges, mid_tiles, scale, owner, hot_own, from_left, from_right, b32,
    fres, winv, basis_pieces,
):
    peers = lax.axis_size("rows")
    blocks, width, ext = b32.shape
    mids = mid_tiles.shape[0]
    count = blocks * ext
    shape = jax.ShapeDtypeStruct
    swap = lambda v, pairs: lax.ppermute(v, "rows", pairs + [(j, i) for i, j in pairs])
    flip = lambda v, n: lax.ppermute(v, "rows", [(i, i ^ n) for i in range(peers)])
    ends = [(0, 1), (peers - 2, peers - 1)] if peers > 4 else [(0, 1), (2, 3)]
    inner = range(2, peers - 4, 4)
    far = swap(sends[1], [(i + 1, i + 2) for i in inner] + [(i, i + 3) for i in inner] + ends)
    beyond = swap(sends[3], [(i + n, i + 2 + n) for i in inner for n in range(2)] + ends)
    near = flip(sends[0], 1)
    other = flip(sends[1], 3)
    nexts = flip(sends[2], 2)
    hot_left, hot_right = pl.pallas_call(
        side_hot_kernel,
        in_specs=[ANY, VM, VM],
        out_specs=[VM] * 2,
        out_shape=[shape((ext, count), BF16)] * 2,
        name="side_one_hot_rows",
        **params(4, ext, ext),
    )(c_edges, from_left, from_right)
    out, grams = pl.pallas_call(
        last_kernel,
        in_specs=[SM, SM] + [VM] * 23,
        out_specs=[HBM, VM],
        out_shape=[
            shape((width, count), F32),
            shape((peers, width // 2, 8 * width), F32),
        ],
        scratch_shapes=[
            pltpu.VMEM((3 * blocks, width, ext), BF16),
            pltpu.VMEM((blocks, width, ext), F32),
            pltpu.VMEM((width, count), BF16),
            pltpu.VMEM((4, width, width), F32),
            pltpu.VMEM((width, count), F32),
            pltpu.SemaphoreType.DMA((2,)),
        ],
        name="prolongation_and_last_smoothing",
        **params(8, 2 * tiles.size * width, tiles.size * 2),
    )(
        index, place, tiles, near, far, other, nexts, beyond, dpart, c_edges, mid_tiles, scale, owner, hot_own, from_left, hot_left,
        from_right, hot_right, b32, fres, winv, *basis_pieces,
    )
    gram = pl.pallas_call(
        sum_kernel,
        in_specs=[VM],
        out_specs=VM,
        out_shape=shape((width, 4 * width), F32),
        name="gram_sum",
        **params(4, 0, 0),
    )(lax.all_to_all(grams, "rows", 0, 0))
    return out.T, gram.T


def solution(mesh):
    in_specs = (
        P("rows", "cols"),
        P("rows", "cols"),
        P("rows", None, None, None),
        P("rows", None),
        P("rows", None, None, None),
        P("rows"),
        P("rows"),
        P("rows", None),
    )
    out_specs = (P("rows", "cols"), P(None, "cols"))
    return jax.shard_map(
        on_device, mesh=mesh, in_specs=in_specs, out_specs=out_specs, check_vma=False
    )
```

```python
import jax
import jax.numpy as jnp
from jax import lax
from jax.experimental import pallas as pl
from jax.experimental.pallas import tpu as pltpu
from jax.sharding import PartitionSpec as P

DAMPING = 0.6666666666666666
F32 = jnp.float32
BF16 = jnp.bfloat16
NT = (((1,), (1,)), ((), ()))
VM = pl.BlockSpec(memory_space=pltpu.VMEM)
SM = pl.BlockSpec(memory_space=pltpu.SMEM)
ANY = pl.BlockSpec(memory_space=pl.ANY)
HBM = pl.BlockSpec(memory_space=pltpu.HBM)

HI_AT, LO_AT, MISC_AT = 512, 576, 640
MESSAGE = 656
FIRST_LIMIT = 52
MID_LIMIT = 8


def dot_nn(a, b):
    return jnp.dot(a, b, preferred_element_type=F32)


def dot_nt(a, b):
    return lax.dot_general(a, b, NT, preferred_element_type=F32)


def eye_mask(n):
    return lax.broadcasted_iota(jnp.int32, (n, n), 0) == lax.broadcasted_iota(jnp.int32, (n, n), 1)


def diag_row(tile, eye):
    return jnp.sum(jnp.where(eye, tile.astype(F32), 0.0), axis=0, keepdims=True)


def params(mib, flops, size):
    return dict(
        compiler_params=pltpu.CompilerParams(vmem_limit_bytes=mib << 20),
        cost_estimate=pl.CostEstimate(flops=flops, bytes_accessed=size, transcendentals=0),
    )


def first_kernel(
    place, res, tiles, mid_tiles, owner, inverse_rows, a_out, near_out, far_out, winv_out,
    res_out, flat, held, picked, inverse_part, sems, side_sems,
):
    blocks, ext = held.shape[0], held.shape[1]
    width = a_out.shape[1]
    parts = sems.shape[0] - 1
    per = blocks // parts

    def copy(part):
        rows = pl.ds(part * per, per)
        return pltpu.make_async_copy(tiles.at[rows, 0], held.at[rows], sems.at[part])

    whole = pltpu.make_async_copy(res, flat, sems.at[parts])
    mids = mid_tiles.shape[0]
    last = mids - 1
    column = place[2]
    odd = place[0] % 2
    choose = lambda *values: jnp.where(
        column < 2,
        jnp.where(column == 0, values[0], values[1]),
        jnp.where(column == 2, values[2], values[3]),
    )
    up = choose(last, last, last - 1, 0), choose(1, 2, 2, 0)
    down = choose(0, 0, 1, last), choose(1, 0, 0, 2)
    tiles_at = [
        [jnp.where(odd == side, one, two) for one, two in zip(up, down)] for side in range(2)
    ] + [(0, 1), (last, 1)]
    share = inverse_part.shape[0]
    begin = pl.multiple_of(column * share, share)
    smalls = [
        pltpu.make_async_copy(inverse_rows.at[pl.ds(begin, share)], inverse_part, side_sems.at[4])
    ] + [
        pltpu.make_async_copy(mid_tiles.at[b, k], picked.at[n], side_sems.at[n])
        for n, (b, k) in enumerate(tiles_at)
    ]
    whole.start()
    for part in range(parts):
        copy(part).start()
    for small in smalls:
        small.start()
    eye = eye_mask(ext)
    quarter = blocks // 4
    rows = pl.ds(pl.multiple_of(column * quarter, quarter), quarter)
    lo, hi = split(owner[rows] - place[0] * (mids * ext), ext)
    mid_block, mid_hi = split(owner[blocks:], ext)
    for small in smalls:
        small.wait()
    extra = far_out.shape[0] - blocks
    singles = [
        jnp.concatenate(
            [
                mid_hi[first : first + 2].astype(F32),
                mid_block[first : first + 2].astype(F32),
                diag_row(picked[2 + side], eye),
                jnp.zeros((width - 5, ext), F32),
            ],
            axis=0,
        )
        for side, first in enumerate((last - 1, 0))
    ]
    tile_blocks = ext // width
    for n, (to, single) in enumerate(
        (
            (near_out, jnp.where(odd == 0, singles[0], singles[1])),
            (far_out, jnp.where(odd == 0, singles[1], singles[0])),
        )
    ):
        for k in range(tile_blocks):
            to[blocks + k] = picked[n, k * width : (k + 1) * width]
        to[blocks + tile_blocks] = hi.astype(F32).astype(BF16)
        to[blocks + tile_blocks + 1] = lo.astype(F32).astype(BF16)
        to[blocks + tile_blocks + 2] = single.astype(BF16)
    tall, wide = share // width, inverse_part.shape[1] // ext
    for i in range(tall):
        for k in range(wide):
            near_out[blocks + extra + i * wide + k] = inverse_part[
                i * width : (i + 1) * width, k * ext : (k + 1) * ext
            ].astype(BF16)

    for part in range(parts):
        copy(part).wait()
        if part == 0:
            whole.wait()
        for g in range(part * per, (part + 1) * per):
            winv = DAMPING * (1.0 / diag_row(held[g], eye))
            winv_out[pl.ds(g, 1), :] = winv
            r = flat[:, g * ext : (g + 1) * ext]
            res_out[g] = r
            value = (winv * r).astype(BF16)
            a_out[g] = value
            near_out[g] = value
            far_out[g] = value


def plan_kernel(place, index, after, owner, hot_out, plan):
    del after
    blocks, ext = index.shape[1], owner.shape[1]
    first = place[0] * blocks
    zero = 3 * blocks

    def row(g, most):
        away, block = [], []
        for s in range(1, 4):
            at = index[s, g] - first
            own = jnp.logical_and(at >= 0, at < blocks)
            away.append(jnp.where(own, 0, 1))
            block.append(at + blocks)
        count = away[0] + away[1] + away[2]
        one = jnp.where(away[0] == 1, 0, jnp.where(away[1] == 1, 1, 2))
        two = jnp.where(away[0] + away[1] == 2, 1, 2)
        pick = lambda k: jnp.where(k == 0, block[0], jnp.where(k == 1, block[1], block[2]))
        plan[0, g] = one + 1
        plan[1, g] = jnp.where(count >= 1, pick(one), zero)
        plan[2, g] = two + 1
        plan[3, g] = jnp.where(count >= 2, pick(two), zero)
        plan[4, g] = 0
        return jnp.maximum(most, count)

    plan[4, 0] = lax.fori_loop(0, blocks, row, 0, unroll=8)
    _, hi = split(owner[0:blocks], ext)
    for g in range(blocks):
        hot_out[:, g * ext : (g + 1) * ext] = one_hot(hi[g : g + 1, :], ext)


def own_rows(index, place, own, window, slots):
    blocks = own.shape[0]
    window[0:blocks] = own[...]
    window[blocks] = jnp.zeros_like(window[blocks])
    first = place[0] * blocks

    def local(s, g):
        at = index[s, g] - first
        return jnp.where(jnp.logical_and(at >= 0, at < blocks), at, blocks)

    def row(g):
        picked = [window[g]] + [window[local(s, g)] for s in range(1, slots)]
        return jnp.concatenate(picked, axis=1)

    return row


def own_first_kernel(index, place, plan, tiles, own, out, turned_out, window):
    del plan
    blocks, slots = tiles.shape[:2]
    row = own_rows(index, place, own, window, slots)
    for g in range(blocks):
        turned = [tiles[g, s].T for s in range(slots)]
        for s in range(slots):
            turned_out[g, s] = turned[s]
        out[g] = dot_nn(row(g), jnp.concatenate(turned, axis=0))


def own_kernel(index, place, turned, own, out, window):
    blocks, slots = turned.shape[:2]
    row = own_rows(index, place, own, window, slots)
    for g in range(blocks):
        out[g] = dot_nn(row(g), jnp.concatenate([turned[g, s] for s in range(slots)], axis=0))


def for_rows(index, plan, offset, tiles, window, part, blocks, then):
    window[3 * blocks] = jnp.zeros_like(window[3 * blocks])

    @pl.when(plan[4, 0] <= 2)
    def _():
        for g in range(blocks):
            picked = [window[plan[1, g]], window[plan[3, g]]]
            matched = [tiles[g, plan[0, g]], tiles[g, plan[2, g]]]
            added = dot_nn(jnp.concatenate(picked, axis=1), jnp.concatenate(matched, axis=0))
            then(g, part[g] + added)

    @pl.when(plan[4, 0] > 2)
    def _():
        @pl.loop(0, blocks)
        def _(g):
            then(g, fine_row(index, offset, tiles, window, g))


def sides_kernel(
    place, a, b, c, d, rows_a, rows_b, rows_c, rows_d, mid_tiles, owner, left_out, right_out,
    inverse_out, scale_out, mid_hot, mid_block, buffer, rows_buffer,
):
    width, ext = a.shape[1:]
    tile_blocks = ext // width
    extra = tile_blocks + 3
    for n, piece in enumerate((a, b, c, d)):
        buffer[place[2] ^ n] = piece[...]
    for n, piece in enumerate((rows_a, rows_b, rows_c, rows_d)):
        rows_buffer[place[2] ^ n] = piece[...]
    share = inverse_out.shape[0] // 4
    wide = inverse_out.shape[1] // ext
    for out, first in ((left_out, 0), (right_out, extra)):
        for n in range(4):
            for k in range(tile_blocks):
                at = n * ext + k * width
                out[at : at + width] = buffer[n, first + k]
            out[HI_AT + n * width : HI_AT + (n + 1) * width] = buffer[n, first + tile_blocks]
            out[LO_AT + n * width : LO_AT + (n + 1) * width] = buffer[n, first + tile_blocks + 1]
        out[MISC_AT:MESSAGE] = buffer[0, first + tile_blocks + 2]
    for n in range(4):
        for i in range(share // width):
            rows = slice(n * share + i * width, n * share + (i + 1) * width)
            for k in range(wide):
                inverse_out[rows, k * ext : (k + 1) * ext] = rows_buffer[n, i * wide + k]
    mids = mid_tiles.shape[0]
    eye = eye_mask(ext)
    has_left, has_right = place[0] > 0, place[0] < place[1] - 1
    left_single, right_single = (m[MISC_AT:MESSAGE].astype(F32) for m in (left_out, right_out))
    scales = [DAMPING * (1.0 / diag_row(mid_tiles[b, 1], eye)) for b in range(mids)] + [
        inverse(diag_row(left_out[0:ext], eye), has_left),
        inverse(diag_row(right_out[0:ext], eye), has_right),
        inverse(left_single[4:5], has_left),
        inverse(right_single[4:5], has_right),
    ]
    scale_out[...] = jnp.concatenate(
        scales + [jnp.zeros((scale_out.shape[0] - len(scales), ext), F32)], axis=0
    )
    blocks = owner.shape[0] - mids
    own_block, own_hi = split(owner[blocks:], ext)
    block = [left_single[2:4].astype(jnp.int32), own_block, right_single[2:4].astype(jnp.int32)]
    hi = [left_single[0:2].astype(jnp.int32), own_hi, right_single[0:2].astype(jnp.int32)]
    hi = jnp.concatenate(hi, axis=0)
    start = place[0] - 2 + place[0] % 2
    mid_block[0 : mids + 4] = jnp.concatenate(block, axis=0) - start
    for b in range(mids + 4):
        mid_hot[:, b * ext : (b + 1) * ext] = one_hot(hi[b : b + 1], ext)


def side_hot_kernel(after, from_left, from_right, hot_left, hot_right):
    del after
    ext = hot_left.shape[0]
    blocks = hot_left.shape[1] // ext
    for message, hot in ((from_left, hot_left), (from_right, hot_right)):
        hi = as_int(message[HI_AT : HI_AT + blocks, :])
        for g in range(blocks):
            hot[:, g * ext : (g + 1) * ext] = one_hot(hi[g : g + 1, :], ext)


def fill_window(window, near, own, far, me):
    blocks = own.shape[0]
    window[pl.ds((1 - me % 2) * (2 * blocks), blocks)] = near[0:blocks]
    window[blocks : 2 * blocks] = own[...]
    window[pl.ds((me % 2) * (2 * blocks), blocks)] = far[0:blocks]


def fine_row(index, offset, tiles, window, g):
    slots = tiles.shape[1]
    picked = [window[index[s, g] - offset] for s in range(slots)]
    return dot_nn(
        jnp.concatenate(picked, axis=1),
        jnp.concatenate([tiles[g, s] for s in range(slots)], axis=0),
    )


def second_kernel(
    index, plan, place, tiles, near, own, far, part, res, winv, hot, basis_b, basis_c, basis_d, b_out,
    b16_out, b16_too, mine_out, rows_out, window,
):
    del hot, basis_b, basis_c, basis_d
    blocks, ext = own.shape[0], own.shape[2]
    offset = (place[0] - 1) * blocks
    fill_window(window, near, own, far, place[0])

    def finish_row(g, product):
        w = winv[pl.ds(g, 1), :]
        r = res[g]
        b = w * r + w * (r - product)
        b_out[g] = b
        b16_out[g] = b.astype(BF16)
        b16_too[g] = b.astype(BF16)

    for_rows(index, plan, offset, tiles, window, part, blocks, finish_row)
    for n in range(blocks, b16_too.shape[0]):
        b16_too[n] = jnp.zeros_like(b16_too[n])
    odd = place[0] % 2
    extra = far.shape[0] - blocks
    mine_out[pl.ds((1 - odd) * extra, extra)] = near[blocks : blocks + extra]
    mine_out[pl.ds(odd * extra, extra)] = far[blocks:]
    rows_out[...] = near[blocks + extra :]


def split(row, ext):
    return lax.shift_right_logical(row, ext.bit_length() - 1), row & (ext - 1)


def one_hot(row, n):
    ids = lax.broadcasted_iota(jnp.int32, (n, row.shape[1]), 0)
    return jnp.where(ids == row, 1.0, 0.0).astype(BF16)


def spread(value, row, n):
    return jnp.concatenate(
        [jnp.where(row == l, value, 0.0).astype(BF16) for l in range(n)], axis=0
    )


def edge(message, row, n=128):
    return message[row : row + n, :]


def as_int(row):
    return row.astype(F32).astype(jnp.int32)


def inverse(row, present):
    return DAMPING * (1.0 / jnp.where(present, row, 1.0))


def mid_product(mid_tiles, v, b):
    ext = mid_tiles.shape[2]
    count = mid_tiles.shape[0]
    ks = [k for k in range(3) if v.get(b - 1 + k) is not None]
    return dot_nt(
        jnp.concatenate([v[b - 1 + k] for k in ks], axis=1),
        jnp.concatenate([mid_tiles[b, k] for k in ks], axis=1),
    )


def third_kernel(
    index, plan, place, tiles, near, own, far, part, res, owner, hot, mid_tiles, from_left,
    from_right, scale, mid_hot, mid_block, fres_out, u_out, bpart_out, send, window, spread_rows,
):
    blocks, ext = own.shape[0], own.shape[2]
    width = own.shape[1]
    mids = mid_tiles.shape[0]
    me = place[0]
    offset = (me - 1) * blocks
    fill_window(window, near, own, far, place[0])

    def finish_row(g, product):
        r = res[g] - product
        fres_out[g] = r
        lo, _ = split(owner[pl.ds(g, 1), :] - me * (mids * ext), ext)
        at = g * ext if isinstance(g, int) else pl.multiple_of(g * ext, ext)
        spread_rows[:, pl.ds(at, ext)] = spread(r, lo, mids)

    for_rows(index, plan, offset, tiles, window, part, blocks, finish_row)
    quarters = [slice(n * blocks // 4 * ext, (n + 1) * blocks // 4 * ext) for n in range(4)]
    total = sum(dot_nt(spread_rows[:, q], hot[:, q]) for q in quarters)
    u = [total[b * width : (b + 1) * width] for b in range(mids)]
    winv = [scale[b : b + 1, :] for b in range(mids)]
    winv_left, winv_right = scale[mids : mids + 1, :], scale[mids + 1 : mids + 2, :]
    left_mid, left_next, left_far = (edge(from_left, 128 * k) for k in range(3))
    right_mid, right_prev, right_far = (edge(from_right, 128 * k) for k in range(3))
    a = [winv[b] * u[b] for b in range(mids)]
    a16 = {b: a[b].astype(BF16) for b in range(mids)}
    mine = {}
    for b in range(mids):
        mine[b] = a[b] + winv[b] * (u[b] - mid_product(mid_tiles, a16, b))
        u_out[b] = u[b]
        bpart_out[b] = mine[b]
    mine[-1] = -winv_left * dot_nt(a16[0], left_next)
    mine[mids] = -winv_right * dot_nt(a16[mids - 1], right_prev)
    p16 = {b: v.astype(BF16) for b, v in mine.items()}
    rest = {b: u[b] - mid_product(mid_tiles, p16, b) for b in range(mids)}
    rest[-1] = -(dot_nt(p16[-1], left_mid) + dot_nt(p16[0], left_next))
    rest[-2] = -dot_nt(p16[-1], left_far)
    rest[mids] = -(dot_nt(p16[mids], right_mid) + dot_nt(p16[mids - 1], right_prev))
    rest[mids + 1] = -dot_nt(p16[mids], right_far)
    spreads = [
        spread(rest[b], mid_block[b + 2 : b + 3, :], 4) for b in range(-2, mids + 2)
    ]
    coarse = dot_nt(jnp.concatenate(spreads, axis=1), mid_hot[...])
    coarse16 = coarse.astype(BF16)
    first, last = u[0].astype(BF16), u[mids - 1].astype(BF16)
    none = jnp.zeros_like(first)
    for d in range(send.shape[0]):
        for k in range(4):
            send[d, k] = coarse16[k * width : (k + 1) * width]
        send[d, 4] = jnp.where(me + 1 == d, last, jnp.where(me - 1 == d, first, none))


def mid_kernel(
    place, got, inverse_rows, partner_rows, mid_tiles, scale, mid_hot, mid_block, u, bpart,
    dpart_out, edges_out, near_out, far_out, next_out, beyond_out,
):
    ext = mid_tiles.shape[2]
    mids = mid_tiles.shape[0]
    peers = got.shape[0]
    width = got.shape[2]
    me = place[0]
    odd = me % 2
    rhs = []
    for k in range(peers):
        terms = [
            got[s, k - (s - 2 + s % 2)].astype(F32)
            for s in range(peers)
            if 0 <= k - (s - 2 + s % 2) < 4
        ]
        rhs.append(sum(terms[1:], terms[0]))
    rhs16 = jnp.concatenate([r.astype(BF16) for r in rhs], axis=1)
    mine = dot_nt(rhs16, inverse_rows[...].astype(BF16))
    other = dot_nt(rhs16, partner_rows[...])
    pair = jnp.concatenate(
        [jnp.where(odd == 0, mine, other), jnp.where(odd == 0, other, mine)], axis=0
    ).astype(BF16)
    winv = [scale[b : b + 1, :] for b in range(mids)]
    winv_left, winv_right = scale[mids : mids + 1, :], scale[mids + 1 : mids + 2, :]
    before = got[lax.rem(me + peers - 1, peers), 4].astype(F32)
    after = got[lax.rem(me + 1, peers), 4].astype(F32)
    a_before = (winv_left * before).astype(BF16)
    a_after = (winv_right * after).astype(BF16)
    c, c16 = {}, {}
    for b in range(mids):
        value = bpart[b]
        if b == 0:
            value = value - winv[b] * dot_nt(a_before, mid_tiles[b, 0])
        if b == mids - 1:
            value = value - winv[b] * dot_nt(a_after, mid_tiles[b, 2])
        hot = mid_hot[:, (b + 2) * ext : (b + 3) * ext]
        both = jnp.dot(pair, hot, preferred_element_type=F32)
        second = mid_block[b + 2 : b + 3, :] == 3 - 2 * odd
        c[b] = value + jnp.where(second, both[width:], both[:width])
        c16[b] = c[b].astype(BF16)
    d16 = []
    for b in range(mids):
        d = c[b] + winv[b] * (u[b] - mid_product(mid_tiles, c16, b))
        dpart_out[b] = d
        d16.append(d.astype(BF16))
    edges_out[0] = c16[0]
    edges_out[1] = c16[mids - 1]
    for b in range(mids):
        near_out[b] = d16[b]
        far_out[b] = d16[b]
    first, last = c16[0], c16[mids - 1]
    low = me % 4 < 2
    near_out[mids] = jnp.where(odd == 0, last, first)
    far_out[mids] = jnp.where(odd == 0, first, last)
    next_out[...] = jnp.where(low, last, first)
    beyond_out[...] = jnp.where(low, first, last)


def prolong(values, hot, lo, width, mids):
    both = jnp.dot(values, hot, preferred_element_type=F32)
    result = jnp.where(lo == 0, both[:width], 0.0)
    for l in range(1, mids):
        result = jnp.where(lo == l, both[l * width : (l + 1) * width], result)
    return result


def last_kernel(
    index, place, tiles, near, far, other, nexts, beyond, dpart, c_edges, mid_tiles, scale, owner, hot_own, from_left, hot_left,
    from_right, hot_right, b_in, fres, winv, basis_a, basis_b, basis_c, basis_d, out, gram_out, window,
    added, rounded, grams, result, sems,
):
    blocks, width, ext = b_in.shape
    mids = mid_tiles.shape[0]
    me, peers = place[0], place[1]
    odd = me % 2
    low = me % 4 < 2
    middle = jnp.logical_or(me % 4 == 1, me % 4 == 2)
    present = jnp.logical_and(me > 0, me < peers - 1)
    none = jnp.zeros_like(nexts[...])
    away = [
        jnp.where(middle, other[b], jnp.where(present, far[b], none)) for b in range(mids + 1)
    ]
    left = [jnp.where(odd == 1, near[b], away[b]) for b in range(mids + 1)]
    right = [jnp.where(odd == 1, away[b], near[b]) for b in range(mids + 1)]
    outer = jnp.where(jnp.logical_and(me > 1, me < peers - 2), beyond[...], none)
    far_left = jnp.where(low, outer, nexts[...])
    far_right = jnp.where(low, nexts[...], outer)
    row = lambda n: scale[n : n + 1, :]
    own = [dpart[b] for b in range(mids)]
    own[0] = own[0] - row(0) * dot_nt(left[mids], mid_tiles[0, 0])
    own[-1] = own[-1] - row(mids - 1) * dot_nt(right[mids], mid_tiles[mids - 1, 2])
    lefts = [v.astype(F32) for v in left[:mids]]
    lefts[0] = lefts[0] - row(mids + 2) * dot_nt(far_left, edge(from_left, 384))
    lefts[-1] = lefts[-1] - row(mids) * dot_nt(c_edges[0], edge(from_left, 128))
    rights = [v.astype(F32) for v in right[:mids]]
    rights[0] = rights[0] - row(mids + 1) * dot_nt(c_edges[1], edge(from_right, 128))
    rights[-1] = rights[-1] - row(mids + 3) * dot_nt(far_right, edge(from_right, 384))
    own16, left16, right16 = (
        jnp.concatenate([v.astype(BF16) for v in side], axis=0) for side in (own, lefts, rights)
    )
    own_lo, _ = split(owner[0:blocks] - me * (mids * ext), ext)
    left_lo, right_lo = (
        as_int(message[LO_AT : LO_AT + blocks, :]) for message in (from_left, from_right)
    )
    for g in range(0, blocks, 2):
        cols = slice(g * ext, (g + 2) * ext)
        for lo, hot, values, base in (
            (own_lo, hot_own, own16, blocks),
            (left_lo, hot_left, left16, 0),
            (right_lo, hot_right, right16, 2 * blocks),
        ):
            row = jnp.concatenate([lo[g : g + 1], lo[g + 1 : g + 2]], axis=1)
            value = prolong(values, hot[:, cols], row, width, mids)
            for n in range(2):
                half = value[:, n * ext : (n + 1) * ext]
                if base == blocks:
                    added[g + n] = half
                window[base + g + n] = half.astype(BF16)
    offset = (me - 1) * blocks
    count = sems.shape[0]
    per = blocks // count

    def copy(part):
        cols = pl.ds(part * per * ext, per * ext)
        return pltpu.make_async_copy(result.at[:, cols], out.at[:, cols], sems.at[part])

    for g in range(blocks):
        product = fine_row(index, offset, tiles, window, g)
        value = b_in[g] + added[g] + winv[pl.ds(g, 1), :] * (fres[g] - product)
        cols = slice(g * ext, (g + 1) * ext)
        result[:, cols] = value
        rounded[:, cols] = value.astype(BF16)
        if (g + 1) % per == 0:
            copy((g + 1) // per - 1).start()
    for n, piece in enumerate((basis_a, basis_b, basis_c, basis_d)):
        grams[place[2] ^ n] = dot_nt(rounded[...], piece[...])
    gram = jnp.concatenate([grams[n] for n in range(4)], axis=1)
    gram = jnp.concatenate([gram[: width // 2], gram[width // 2 :]], axis=1)
    for d in range(gram_out.shape[0]):
        gram_out[d] = gram
    for part in range(count):
        copy(part).wait()


def sum_kernel(got, out):
    total = got[0]
    for s in range(1, got.shape[0]):
        total = total + got[s]
    half, wide = out.shape[0] // 2, out.shape[1]
    out[0:half] = total[:, :wide]
    out[half:] = total[:, wide:]


def halo(for_partner, for_other):
    peers = lax.axis_size("rows")
    odd = [(i, i + 1) for i in range(1, peers - 1, 2)]
    even = [(i, i + 1) for i in range(0, peers - 1, 2)]
    swap = lambda pairs: pairs + [(j, i) for i, j in pairs]
    near = lax.ppermute(for_partner, "rows", swap(even))
    far = lax.ppermute(for_other, "rows", swap(odd))
    return near, far


def relay_kernel(after, *refs):
    del after
    half = len(refs) // 2
    for value, out in zip(refs[:half], refs[half:]):
        out[...] = value[...]


def from_columns(values, relay=lambda *v: v):
    peers = lax.axis_size("cols")
    swap = lambda v, n: lax.ppermute(v, "cols", [(i, i ^ n) for i in range(peers)])
    across = [swap(v, 2) for v in values]
    count = len(values)
    held = relay(*values, *across)
    return [[swap(held[n], 1), across[n], swap(held[count + n], 1)] for n in range(count)]


def on_device(
    residual_block, basis, fine_tiles, fine_index, mid_tiles, fine_owner, mid_owner, coarse_inverse
):
    peers = lax.axis_size("rows")
    me = lax.axis_index("rows")
    blocks, slots, ext, _ = fine_tiles.shape
    mids = mid_tiles.shape[0]
    count = blocks * ext
    width = residual_block.shape[1]
    res = residual_block.T
    index = fine_index.T
    place = jnp.stack([me, jnp.int32(peers), lax.axis_index("cols")])
    owner = jnp.concatenate([fine_owner, mid_owner]).reshape(blocks + mids, ext)
    shape = jax.ShapeDtypeStruct
    tile_bytes = fine_tiles.size * 2
    fine_flops = 2 * fine_tiles.size * width
    extra = ext // width + 3

    columns = lax.axis_size("cols")
    share = coarse_inverse.shape[0] // columns
    whole_row = coarse_inverse.shape[1]
    quarter = (share // width) * (whole_row // ext)

    a16, for_partner, for_other, winv, res_blocks = pl.pallas_call(
        first_kernel,
        in_specs=[SM] + [HBM] * 3 + [VM, HBM],
        out_specs=[VM] * 5,
        out_shape=[
            shape((blocks, width, ext), BF16),
            shape((blocks + extra + quarter, width, ext), BF16),
            shape((blocks + extra, width, ext), BF16),
            shape((blocks, ext), F32),
            shape((blocks, width, ext), F32),
        ],
        scratch_shapes=[
            pltpu.VMEM((width, count), F32),
            pltpu.VMEM((blocks, ext, ext), BF16),
            pltpu.VMEM((4, ext, ext), BF16),
            pltpu.VMEM((share, whole_row), F32),
            pltpu.SemaphoreType.DMA((5,)),
            pltpu.SemaphoreType.DMA((5,)),
        ],
        name="first_smoothing",
        **params(FIRST_LIMIT, count * ext, tile_bytes // 4),
    )(place, res, fine_tiles, mid_tiles, owner, coarse_inverse)

    near, far = halo(for_partner, for_other)
    hot_own, plan = pl.pallas_call(
        plan_kernel,
        in_specs=[SM, SM, ANY, VM],
        out_specs=[VM, SM],
        out_shape=[shape((ext, count), BF16), shape((5, blocks), jnp.int32)],
        name="one_hot_rows",
        **params(4, count * ext, 4 * tile_bytes),
    )(place, index, winv, owner)

    part_shape = shape((blocks, width, ext), F32)
    part, tiles = pl.pallas_call(
        own_first_kernel,
        in_specs=[SM, SM, SM, VM, VM],
        out_specs=[VM, VM],
        out_shape=[part_shape, shape(fine_tiles.shape, BF16)],
        scratch_shapes=[pltpu.VMEM((blocks + 1, width, ext), BF16)],
        name="own_part_and_turned_tiles",
        **params(4, ext, ext),
    )(index, place, plan, fine_tiles, a16)
    basis_pieces = [basis.T] + from_columns([basis.T])[0]

    b32, b16, b16_too, mine, mine_rows = pl.pallas_call(
        second_kernel,
        in_specs=[SM] * 3 + [VM] * 7 + [ANY] * 4,
        out_specs=[VM] * 5,
        out_shape=[
            shape((blocks, width, ext), F32),
            shape((blocks, width, ext), BF16),
            shape((blocks + 1, width, ext), BF16),
            shape((2 * extra, width, ext), BF16),
            shape((quarter, width, ext), BF16),
        ],
        scratch_shapes=[pltpu.VMEM((3 * blocks + 1, width, ext), BF16)],
        name="second_smoothing",
        **params(6, fine_flops, tile_bytes),
    )(
        index, plan, place, tiles, near, a16, far, part, res_blocks, winv, hot_own,
        *basis_pieces[1:],
    )

    near, far = halo(b16_too, b16)
    part = pl.pallas_call(
        own_kernel,
        in_specs=[SM, SM, VM, VM],
        out_specs=VM,
        out_shape=part_shape,
        scratch_shapes=[pltpu.VMEM((blocks + 1, width, ext), BF16)],
        name="own_part_of_residual",
        **params(4, ext, ext),
    )(index, place, tiles, b16)
    def relay(*values):
        return pl.pallas_call(
            relay_kernel,
            in_specs=[ANY] + [VM] * len(values),
            out_specs=[VM] * len(values),
            out_shape=[shape(v.shape, BF16) for v in values],
            name="relay",
            **params(4, ext, ext),
        )(part, *values)

    mine_pieces, rows_pieces = from_columns([mine, mine_rows], relay)
    from_left, from_right, partner_rows, scale, mid_hot, mid_block = pl.pallas_call(
        sides_kernel,
        in_specs=[SM] + [VM] * 10,
        out_specs=[VM] * 6,
        out_shape=[
            shape((MESSAGE, ext), BF16),
            shape((MESSAGE, ext), BF16),
            shape(coarse_inverse.shape, BF16),
            shape((16, ext), F32),
            shape((ext, (mids + 4) * ext), BF16),
            shape((16, ext), jnp.int32),
        ],
        scratch_shapes=[
            pltpu.VMEM((4, 2 * extra, width, ext), BF16),
            pltpu.VMEM((4, quarter, width, ext), BF16),
        ],
        name="side_messages",
        **params(4, ext, ext),
    )(
        place, mine, *mine_pieces, mine_rows, *rows_pieces, mid_tiles, owner,
    )

    fres, u, bpart, send = pl.pallas_call(
        third_kernel,
        in_specs=[SM] * 3 + [VM] * 14,
        out_specs=[VM] * 4,
        out_shape=[
            shape((blocks, width, ext), F32),
            shape((mids, width, ext), F32),
            shape((mids, width, ext), F32),
            shape((peers, 5, width, ext), BF16),
        ],
        scratch_shapes=[
            pltpu.VMEM((3 * blocks + 1, width, ext), BF16),
            pltpu.VMEM((mids * width, count), BF16),
        ],
        name="residual_and_restriction",
        **params(10, fine_flops, tile_bytes),
    )(
        index, plan, place, tiles, near, b16, far, part, res_blocks, owner, hot_own, mid_tiles,
        from_left, from_right, scale, mid_hot, mid_block,
    )

    got = lax.all_to_all(send, "rows", 0, 0)
    dpart, c_edges, *sends = pl.pallas_call(
        mid_kernel,
        in_specs=[SM] + [VM] * 9,
        out_specs=[VM] * 6,
        out_shape=[
            shape((mids, width, ext), F32),
            shape((2, width, ext), BF16),
            shape((mids + 1, width, ext), BF16),
            shape((mids + 1, width, ext), BF16),
            shape((width, ext), BF16),
            shape((width, ext), BF16),
        ],
        name="coarse_and_mid_level",
        **params(MID_LIMIT, 4 * width * coarse_inverse.size, coarse_inverse.size * 4),
    )(
        place, got, coarse_inverse, partner_rows, mid_tiles, scale, mid_hot, mid_block, u, bpart,
    )

    return finish(
        place, index, tiles, sends, dpart, c_edges, mid_tiles, scale, owner, hot_own, from_left, from_right,
        b32, fres, winv, basis_pieces,
    )


def finish(
    place, index, tiles, sends, dpart, c_edges, mid_tiles, scale, owner, hot_own, from_left, from_right, b32,
    fres, winv, basis_pieces,
):
    peers = lax.axis_size("rows")
    blocks, width, ext = b32.shape
    mids = mid_tiles.shape[0]
    count = blocks * ext
    shape = jax.ShapeDtypeStruct
    swap = lambda v, pairs: lax.ppermute(v, "rows", pairs + [(j, i) for i, j in pairs])
    flip = lambda v, n: lax.ppermute(v, "rows", [(i, i ^ n) for i in range(peers)])
    ends = [(0, 1), (peers - 2, peers - 1)] if peers > 4 else [(0, 1), (2, 3)]
    inner = range(2, peers - 4, 4)
    far = swap(sends[1], [(i + 1, i + 2) for i in inner] + [(i, i + 3) for i in inner] + ends)
    beyond = swap(sends[3], [(i + n, i + 2 + n) for i in inner for n in range(2)] + ends)
    near = flip(sends[0], 1)
    other = flip(sends[1], 3)
    nexts = flip(sends[2], 2)
    hot_left, hot_right = pl.pallas_call(
        side_hot_kernel,
        in_specs=[ANY, VM, VM],
        out_specs=[VM] * 2,
        out_shape=[shape((ext, count), BF16)] * 2,
        name="side_one_hot_rows",
        **params(4, ext, ext),
    )(c_edges, from_left, from_right)
    out, grams = pl.pallas_call(
        last_kernel,
        in_specs=[SM, SM] + [VM] * 23,
        out_specs=[HBM, VM],
        out_shape=[
            shape((width, count), F32),
            shape((peers, width // 2, 8 * width), F32),
        ],
        scratch_shapes=[
            pltpu.VMEM((3 * blocks, width, ext), BF16),
            pltpu.VMEM((blocks, width, ext), F32),
            pltpu.VMEM((width, count), BF16),
            pltpu.VMEM((4, width, width), F32),
            pltpu.VMEM((width, count), F32),
            pltpu.SemaphoreType.DMA((2,)),
        ],
        name="prolongation_and_last_smoothing",
        **params(8, 2 * tiles.size * width, tiles.size * 2),
    )(
        index, place, tiles, near, far, other, nexts, beyond, dpart, c_edges, mid_tiles, scale, owner, hot_own, from_left, hot_left,
        from_right, hot_right, b32, fres, winv, *basis_pieces,
    )
    gram = pl.pallas_call(
        sum_kernel,
        in_specs=[VM],
        out_specs=VM,
        out_shape=shape((width, 4 * width), F32),
        name="gram_sum",
        **params(4, 0, 0),
    )(lax.all_to_all(grams, "rows", 0, 0))
    return out.T, gram.T


def solution(mesh):
    in_specs = (
        P("rows", "cols"),
        P("rows", "cols"),
        P("rows", None, None, None),
        P("rows", None),
        P("rows", None, None, None),
        P("rows"),
        P("rows"),
        P("rows", None),
    )
    out_specs = (P("rows", "cols"), P(None, "cols"))
    return jax.shard_map(
        on_device, mesh=mesh, in_specs=in_specs, out_specs=out_specs, check_vma=False
    )
```
